32 devices in a mesh: stream: 4 (over y, x), seq: 8 (over z, core).
Axes of the slice: x: 2, y: 2, z: 4, core: 2. Of those that a mesh axis runs over, the one named last changes fastest.
Arguments:
- tokens: bfloat16 [4, 8192, 768], P('stream', 'seq'), may hold values from -6 to 6
- global_states: bfloat16 [4, 256, 768], P('stream', 'seq'), may hold values from -6 to 6
- cotangent: bfloat16 [4, 8192, 768], P('stream', 'seq'), may hold values from -6 to 6
- w_qkv: bfloat16 [768, 2304], replicated, may hold values from -0.21875 to 0.21875
- w_out: bfloat16 [768, 768], replicated, may hold values from -1.75 to 1.75
- w_up: bfloat16 [768, 3072], replicated, may hold values from -0.21875 to 0.21875
- w_down: bfloat16 [3072, 768], replicated, may hold values from -0.109375 to 0.109375
- first_gain: float32 [768], replicated, may hold values from 0.5 to 1.5
- first_shift: float32 [768], replicated, may hold values from -3 to 3
- second_gain: float32 [768], replicated, may hold values from 0.5 to 1.5
- second_shift: float32 [768], replicated, may hold values from -3 to 3
- rich_query: float32 [4, 768], replicated, may hold values from -0.75 to 0.75
- rich_key: float32 [4, 768], replicated, may hold values from -0.75 to 0.75
- rich_bias: float32 [4, 12], replicated, may hold values from 0.5 to 3.5
- rich_theta: float32 [2, 12], replicated, may hold values from 0.3 to 0.8
- bucket_units: int32 [4, 4], P('stream'), may hold values from 1 to 4, as said below
- form_lengths: int32 [4, 4], P('stream'), may hold values from 128 to 4608, as said below
- coords: int32 [4, 2, 8192], P('stream'), may hold values from 0 to 99
- glob_owner: int32 [4, 256], P('stream'), may hold values from 0 to 3, as said below
Outputs:
- layer_out: bfloat16 [4, 8192, 768], P('stream', 'seq')
- tokens_grad: bfloat16 [4, 8192, 768], P('stream', 'seq')
- glob_grad: bfloat16 [4, 256, 768], P('stream', 'seq')
- w_qkv_grad: float32 [768, 2304], P('seq')
- w_out_grad: float32 [768, 768], P('seq')
- w_up_grad: float32 [768, 3072], P('seq')
- w_down_grad: float32 [3072, 768], P('seq')
- first_gain_grad: float32 [768], P('seq')
- first_shift_grad: float32 [768], P('seq')
- second_gain_grad: float32 [768], P('seq')
- second_shift_grad: float32 [768], P('seq')
- rich_query_grad: float32 [4, 768], P(None, 'seq')
- rich_key_grad: float32 [4, 768], P(None, 'seq')
- rich_bias_grad: float32 [4, 12], replicated
- rich_theta_grad: float32 [2, 12], replicated
The draws below stay inside these ranges and needn't reach their ends.
Inputs may be any that keep to these rules, and one draw needn't show every extreme that they name: `bucket_units`: per stream the 4 values sum to 8; each stream has one value 4. form_lengths[s, f] is at most the size of bucket f of stream s (steps' starts[f+1] - starts[f], the last one ending at 8192) and at least that size minus 1024 // 2 plus 128. `glob_owner`: every form of a stream owns exactly 64 of that stream's global tokens.
All inputs are finite; a program needn't handle non-finite values.
Results may differ from the reference program's by a relative error of at most 0.019.
Values may be sent and summed in bfloat16 or wider, within the bound.
No kernel may reach another device: no remote copies, remote signals or barrier semaphores. Data moves between devices by JAX's collectives and lax.ppermute only.
A program may use at most 256 MiB of HBM per device.

```python
import jax
import jax.numpy as jnp
from jax import lax

D = 768
HEADS = 12
HEAD_DIM = 64
FF = 3072
RADIUS = 128
GLOB_FORM = 64
QBLOCK = 512
TOK_DEV = 1024
STREAMS = 4
SEQLEN = 8192
FORMS = 4
GLOBALS = 256


def stream_units(key):
    key = jax.random.fold_in(key, 11)

    def single(stream_key):
        move_key, order_key = jax.random.split(stream_key)
        position = jnp.arange(FORMS)
        offset = position - 3
        paired = jnp.where(offset % 2 == 0, position + 1 < FORMS, True)
        moves_drawn = jax.random.randint(move_key, (FORMS,), -1, 2)
        signed = jnp.where(offset % 2 == 0, 1, -1) * moves_drawn[jnp.maximum(offset, 0) // 2]
        start_counts = jnp.where(position == 0, 4, jnp.where(position < 3, 1, 2))
        unit_counts = start_counts + jnp.where((position >= 3) & paired, signed, 0)
        return unit_counts[jax.random.permutation(order_key, FORMS)]
    return jax.vmap(single)(jax.random.split(key, STREAMS)).astype(jnp.int32)


def draw_bucket_units(key, part):
    return stream_units(key)


def draw_form_lengths(key, part):
    unit_counts = stream_units(key)
    key = jax.random.fold_in(key, 5)
    position = jnp.arange(FORMS)[None, :]
    bucket_rows = TOK_DEV * unit_counts + jnp.where(position == 0, TOK_DEV // 2, 0) - jnp.where(position == FORMS - 1, TOK_DEV // 2, 0)
    shortfall = jax.random.randint(key, unit_counts.shape, 0, TOK_DEV // 2 - RADIUS + 1)
    return (bucket_rows - shortfall).astype(jnp.int32)


def draw_glob_owner(key, part):
    key = jax.random.fold_in(key, 7)

    def single(stream_key):
        return jax.random.permutation(stream_key, GLOBALS) // GLOB_FORM
    return jax.vmap(single)(jax.random.split(key, STREAMS)).astype(jnp.int32)


def place_ends(entries, own_key, smallest, high):
    dims = entries.shape
    spot = [jax.random.randint(jax.random.fold_in(own_key, axis), (), 0, dims[axis]) for axis in range(len(dims))]
    entries = entries.at[tuple(spot)].set(smallest)
    longest = dims.index(max(dims))
    spot[longest] = (spot[longest] + 1) % dims[longest]
    return entries.at[tuple(spot)].set(high)


def levels(own_key, dims, pieces, low, top_value):
    level = 1.0
    for axis_at, parts in pieces:
        draws = jax.random.uniform(jax.random.fold_in(jax.random.fold_in(own_key, 6), axis_at), (parts,), jnp.float32, low / len(pieces), top_value / len(pieces))
        level = level * jnp.repeat(jnp.exp(draws), dims[axis_at] // parts).reshape((-1,) + (1,) * (len(dims) - 1 - axis_at))
    return level


def normal_values(own_key, shape, width, reach, pieces=(), held_as=jnp.bfloat16):
    result = width * jax.random.normal(own_key, shape, jnp.float32)
    if pieces:
        result = result * levels(own_key, shape, pieces, -0.22, 0.18)
    return jnp.clip(result, -reach, reach).astype(held_as)


def setup_inputs(seed: int = 0) -> dict:
    key_of = jax.random.split(jax.random.key(seed), 20)
    tokens = normal_values(key_of[0], (STREAMS, SEQLEN, D), 1.0, 6.0, ((0, 4), (1, 8)))
    global_states = normal_values(key_of[1], (STREAMS, GLOBALS, D), 1.0, 6.0, ((0, 4), (1, 8)))
    cotangent = normal_values(key_of[2], (STREAMS, SEQLEN, D), 1.0, 6.0, ((0, 4), (1, 8)))
    w_qkv = normal_values(key_of[3], (D, 3 * D), D ** -0.5, 0.21875)
    w_out = normal_values(key_of[4], (D, D), (max(D // 64, 4)) ** -0.5, 1.75)
    w_up = normal_values(key_of[5], (D, FF), D ** -0.5, 0.21875)
    w_down = normal_values(key_of[6], (FF, D), FF ** -0.5, 0.109375)
    first_gain = jnp.clip(1.0 + 0.1 * jax.random.normal(key_of[7], (D,), jnp.float32), 0.5, 1.5)
    first_shift = normal_values(key_of[8], (D,), 0.5, 3.0, (), jnp.float32)
    second_gain = jnp.clip(1.0 + 0.1 * jax.random.normal(key_of[9], (D,), jnp.float32), 0.5, 1.5)
    second_shift = normal_values(key_of[10], (D,), 0.5, 3.0, (), jnp.float32)
    rich_query = normal_values(key_of[11], (4, D), HEAD_DIM ** -0.5, 0.75, (), jnp.float32)
    rich_key = normal_values(key_of[12], (4, D), HEAD_DIM ** -0.5, 0.75, (), jnp.float32)
    rich_bias = jnp.clip(jax.random.uniform(key_of[13], (4, HEADS), jnp.float32, 0.5, 3.5), 0.5, 3.5)
    rich_theta = jnp.clip(jax.random.uniform(key_of[14], (2, HEADS), jnp.float32, 0.3, 0.8), 0.3, 0.8)
    bucket_units = draw_bucket_units(jax.random.fold_in(key_of[19], 71), 0)
    form_lengths = draw_form_lengths(jax.random.fold_in(key_of[19], 71), 0)
    coords = place_ends(jax.random.randint(key_of[17], (STREAMS, 2, SEQLEN), 0, 100), jax.random.fold_in(key_of[17], 1), 0, 99).astype(jnp.int32)
    glob_owner = draw_glob_owner(jax.random.fold_in(key_of[19], 71), 0)
    return dict(tokens=tokens, global_states=global_states, cotangent=cotangent, w_qkv=w_qkv, w_out=w_out, w_up=w_up, w_down=w_down, first_gain=first_gain, first_shift=first_shift, second_gain=second_gain, second_shift=second_shift, rich_query=rich_query, rich_key=rich_key, rich_bias=rich_bias, rich_theta=rich_theta, bucket_units=bucket_units, form_lengths=form_lengths, coords=coords, glob_owner=glob_owner)


EPSILON = 1e-06
NEGATIVE = -1e+30
HIGHEST = lax.Precision.HIGHEST

@jax.custom_vjp
def low(v):
    return lax.optimization_barrier(v.astype(jnp.bfloat16)).astype(jnp.float32)

@jax.custom_vjp
def low_back(v):
    return v

def low_keep(v):
    return (low(v), None)

def low_pass(kept, grad):
    return (grad,)

def back_keep(v):
    return (v, None)

def back_low(kept, grad):
    return (low(grad),)
low.defvjp(low_keep, low_pass)
low_back.defvjp(back_keep, back_low)

def low_both(values):
    return low_back(low(values))

def layer_norm(values, norm_gain, norm_shift):
    centre = lax.optimization_barrier(jnp.mean(values, axis=-1, keepdims=True))
    centred = values - centre
    spread = lax.optimization_barrier(jnp.mean(centred * centred, axis=-1, keepdims=True))
    return centred * lax.rsqrt(spread + EPSILON) * norm_gain + norm_shift

def bucket_starts(unit_counts):
    position = jnp.arange(FORMS, dtype=jnp.int32)
    before = jnp.cumsum(unit_counts) - unit_counts
    return jnp.where(position == 0, 0, TOK_DEV // 2 + TOK_DEV * before).astype(jnp.int32)

def locate(position, starts, lengths):
    form_index = lax.optimization_barrier(jnp.sum((position[:, None] >= starts[None, 1:]).astype(jnp.int32), axis=1)).astype(jnp.int32)
    chosen = form_index[:, None] == jnp.arange(FORMS, dtype=jnp.int32)[None, :]
    first_row = lax.optimization_barrier(jnp.sum(jnp.where(chosen, starts[None, :], 0), axis=1)).astype(jnp.int32)
    live_rows = lax.optimization_barrier(jnp.sum(jnp.where(chosen, lengths[None, :], 0), axis=1)).astype(jnp.int32)
    is_live = (position >= 0) & (position < SEQLEN) & (position - first_row < live_rows)
    return (form_index, is_live)

def geometry(coord_query, coord_key):
    ahead_sign = jnp.where(coord_key[:, None, :] > coord_query[:, :, None], 1.0, -1.0).astype(jnp.float32)
    log_apart = jnp.log1p(jnp.abs(coord_query[:, :, None] - coord_key[:, None, :]).astype(jnp.float32))
    return (ahead_sign[0], ahead_sign[1], log_apart[0], log_apart[1])

def rich_terms(query_rich, key_rich, rich_shift, rich_width, pair_geometry):
    sign_x, sign_y, dist_x, dist_y = pair_geometry

    def summed(column):
        return query_rich[column][:, :, None] + key_rich[column][:, None, :] + rich_shift[column][:, None, None]
    ordered = -jax.nn.softplus(-sign_x * summed(0)) - jax.nn.softplus(-sign_y * summed(1))
    gap_x = dist_x - summed(2)
    gap_y = dist_y - summed(3)
    half_x = 0.5 * rich_width[0] * rich_width[0]
    half_y = 0.5 * rich_width[1] * rich_width[1]
    return ordered - half_x[:, None, None] * gap_x * gap_x - half_y[:, None, None] * gap_y * gap_y

def stream_layer(inputs, glob_in, w_qkv, w_out, w_up, w_down, first_gain, first_shift, second_gain, second_shift, rich_query, rich_key, rich_bias, rich_theta, starts, lengths, coord_pad, owners):
    hidden_one = low(layer_norm(inputs, first_gain, first_shift))
    projected = low_both(jnp.dot(hidden_one, w_qkv, precision=HIGHEST))
    queries = projected[:, :D]
    key_rows = projected[:, D:2 * D]
    value_rows = projected[:, 2 * D:]
    glob_hidden = low(layer_norm(glob_in, first_gain, first_shift))
    glob_pairs = low(jnp.dot(glob_hidden, w_qkv[:, D:], precision=HIGHEST))
    glob_keys = glob_pairs[:, :D].reshape(GLOBALS, HEADS, HEAD_DIM)
    glob_values = glob_pairs[:, D:].reshape(GLOBALS, HEADS, HEAD_DIM)
    query_rich = jnp.einsum('she,che->chs', queries.reshape(SEQLEN, HEADS, HEAD_DIM), rich_query.reshape(4, HEADS, HEAD_DIM), precision=HIGHEST)
    key_rich = jnp.einsum('she,che->chs', key_rows.reshape(SEQLEN, HEADS, HEAD_DIM), rich_key.reshape(4, HEADS, HEAD_DIM), precision=HIGHEST)
    border = jnp.zeros((RADIUS, D), jnp.float32)
    key_pad = jnp.concatenate([border, key_rows, border], axis=0)
    value_pad = jnp.concatenate([border, value_rows, border], axis=0)
    key_rich_pad = jnp.pad(key_rich, ((0, 0), (0, 0), (RADIUS, RADIUS)))
    band_span = QBLOCK + 2 * RADIUS

    def attend(block_index):
        first_row = block_index * QBLOCK
        pos_query = first_row + jnp.arange(QBLOCK, dtype=jnp.int32)
        pos_key = first_row - RADIUS + jnp.arange(band_span, dtype=jnp.int32)
        form_query = locate(pos_query, starts, lengths)[0]
        form_key, live_key = locate(pos_key, starts, lengths)
        near_mask = live_key[None, :] & (form_key[None, :] == form_query[:, None]) & (jnp.abs(pos_query[:, None] - pos_key[None, :]) <= RADIUS)
        far_mask = owners[None, :] == form_query[:, None]
        pair_geometry = geometry(lax.dynamic_slice_in_dim(coord_pad, first_row + RADIUS, QBLOCK, 1), lax.dynamic_slice_in_dim(coord_pad, first_row, band_span, 1))
        query_block = lax.dynamic_slice_in_dim(queries, first_row, QBLOCK, 0).reshape(QBLOCK, HEADS, HEAD_DIM)
        key_block = lax.dynamic_slice_in_dim(key_pad, first_row, band_span, 0).reshape(band_span, HEADS, HEAD_DIM)
        value_block = lax.dynamic_slice_in_dim(value_pad, first_row, band_span, 0).reshape(band_span, HEADS, HEAD_DIM)
        near_part = jnp.einsum('qhe,khe->hqk', query_block, key_block, precision=HIGHEST) * 0.125
        near_part = near_part + rich_terms(lax.dynamic_slice_in_dim(query_rich, first_row, QBLOCK, 2), lax.dynamic_slice_in_dim(key_rich_pad, first_row, band_span, 2), rich_bias, rich_theta, pair_geometry)
        far_part = jnp.einsum('qhe,ghe->hqg', query_block, glob_keys, precision=HIGHEST) * 0.125
        scores = low_back(jnp.concatenate([jnp.where(near_mask[None], near_part, NEGATIVE), jnp.where(far_mask[None], far_part, NEGATIVE)], axis=2))
        row_max = lax.optimization_barrier(jnp.max(scores, axis=2, keepdims=True))
        exp_scores = jnp.exp(scores - row_max)
        attn_probs = low(exp_scores / lax.optimization_barrier(jnp.sum(exp_scores, axis=2, keepdims=True)))
        context = jnp.einsum('hqk,khe->qhe', attn_probs[:, :, :band_span], value_block, precision=HIGHEST) + jnp.einsum('hqg,ghe->qhe', attn_probs[:, :, band_span:], glob_values, precision=HIGHEST)
        return context.reshape(QBLOCK, D)
    context = lax.map(jax.checkpoint(attend), jnp.arange(SEQLEN // QBLOCK, dtype=jnp.int32))
    context = low_both(context.reshape(SEQLEN, D))
    middle = inputs + low_back(jnp.dot(context, w_out, precision=HIGHEST))
    hidden_two = low(layer_norm(middle, second_gain, second_shift))
    pre_act = low_back(jnp.dot(hidden_two, w_up, precision=HIGHEST))
    activated = low(jax.nn.gelu(pre_act, approximate=False))
    return middle + low_back(jnp.dot(activated, w_down, precision=HIGHEST))

def reference(tokens, global_states, cotangent, w_qkv, w_out, w_up, w_down, first_gain, first_shift, second_gain, second_shift, rich_query, rich_key, rich_bias, rich_theta, bucket_units, form_lengths, coords, glob_owner):
    weights = (w_qkv.astype(jnp.float32), w_out.astype(jnp.float32), w_up.astype(jnp.float32), w_down.astype(jnp.float32), first_gain, first_shift, second_gain, second_shift, rich_query, rich_key, rich_bias, rich_theta)

    def one_stream(totals, items):
        stream_tokens, stream_globals, stream_grad, unit_counts, lengths, stream_coords, owners = items
        starts = bucket_starts(unit_counts)
        coord_pad = jnp.pad(stream_coords, ((0, 0), (RADIUS, RADIUS)))

        def forward(inputs, glob_in, *params):
            return stream_layer(inputs, glob_in, *params, starts, lengths, coord_pad, owners)
        layer_out, pull_back = jax.vjp(forward, stream_tokens.astype(jnp.float32), stream_globals.astype(jnp.float32), *weights)
        gradients = pull_back(stream_grad.astype(jnp.float32))
        totals = tuple((running + addend for running, addend in zip(totals, gradients[2:])))
        return (totals, (layer_out.astype(jnp.bfloat16), gradients[0].astype(jnp.bfloat16), gradients[1].astype(jnp.bfloat16)))
    start_sums = tuple((jnp.zeros_like(weight) for weight in weights))
    totals, outputs = lax.scan(one_stream, start_sums, (tokens, global_states, cotangent, bucket_units, form_lengths, coords, glob_owner))
    return (outputs[0], outputs[1], outputs[2], totals[0], totals[1], totals[2], totals[3], totals[4], totals[5], totals[6], totals[7], totals[8], totals[9], totals[10], totals[11])
```

```python
from functools import partial
import math

import jax
import jax.numpy as jnp
from jax import lax
from jax.experimental import pallas as pl
from jax.experimental.pallas import tpu as pltpu
from jax.sharding import PartitionSpec as P

RADIUS = 128
GLOB_FORM = 64
QBLOCK = 512
TOK_DEV = 1024


EPSILON = 1e-06
HIGHEST = lax.Precision.HIGHEST


def padded(shard, sides, width):
    for axis, dim in sides:
        peers, length = (lax.axis_size(axis), shard.shape[dim])
        up = [(i, (i + 1) % peers) for i in range(peers - 1)]
        down = [(j, i) for i, j in up]
        last = lax.slice_in_dim(shard, length - width, length, axis=dim)
        first = lax.slice_in_dim(shard, 0, width, axis=dim)
        before = lax.ppermute(last, axis, up)
        after = lax.ppermute(first, axis, down)
        shard = jnp.concatenate([before, shard, after], axis=dim)
    return shard


def layer_norm(values, norm_gain, norm_shift):
    centre = jnp.mean(values, axis=-1, keepdims=True)
    centred = values - centre
    spread = jnp.mean(centred * centred, axis=-1, keepdims=True)
    return centred * lax.rsqrt(spread + EPSILON) * norm_gain + norm_shift


def gelu_exact(values):
    return jax.nn.gelu(values, approximate=False)


def bucket_starts(unit_counts):
    position = jnp.arange(unit_counts.shape[0], dtype=jnp.int32)
    before = jnp.cumsum(unit_counts) - unit_counts
    return jnp.where(position == 0, 0, TOK_DEV // 2 + TOK_DEV * before)


def locate(position, starts, lengths, stream_len):
    form_count = starts.shape[0]
    form_index = jnp.sum((position[:, None] >= starts[None, 1:]).astype(jnp.int32), axis=1)
    chosen = form_index[:, None] == jnp.arange(form_count, dtype=jnp.int32)[None, :]
    first_row = jnp.sum(jnp.where(chosen, starts[None, :], 0), axis=1)
    live_rows = jnp.sum(jnp.where(chosen, lengths[None, :], 0), axis=1)
    is_live = (position >= 0) & (position < stream_len) & (position - first_row < live_rows)
    return (form_index, is_live)


TILE = 128
SPAN = 384
LOG2E = math.log2(math.e)
FAR_AWAY = 1e15
CH = 16
F32 = jnp.float32
BF16 = jnp.bfloat16

def mm(a, b):
    return lax.dot_general(a, b, (((1,), (0,)), ((), ())), preferred_element_type=F32)

def mm_nt(a, b):
    return lax.dot_general(a, b, (((1,), (1,)), ((), ())), preferred_element_type=F32)

def split3(values):
    hi = lax.reduce_precision(values, 8, 7)
    rest = values - hi
    mid = lax.reduce_precision(rest, 8, 7)
    low = rest - mid
    return hi.astype(BF16), mid.astype(BF16), low.astype(BF16)

def half_masks(dtype):
    lane = lax.broadcasted_iota(jnp.int32, (1, 128), 1)
    low = (lane < 64).astype(F32)
    return low.astype(dtype), (1.0 - low).astype(dtype)

def geometry_into(cq_ref, ck_ref, t, refs, masked):
    ox_ref, oy_ref, dx_ref, dy_ref = refs
    for r in range(0, TILE, 32):
        xq = cq_ref[r : r + 32, 0:1]
        yq = cq_ref[r : r + 32, 1:2]
        fq = cq_ref[r : r + 32, 2:3]
        for lt in range(3):
            cols = pl.ds(pl.multiple_of(t * TILE + lt * 128, 128), 128)
            xk = ck_ref[0:1, cols]
            yk = ck_ref[1:2, cols]
            out = (slice(r, r + 32), slice(lt * 128, lt * 128 + 128))
            dx = jnp.log(1.0 + jnp.abs(xq - xk))
            dy = jnp.log(1.0 + jnp.abs(yq - yk))
            if masked:
                fk = ck_ref[2:3, cols]
                row = lax.broadcasted_iota(jnp.int32, (32, 128), 0) + r
                col = lax.broadcasted_iota(jnp.int32, (32, 128), 1) + lt * 128
                ok = (fq == fk) & (col >= row) & (col - row <= 2 * RADIUS)
                dx = jnp.where(ok, dx, FAR_AWAY)
                ox_ref[out] = jnp.where(xk > xq, 1.0, -1.0)
                oy_ref[out] = jnp.where(yk > yq, 1.0, -1.0)
            dx_ref[out] = dx
            dy_ref[out] = dy

def fwd_kernel(w_ref, q_ref, k_ref, v_ref, kg_ref, vg_ref, cq_ref, ck_ref, rq_ref, rk_ref, rb_ref,
               ctx_ref, pn_ref, pf_ref, g0_ref, g1_ref,
               ox_ref, oy_ref, dx_ref, dy_ref, s_ref, sf_ref, a_ref, b_ref, *, pairs):
    t = pl.program_id(0)
    geometry_into(cq_ref, ck_ref, t, (ox_ref, oy_ref, dx_ref, dy_ref), True)
    lo16, hi16 = half_masks(BF16)
    lane = lax.broadcasted_iota(jnp.int32, (CH, 128), 1)
    low = lane < 64
    rows = pl.ds(pl.multiple_of(t * TILE, TILE), SPAN)

    def one_pair(p, carry):
        cols = pl.ds(pl.multiple_of(p * 128, 128), 128)
        qp = q_ref[:, cols]
        kp = k_ref[rows, cols]
        vp = v_ref[rows, cols]
        kgp = kg_ref[0, :, cols]
        vgp = vg_ref[0, :, cols]
        s_ref[...] = mm_nt(jnp.concatenate([qp * lo16, qp * hi16], axis=0), kp)
        sf_ref[...] = mm_nt(qp, jnp.concatenate([kgp * lo16, kgp * hi16], axis=0))
        a_ref[...] = mm_nt(jnp.concatenate([qp, qp, qp], axis=1), rq_ref[p]) + rb_ref[p]
        b24 = mm_nt(rk_ref[p], kp)
        b_ref[...] = b24[0:8] + b24[8:16] + b24[16:24]
        for r in range(0, TILE, CH):
            far = sf_ref[r : r + CH, :] * (0.125 * LOG2E)
            tops = []
            held = []
            for e in range(2):
                u0 = (a_ref[r : r + CH, e : e + 1] + b_ref[e : e + 1, :]) * ox_ref[r : r + CH, :]
                u1 = (a_ref[r : r + CH, 2 + e : 3 + e] + b_ref[2 + e : 3 + e, :]) * oy_ref[r : r + CH, :]
                e0 = jnp.exp2(jnp.minimum(u0, -u0))
                e1 = jnp.exp2(jnp.minimum(u1, -u1))
                f0 = 1.0 + e0
                f1 = 1.0 + e1
                rr = 1.0 / (f0 * f1)
                gx = (w_ref[2 * p + e, 0] * dx_ref[r : r + CH, :] - a_ref[r : r + CH, 4 + e : 5 + e]) - b_ref[4 + e : 5 + e, :]
                gy = (w_ref[2 * p + e, 1] * dy_ref[r : r + CH, :] - a_ref[r : r + CH, 6 + e : 7 + e]) - b_ref[6 + e : 7 + e, :]
                s = s_ref[e * TILE + r : e * TILE + r + CH, :] * (0.125 * LOG2E)
                s = s + jnp.minimum(u0, 0.0) + jnp.minimum(u1, 0.0) - gx * gx - gy * gy
                top = jnp.maximum(jnp.maximum(s[:, 0:128], s[:, 128:256]), s[:, 256:384])
                here = low if e == 0 else ~low
                top = jnp.maximum(top, jnp.where(here, far, -3e38))
                tops.append(jnp.max(top, axis=1, keepdims=True))
                g0 = jnp.where(u0 >= 0.0, e0, 1.0) * ox_ref[r : r + CH, :] * (f1 * rr)
                g1 = jnp.where(u1 >= 0.0, e1, 1.0) * oy_ref[r : r + CH, :] * (f0 * rr)
                g0_ref[0, 2 * p + e, r : r + CH, :] = g0.astype(BF16)
                g1_ref[0, 2 * p + e, r : r + CH, :] = g1.astype(BF16)
                held.append((s, rr))
            pfar = jnp.exp2(far - jnp.where(low, tops[0], tops[1]))
            invs = []
            for e in range(2):
                s, rr = held[e]
                pe = jnp.exp2(s - tops[e]) * rr
                here = low if e == 0 else ~low
                tot = pe[:, 0:128] + pe[:, 128:256] + pe[:, 256:384] + jnp.where(here, pfar, 0.0)
                inv = 1.0 / jnp.sum(tot, axis=1, keepdims=True)
                invs.append(inv)
                pn_ref[0, 2 * p + e, r : r + CH, :] = (pe * inv).astype(BF16)
            pf_ref[0, p, r : r + CH, :] = (pfar * jnp.where(low, invs[0], invs[1])).astype(BF16)
        ctx = mm(pn_ref[0, 2 * p], vp * lo16) + mm(pn_ref[0, 2 * p + 1], vp * hi16)
        ctx = ctx + mm(pf_ref[0, p], jnp.concatenate([vgp * lo16, vgp * hi16], axis=0))
        ctx_ref[:, cols] = ctx.astype(BF16)
        return carry

    lax.fori_loop(0, pairs, one_pair, 0)

def bwd_kernel(q_ref, dc_ref, ctx_ref, k_ref, v_ref, kg_ref, vg_ref, cq_ref, ck_ref, rq_ref, rk_ref, rb_ref, rv_ref,
               pn_ref, pf_ref, g0_ref, g1_ref,
               dq_ref, dk_ref, dv_ref, dkg_ref, dvg_ref, db_ref, rqg_ref, th_ref,
               dx_ref, dy_ref, dp_ref, dpf_ref, ds_ref, dsf_ref, a_ref, b_ref, dqr_ref, D_ref, *, pairs, per_block):
    t = pl.program_id(0)

    @pl.when(t == 0)
    def _():
        dk_ref[...] = jnp.zeros_like(dk_ref)
        dv_ref[...] = jnp.zeros_like(dv_ref)
        db_ref[...] = jnp.zeros_like(db_ref)
        rqg_ref[...] = jnp.zeros_like(rqg_ref)
        th_ref[...] = jnp.zeros_like(th_ref)

    @pl.when(t % per_block == 0)
    def _():
        dkg_ref[...] = jnp.zeros_like(dkg_ref)
        dvg_ref[...] = jnp.zeros_like(dvg_ref)

    geometry_into(cq_ref, ck_ref, t, (None, None, dx_ref, dy_ref), False)
    lo16, hi16 = half_masks(BF16)
    lane = lax.broadcasted_iota(jnp.int32, (CH, 128), 1)
    low = lane < 64
    sub = lax.broadcasted_iota(jnp.int32, (128, 1), 0)
    lo16c = (sub < 64).astype(F32).astype(BF16)
    hi16c = (sub >= 64).astype(F32).astype(BF16)
    rows = pl.ds(pl.multiple_of(t * TILE, TILE), SPAN)

    def one_pair(p, carry):
        cols = pl.ds(pl.multiple_of(p * 128, 128), 128)
        qp = q_ref[:, cols]
        dcp = dc_ref[:, cols]
        kp = k_ref[rows, cols]
        vp = v_ref[rows, cols]
        kgp = kg_ref[0, :, cols]
        vgp = vg_ref[0, :, cols]
        kg2 = jnp.concatenate([kgp * lo16, kgp * hi16], axis=0)
        vg2 = jnp.concatenate([vgp * lo16, vgp * hi16], axis=0)
        dp_ref[...] = mm_nt(jnp.concatenate([dcp * lo16, dcp * hi16], axis=0), vp)
        dpf_ref[...] = mm_nt(dcp, vg2)
        a_ref[...] = mm_nt(jnp.concatenate([qp, qp, qp], axis=1), rq_ref[p]) + rb_ref[p]
        b24 = mm_nt(rk_ref[p], kp)
        b_ref[...] = b24[0:8] + b24[8:16] + b24[16:24]
        col_sums = [[jnp.zeros((8, SPAN), F32) for _ in range(4)] for _ in range(2)]
        thetas = [[jnp.zeros((8, 128), F32) for _ in range(2)] for _ in range(2)]
        query_sums = [jnp.zeros((8, 128), F32) for _ in range(4)]
        for r in range(0, TILE, CH):
            prod = dc_ref[r : r + CH, cols].astype(F32) * ctx_ref[r : r + CH, cols].astype(F32)
            row_sums = []
            dots = []
            for e in range(2):
                here = low if e == 0 else ~low
                dot = jnp.sum(jnp.where(here, prod, 0.0), axis=1, keepdims=True)
                dots.append(dot)
                rs = slice(r, r + CH)
                es = slice(e * TILE + r, e * TILE + r + CH)
                ds = pn_ref[0, 2 * p + e, rs, :].astype(F32) * (dp_ref[es, :] - dot)
                ds_ref[es, :] = ds.astype(BF16)
                t0 = ds * g0_ref[0, 2 * p + e, rs, :].astype(F32)
                t1 = ds * g1_ref[0, 2 * p + e, rs, :].astype(F32)
                gx = (dx_ref[rs, :] - a_ref[rs, 4 + e : 5 + e]) - b_ref[4 + e : 5 + e, :]
                gy = (dy_ref[rs, :] - a_ref[rs, 6 + e : 7 + e]) - b_ref[6 + e : 7 + e, :]
                tx = ds * gx
                ty = ds * gy
                xx = tx * gx
                yy = ty * gy
                for i, full in enumerate((xx, yy)):
                    part = full[:, 0:128] + full[:, 128:256] + full[:, 256:384]
                    thetas[e][i] = thetas[e][i] + (part[0:8] + part[8:16])
                sums = []
                for c, full in enumerate((t0, t1, tx, ty)):
                    col_sums[e][c] = col_sums[e][c] + (full[0:8] + full[8:16])
                    sums.append(jnp.sum(full[:, 0:128] + full[:, 128:256] + full[:, 256:384], axis=1, keepdims=True))
                row_sums.append(sums)
            dsf = pf_ref[0, p, r : r + CH, :].astype(F32) * (dpf_ref[r : r + CH, :] - jnp.where(low, dots[0], dots[1]))
            dsf_ref[r : r + CH, :] = dsf.astype(BF16)
            qf = q_ref[r : r + CH, cols].astype(F32)
            dqr = jnp.zeros((CH, 128), F32)
            for c in range(4):
                da = jnp.where(low, row_sums[0][c], row_sums[1][c])
                dqr = dqr + da * rv_ref[p, c : c + 1, :]
                part = da * qf
                query_sums[c] = query_sums[c] + (part[0:8] + part[8:16])
            dqr_ref[r : r + CH, :] = dqr
        for c in range(4):
            rqg_ref[p, c] += query_sums[c]
        for e in range(2):
            for i in range(2):
                th_ref[p, 2 * e + i] += thetas[e][i]
        packed = jnp.concatenate([jnp.sum(col_sums[e][c], axis=0, keepdims=True) for c in range(4) for e in range(2)], axis=0)
        db_ref[p, :, rows] += packed
        dq = mm(ds_ref[0:TILE, :], kp * lo16) + mm(ds_ref[TILE : 2 * TILE, :], kp * hi16) + mm(dsf_ref[...], kg2)
        dq_ref[:, cols] = (dq * 0.125 + dqr_ref[...]).astype(BF16)
        qT = jnp.transpose(qp)
        dcT = jnp.transpose(dcp)
        dk_ref[cols, rows] += mm(jnp.concatenate([qT * lo16c, qT * hi16c], axis=1), ds_ref[...])
        dv_ref[cols, rows] += mm(dcT * lo16c, pn_ref[0, 2 * p]) + mm(dcT * hi16c, pn_ref[0, 2 * p + 1])
        dkg_ref[0, cols, :] += mm(qT, dsf_ref[...])
        dvg_ref[0, cols, :] += mm(dcT, pf_ref[0, p])
        return carry

    lax.fori_loop(0, pairs, one_pair, 0)

def rich_rows(vectors, scale):
    heads = scale.shape[1]
    v = vectors.reshape(4, heads, 64) * scale[:, :, None]
    v = v.reshape(4, heads // 2, 2, 64)
    eye = jnp.eye(2, dtype=F32)
    full = v[:, :, :, None, :] * eye[None, None, :, :, None]
    return full.transpose(1, 0, 2, 3, 4).reshape(heads // 2, 8, 128)

def rich_operands(rich_query, rich_key, rich_bias, scale):
    heads = scale.shape[1]
    rq = jnp.concatenate(split3(rich_rows(rich_query, scale)), axis=2)
    rk = jnp.concatenate(split3(rich_rows(rich_key, scale)), axis=1)
    rb = (rich_bias * scale).reshape(4, heads // 2, 2).transpose(1, 0, 2).reshape(heads // 2, 1, 8)
    return rq, rk, rb

VMEM_LIMIT = 58 * 1024 * 1024

def attn_forward(q, k_pad, v_pad, kg, vg, cq, ck, rich_query, rich_key, rich_bias, rich_theta):
    rows, width = q.shape
    heads = rich_bias.shape[1]
    pairs = heads // 2
    tiles = rows // TILE
    blocks = kg.shape[0]
    per_block = tiles // blocks
    w = rich_theta * math.sqrt(0.5 * LOG2E)
    scale = jnp.concatenate([jnp.full((2, heads), LOG2E, F32), w], axis=0)
    rq, rk, rb = rich_operands(rich_query, rich_key, rich_bias, scale)
    whole = lambda a: pl.BlockSpec(a.shape, lambda t: (0,) * a.ndim)
    return pl.pallas_call(
        partial(fwd_kernel, pairs=pairs),
        grid=(tiles,),
        in_specs=[
            pl.BlockSpec(memory_space=pltpu.SMEM),
            pl.BlockSpec((TILE, width), lambda t: (t, 0)),
            whole(k_pad), whole(v_pad),
            pl.BlockSpec((1,) + kg.shape[1:], lambda t: (t // per_block, 0, 0)),
            pl.BlockSpec((1,) + vg.shape[1:], lambda t: (t // per_block, 0, 0)),
            pl.BlockSpec((TILE, cq.shape[1]), lambda t: (t, 0)),
            whole(ck), whole(rq), whole(rk), whole(rb),
        ],
        out_specs=[
            pl.BlockSpec((TILE, width), lambda t: (t, 0)),
            pl.BlockSpec((1, heads, TILE, SPAN), lambda t: (t, 0, 0, 0)),
            pl.BlockSpec((1, pairs, TILE, 128), lambda t: (t, 0, 0, 0)),
            pl.BlockSpec((1, heads, TILE, SPAN), lambda t: (t, 0, 0, 0)),
            pl.BlockSpec((1, heads, TILE, SPAN), lambda t: (t, 0, 0, 0)),
        ],
        out_shape=[
            jax.ShapeDtypeStruct((rows, width), BF16),
            jax.ShapeDtypeStruct((tiles, heads, TILE, SPAN), BF16),
            jax.ShapeDtypeStruct((tiles, pairs, TILE, 128), BF16),
            jax.ShapeDtypeStruct((tiles, heads, TILE, SPAN), BF16),
            jax.ShapeDtypeStruct((tiles, heads, TILE, SPAN), BF16),
        ],
        scratch_shapes=[
            pltpu.VMEM((TILE, SPAN), F32), pltpu.VMEM((TILE, SPAN), F32),
            pltpu.VMEM((TILE, SPAN), F32), pltpu.VMEM((TILE, SPAN), F32),
            pltpu.VMEM((2 * TILE, SPAN), F32), pltpu.VMEM((TILE, 128), F32),
            pltpu.VMEM((TILE, 8), F32), pltpu.VMEM((8, SPAN), F32),
        ],
        compiler_params=pltpu.CompilerParams(vmem_limit_bytes=VMEM_LIMIT),
        name="attn_forward",
    )(w.T, q, k_pad, v_pad, kg, vg, cq, ck, rq, rk, rb)

def attn_backward(q, dctx, ctx, k_pad, v_pad, kg, vg, cq, ck, rich_query, rich_key, rich_bias, rich_theta, pn, pf, g0, g1):
    rows, width = q.shape
    heads = rich_bias.shape[1]
    pairs = heads // 2
    tiles = rows // TILE
    blocks = kg.shape[0]
    per_block = tiles // blocks
    rq, rk, rb = rich_operands(rich_query, rich_key, rich_bias, jnp.ones((4, heads), F32))
    factor = jnp.concatenate([jnp.ones((2, heads), F32), rich_theta * rich_theta], axis=0)
    rv = (rich_query.reshape(4, heads, 64) * factor[:, :, None]).reshape(4, pairs, 128).transpose(1, 0, 2)
    whole = lambda a: pl.BlockSpec(a.shape, lambda t: (0,) * a.ndim)
    tile_rows = pl.BlockSpec((TILE, width), lambda t: (t, 0))
    padded = k_pad.shape[0]
    outs = pl.pallas_call(
        partial(bwd_kernel, pairs=pairs, per_block=per_block),
        grid=(tiles,),
        in_specs=[
            tile_rows, tile_rows, tile_rows,
            whole(k_pad), whole(v_pad),
            pl.BlockSpec((1,) + kg.shape[1:], lambda t: (t // per_block, 0, 0)),
            pl.BlockSpec((1,) + vg.shape[1:], lambda t: (t // per_block, 0, 0)),
            pl.BlockSpec((TILE, cq.shape[1]), lambda t: (t, 0)),
            whole(ck), whole(rq), whole(rk), whole(rb), whole(rv),
            pl.BlockSpec((1, heads, TILE, SPAN), lambda t: (t, 0, 0, 0)),
            pl.BlockSpec((1, pairs, TILE, 128), lambda t: (t, 0, 0, 0)),
            pl.BlockSpec((1, heads, TILE, SPAN), lambda t: (t, 0, 0, 0)),
            pl.BlockSpec((1, heads, TILE, SPAN), lambda t: (t, 0, 0, 0)),
        ],
        out_specs=[
            tile_rows,
            pl.BlockSpec((width, padded), lambda t: (0, 0)),
            pl.BlockSpec((width, padded), lambda t: (0, 0)),
            pl.BlockSpec((1, width, 128), lambda t: (t // per_block, 0, 0)),
            pl.BlockSpec((1, width, 128), lambda t: (t // per_block, 0, 0)),
            pl.BlockSpec((pairs, 8, padded), lambda t: (0, 0, 0)),
            pl.BlockSpec((pairs, 4, 8, 128), lambda t: (0, 0, 0, 0)),
            pl.BlockSpec((pairs, 4, 8, 128), lambda t: (0, 0, 0, 0)),
        ],
        out_shape=[
            jax.ShapeDtypeStruct((rows, width), BF16),
            jax.ShapeDtypeStruct((width, padded), F32),
            jax.ShapeDtypeStruct((width, padded), F32),
            jax.ShapeDtypeStruct((blocks, width, 128), F32),
            jax.ShapeDtypeStruct((blocks, width, 128), F32),
            jax.ShapeDtypeStruct((pairs, 8, padded), F32),
            jax.ShapeDtypeStruct((pairs, 4, 8, 128), F32),
            jax.ShapeDtypeStruct((pairs, 4, 8, 128), F32),
        ],
        scratch_shapes=[
            pltpu.VMEM((TILE, SPAN), F32), pltpu.VMEM((TILE, SPAN), F32),
            pltpu.VMEM((2 * TILE, SPAN), F32), pltpu.VMEM((TILE, 128), F32),
            pltpu.VMEM((2 * TILE, SPAN), BF16), pltpu.VMEM((TILE, 128), BF16),
            pltpu.VMEM((TILE, 8), F32), pltpu.VMEM((8, SPAN), F32),
            pltpu.VMEM((TILE, 128), F32), pltpu.VMEM((TILE, 128), F32),
        ],
        compiler_params=pltpu.CompilerParams(vmem_limit_bytes=VMEM_LIMIT),
        name="attn_backward",
    )(q, dctx, ctx, k_pad, v_pad, kg, vg, cq, ck, rq, rk, rb, rv, pn, pf, g0, g1)
    dq, dkT, dvT, dkgT, dvgT, db, rqg, th = outs
    dbh = db.reshape(pairs, 4, 2, padded).transpose(1, 0, 2, 3).reshape(4, heads, padded) * factor[:, :, None]
    bias_grad = jnp.sum(dbh, axis=2)
    theta_grad = -rich_theta * jnp.sum(th, axis=(2, 3)).reshape(pairs, 2, 2).transpose(2, 0, 1).reshape(2, heads)
    rich_query_grad = (jnp.sum(rqg, axis=2).transpose(1, 0, 2).reshape(4, heads, 64) * factor[:, :, None]).reshape(4, width)
    kvec = rich_key.reshape(4, heads, 64)
    dk_rich = jnp.einsum("chs,che->hes", dbh, kvec, precision=HIGHEST).reshape(width, padded)
    rich_key_grad = jnp.einsum("chs,she->che", dbh, k_pad.astype(F32).reshape(padded, heads, 64), precision=HIGHEST).reshape(4, width)
    dkT = dkT * 0.125 + dk_rich

    def pick(full, factor):
        f = full.reshape(blocks, pairs, 2, 64, 2, 64)
        own = jnp.stack([f[:, :, 0, :, 0, :], f[:, :, 1, :, 1, :]], axis=2)
        return own.transpose(0, 4, 1, 2, 3).reshape(blocks, 64, width) * factor

    return dq, dkT, dvT, pick(dkgT, 0.125), pick(dvgT, 1.0), rich_query_grad, rich_key_grad, bias_grad, theta_grad


def body(
    tokens,
    global_states,
    cotangent,
    w_qkv,
    w_out,
    w_up,
    w_down,
    first_gain,
    first_shift,
    second_gain,
    second_shift,
    rich_query,
    rich_key,
    rich_bias,
    rich_theta,
    bucket_units,
    form_lengths,
    coords,
    glob_owner,
):
    row_count = tokens.shape[1]
    model_width = tokens.shape[2]
    stream_len = row_count * lax.axis_size("seq")
    offset = lax.axis_index("seq") * row_count
    block_count = row_count // QBLOCK
    starts = bucket_starts(bucket_units[0])
    lengths = form_lengths[0]
    coord_pad = jnp.pad(coords[0], ((0, 0), (RADIUS, RADIUS)))

    block_row = offset + QBLOCK * jnp.arange(block_count, dtype=jnp.int32)
    block_form = locate(block_row, starts, lengths, stream_len)[0]
    matches = (glob_owner[0][None, :] == block_form[:, None]).astype(jnp.int32)
    ranks = jnp.cumsum(matches, axis=1) - 1
    slots = jnp.arange(GLOB_FORM, dtype=jnp.int32)
    picked = (matches[:, None, :] == 1) & (ranks[:, None, :] == slots[None, :, None])
    picked = picked.reshape(block_count * GLOB_FORM, glob_owner.shape[1])

    pos_key = offset - RADIUS + jnp.arange(row_count + 2 * RADIUS, dtype=jnp.int32)
    form_key, live_key = locate(pos_key, starts, lengths, stream_len)
    coord_key = lax.dynamic_slice_in_dim(coord_pad, offset, row_count + 2 * RADIUS, 1)
    key_info = jnp.concatenate(
        [
            coord_key.astype(jnp.float32),
            jnp.where(live_key, form_key, -1).astype(jnp.float32)[None],
            jnp.zeros((5, row_count + 2 * RADIUS), jnp.float32),
        ],
        axis=0,
    )
    form_query = jnp.repeat(block_form, QBLOCK).astype(jnp.float32)
    query_info = jnp.stack(
        [
            coord_key[0, RADIUS : RADIUS + row_count].astype(jnp.float32),
            coord_key[1, RADIUS : RADIUS + row_count].astype(jnp.float32),
            form_query,
            jnp.zeros_like(form_query),
        ],
        axis=1,
    )

    every_glob = lax.all_gather(global_states[0], "seq", axis=0, tiled=True)
    inputs = tokens[0].astype(jnp.float32)
    norm_first, pull_first = jax.vjp(layer_norm, inputs, first_gain, first_shift)
    hidden_one = norm_first.astype(jnp.bfloat16)
    projected = jnp.dot(hidden_one, w_qkv, preferred_element_type=jnp.float32).astype(jnp.bfloat16)
    queries = projected[:, :model_width]
    stacked_pairs = jnp.stack(
        [projected[:, model_width : 2 * model_width], projected[:, 2 * model_width :]]
    )
    padded_pairs = padded(stacked_pairs, (("seq", 1),), RADIUS)
    key_pad = padded_pairs[0]
    value_pad = padded_pairs[1]
    pick_low = picked.astype(jnp.bfloat16)
    glob_in = jnp.dot(pick_low, every_glob, preferred_element_type=jnp.float32)
    glob_hidden = layer_norm(glob_in, first_gain, first_shift).astype(jnp.bfloat16)
    w_pair = w_qkv[:, model_width:]
    glob_pairs = jnp.dot(glob_hidden, w_pair, preferred_element_type=jnp.float32)
    glob_pairs = glob_pairs.astype(jnp.bfloat16).reshape(block_count, GLOB_FORM, 2 * model_width)
    glob_keys = glob_pairs[:, :, :model_width]
    glob_values = glob_pairs[:, :, model_width:]
    pull_glob = jax.vjp(
        layer_norm, global_states[0].astype(jnp.float32), first_gain, first_shift
    )[1]
    rich = (rich_query, rich_key, rich_bias, rich_theta)
    context_low, *kept = attn_forward(
        queries, key_pad, value_pad, glob_keys, glob_values, query_info, key_info, *rich
    )
    middle = inputs + jnp.dot(context_low, w_out, preferred_element_type=jnp.float32)
    norm_second, pull_second = jax.vjp(layer_norm, middle, second_gain, second_shift)
    hidden_two = norm_second.astype(jnp.bfloat16)
    pre_act = jnp.dot(hidden_two, w_up, preferred_element_type=jnp.float32)
    activated, pull_gelu = jax.vjp(gelu_exact, pre_act)
    act_low = activated.astype(jnp.bfloat16)
    layer_out = (middle + jnp.dot(act_low, w_down, preferred_element_type=jnp.float32)).astype(
        jnp.bfloat16
    )
    grad_branch = cotangent[0]
    grad_w_down = jnp.einsum("nf,nd->fd", act_low, grad_branch, preferred_element_type=jnp.float32)
    grad_act = jnp.einsum("nd,fd->nf", grad_branch, w_down, preferred_element_type=jnp.float32)
    grad_pre = pull_gelu(grad_act)[0].astype(jnp.bfloat16)
    grad_w_up = jnp.einsum("nd,nf->df", hidden_two, grad_pre, preferred_element_type=jnp.float32)
    grad_hidden_two = jnp.einsum("nf,df->nd", grad_pre, w_up, preferred_element_type=jnp.float32)
    grad_middle_norm, grad_second_gain, grad_second_shift = pull_second(grad_hidden_two)
    grad_middle = grad_branch.astype(jnp.float32) + grad_middle_norm
    grad_attn = grad_middle.astype(jnp.bfloat16)
    grad_w_out = jnp.einsum("nd,ne->de", context_low, grad_attn, preferred_element_type=jnp.float32)
    grad_context = jnp.einsum(
        "ne,de->nd", grad_attn, w_out, preferred_element_type=jnp.float32
    ).astype(jnp.bfloat16)

    (
        query_grads,
        grad_key_pad,
        grad_value_pad,
        grad_glob_key,
        grad_glob_value,
        rich_query_grad,
        rich_key_grad,
        grad_shift,
        grad_width,
    ) = attn_backward(
        queries, grad_context, context_low, key_pad, value_pad, glob_keys, glob_values,
        query_info, key_info, *rich, *kept
    )
    grad_pads = jnp.stack([grad_key_pad.T, grad_value_pad.T])
    rim_send = jnp.concatenate([grad_pads[:, :RADIUS], grad_pads[:, row_count + RADIUS :]], axis=1)
    rim_back = padded(rim_send.astype(jnp.bfloat16), (("seq", 1),), RADIUS).astype(rim_send.dtype)
    own_pairs = grad_pads[:, RADIUS : RADIUS + row_count]
    own_pairs = own_pairs.at[:, :RADIUS].add(rim_back[:, :RADIUS])
    own_pairs = own_pairs.at[:, row_count - RADIUS :].add(rim_back[:, 3 * RADIUS :])
    grad_projected = jnp.concatenate(
        [query_grads, own_pairs[0].astype(jnp.bfloat16), own_pairs[1].astype(jnp.bfloat16)], axis=1
    )
    glob_grad_own = jnp.concatenate([grad_glob_key, grad_glob_value], axis=2).reshape(
        block_count * GLOB_FORM, 2 * model_width
    )
    grad_w_pair = jnp.dot(glob_hidden.astype(jnp.float32).T, glob_grad_own, precision=HIGHEST)
    grad_glob_part = jnp.dot(glob_grad_own, w_pair.astype(jnp.float32).T, precision=HIGHEST)
    grad_glob_part = jnp.dot(picked.astype(jnp.float32).T, grad_glob_part, precision=HIGHEST)
    grad_glob_hidden = lax.psum_scatter(
        grad_glob_part.astype(jnp.bfloat16), "seq", scatter_dimension=0, tiled=True
    ).astype(jnp.float32)
    grad_w_qkv = jnp.einsum(
        "nd,ne->de", hidden_one, grad_projected, preferred_element_type=jnp.float32
    )
    grad_w_qkv = jnp.concatenate(
        [grad_w_qkv[:, :model_width], grad_w_qkv[:, model_width:] + grad_w_pair], axis=1
    )
    grad_hidden_one = jnp.einsum(
        "ne,de->nd", grad_projected, w_qkv, preferred_element_type=jnp.float32
    )
    grad_inputs_norm, grad_gain_tokens, grad_shift_tokens = pull_first(grad_hidden_one)
    grad_glob_in, grad_gain_globals, grad_shift_globals = pull_glob(grad_glob_hidden)
    tokens_grad = (grad_middle + grad_inputs_norm).astype(jnp.bfloat16)
    glob_grad = grad_glob_in.astype(jnp.bfloat16)
    grad_first_gain = grad_gain_tokens + grad_gain_globals
    grad_first_shift = grad_shift_tokens + grad_shift_globals
    every_share = (
        lax.psum_scatter(
            grad_w_up.astype(jnp.bfloat16), "seq", scatter_dimension=0, tiled=True
        ).astype(jnp.float32),
        lax.psum_scatter(
            grad_w_down.astype(jnp.bfloat16), "seq", scatter_dimension=0, tiled=True
        ).astype(jnp.float32),
        lax.psum_scatter(
            grad_second_gain.astype(jnp.bfloat16), "seq", scatter_dimension=0, tiled=True
        ).astype(jnp.float32),
        lax.psum_scatter(
            grad_second_shift.astype(jnp.bfloat16), "seq", scatter_dimension=0, tiled=True
        ).astype(jnp.float32),
        lax.psum_scatter(
            grad_w_qkv.astype(jnp.bfloat16), "seq", scatter_dimension=0, tiled=True
        ).astype(jnp.float32),
        lax.psum_scatter(
            grad_w_out.astype(jnp.bfloat16), "seq", scatter_dimension=0, tiled=True
        ).astype(jnp.float32),
        lax.psum_scatter(
            grad_first_gain.astype(jnp.bfloat16), "seq", scatter_dimension=0, tiled=True
        ).astype(jnp.float32),
        lax.psum_scatter(
            grad_first_shift.astype(jnp.bfloat16), "seq", scatter_dimension=0, tiled=True
        ).astype(jnp.float32),
        lax.psum_scatter(
            rich_query_grad.astype(jnp.bfloat16), "seq", scatter_dimension=1, tiled=True
        ).astype(jnp.float32),
        lax.psum_scatter(
            rich_key_grad.astype(jnp.bfloat16), "seq", scatter_dimension=1, tiled=True
        ).astype(jnp.float32),
    )
    every_share = (
        lax.psum(every_share[0].astype(jnp.bfloat16), "stream").astype(jnp.float32),
        lax.psum(every_share[1].astype(jnp.bfloat16), "stream").astype(jnp.float32),
        lax.psum(every_share[2].astype(jnp.bfloat16), "stream").astype(jnp.float32),
        lax.psum(every_share[3].astype(jnp.bfloat16), "stream").astype(jnp.float32),
        lax.psum(every_share[4].astype(jnp.bfloat16), "stream").astype(jnp.float32),
        lax.psum(every_share[5].astype(jnp.bfloat16), "stream").astype(jnp.float32),
        lax.psum(every_share[6].astype(jnp.bfloat16), "stream").astype(jnp.float32),
        lax.psum(every_share[7].astype(jnp.bfloat16), "stream").astype(jnp.float32),
        lax.psum(every_share[8].astype(jnp.bfloat16), "stream").astype(jnp.float32),
        lax.psum(every_share[9].astype(jnp.bfloat16), "stream").astype(jnp.float32),
    )
    ffn_shares = every_share[:4]
    attn_shares = every_share[4:]
    small_sums = lax.psum((grad_shift, grad_width), ("stream", "seq"))
    return (
        layer_out[None],
        tokens_grad[None],
        glob_grad[None],
        attn_shares[0],
        attn_shares[1],
        ffn_shares[0],
        ffn_shares[1],
        attn_shares[2],
        attn_shares[3],
        ffn_shares[2],
        ffn_shares[3],
        attn_shares[4],
        attn_shares[5],
        small_sums[0],
        small_sums[1],
    )


def solution(mesh):
    return jax.shard_map(
        body,
        mesh=mesh,
        in_specs=(
            P("stream", "seq", None),
            P("stream", "seq", None),
            P("stream", "seq", None),
            P(),
            P(),
            P(),
            P(),
            P(),
            P(),
            P(),
            P(),
            P(),
            P(),
            P(),
            P(),
            P("stream", None),
            P("stream", None),
            P("stream", None, None),
            P("stream", None),
        ),
        out_specs=(
            P("stream", "seq", None),
            P("stream", "seq", None),
            P("stream", "seq", None),
            P("seq", None),
            P("seq", None),
            P("seq", None),
            P("seq", None),
            P("seq"),
            P("seq"),
            P("seq"),
            P("seq"),
            P(None, "seq"),
            P(None, "seq"),
            P(),
            P(),
        ),
        check_vma=False,
    )
```

```python
from functools import partial
import math

import jax
import jax.numpy as jnp
from jax import lax
from jax.experimental import pallas as pl
from jax.experimental.pallas import tpu as pltpu
from jax.sharding import PartitionSpec as P

RADIUS = 128
GLOB_FORM = 64
QBLOCK = 512
TOK_DEV = 1024


EPSILON = 1e-06


TILE = 128
SPAN = 384
LOG2E = math.log2(math.e)
FAR_AWAY = 1e15
CH = 16
F32 = jnp.float32
BF16 = jnp.bfloat16
VMEM_LIMIT = 58 * 1024 * 1024


def mm(a, b):
    return lax.dot_general(a, b, (((1,), (0,)), ((), ())), preferred_element_type=F32)


def mm_nt(a, b):
    return lax.dot_general(a, b, (((1,), (1,)), ((), ())), preferred_element_type=F32)


def mm_tn(a, b):
    return lax.dot_general(a, b, (((0,), (0,)), ((), ())), preferred_element_type=F32)


def norm_parts(values):
    centre = jnp.mean(values, axis=-1, keepdims=True)
    centred = values - centre
    spread = jnp.mean(centred * centred, axis=-1, keepdims=True)
    scale = lax.rsqrt(spread + EPSILON)
    return centred * scale, scale


def norm_pull(grad, normed, scale, gain):
    e = grad * gain
    mean_e = jnp.mean(e, axis=-1, keepdims=True)
    mean_en = jnp.mean(e * normed, axis=-1, keepdims=True)
    return scale * (e - mean_e - normed * mean_en)


def split3(values):
    hi = values.astype(BF16).astype(F32)
    rest = values - hi
    mid = rest.astype(BF16).astype(F32)
    return hi, mid, rest - mid


def half_masks(dtype):
    lane = lax.broadcasted_iota(jnp.int32, (1, 128), 1)
    low = (lane < 64).astype(F32)
    return low.astype(dtype), (1.0 - low).astype(dtype)


def by_row(values):
    row = lax.broadcasted_iota(jnp.int32, (8, 128), 0)
    out = jnp.full((8, 128), values[7], F32)
    for index in range(7):
        out = jnp.where(row == index, values[index], out)
    return out


def rich_rows(vectors, scales):
    row = lax.broadcasted_iota(jnp.int32, (8, 128), 0)
    lane = lax.broadcasted_iota(jnp.int32, (8, 128), 1)
    both = jnp.concatenate([vectors, vectors], axis=0)
    both = both if scales is None else both * scales
    return jnp.where((row < 4) == (lane < 64), both, 0.0)


def rich_sums(qp, kp, query_vec, key_vec, scales, bias8):
    rq = jnp.concatenate(split3(rich_rows(query_vec, scales)), axis=1).astype(BF16)
    rk = jnp.concatenate(split3(rich_rows(key_vec, scales)), axis=0).astype(BF16)
    a = mm_nt(jnp.concatenate([qp, qp, qp], axis=1), rq)
    b24 = mm_nt(rk, kp)
    return a, b24[0:8] + b24[8:16] + b24[16:24] + bias8[:, 0:1]


def form_of(units_ref, lengths_ref, row):
    form, low, high, before = 0, 0, lengths_ref[0, 0], 0
    for index in range(1, units_ref.shape[1]):
        before = before + units_ref[0, index - 1]
        start = TOK_DEV // 2 + TOK_DEV * before
        taken = row >= start
        form = jnp.where(taken, index, form)
        low = jnp.where(taken, start, low)
        high = jnp.where(taken, start + lengths_ref[0, index], high)
    return form, low, high


def coord_row(coords_ref, axis, tile_index):
    tile_index = jnp.clip(tile_index, 0, coords_ref.shape[1] // 128 - 1)
    return coords_ref[axis : axis + 1, pl.ds(pl.multiple_of(tile_index * 128, 128), 128)].astype(F32)


def query_columns(coords_ref, axis, tile_index):
    return jnp.transpose(jnp.broadcast_to(coord_row(coords_ref, axis, tile_index), (128, 128)))


def geometry_into(coords_ref, first_tile, span, refs):
    ox_ref, oy_ref, dx_ref, dy_ref = refs
    xq = query_columns(coords_ref, 0, first_tile + 1)
    yq = query_columns(coords_ref, 1, first_tile + 1)
    for lt in range(3):
        xk = coord_row(coords_ref, 0, first_tile + lt)
        yk = coord_row(coords_ref, 1, first_tile + lt)
        out = (slice(None), slice(lt * 128, lt * 128 + 128))
        dx = jnp.log(1.0 + jnp.abs(xq - xk))
        dy = jnp.log(1.0 + jnp.abs(yq - yk))
        if span is not None:
            row = lax.broadcasted_iota(jnp.int32, (128, 128), 0)
            col = lax.broadcasted_iota(jnp.int32, (128, 128), 1) + lt * 128
            near = (col >= row) & (col - row <= 2 * RADIUS)
            dx = jnp.where(near & (col >= span[0]) & (col < span[1]), dx, FAR_AWAY)
            ox_ref[out] = jnp.where(xk > xq, 1.0, -1.0)
            oy_ref[out] = jnp.where(yk > yq, 1.0, -1.0)
        dx_ref[out] = dx
        dy_ref[out] = dy


def qkv_kernel(tok_ref, w_ref, norms_ref, q_ref, k_ref, v_ref, ht_ref):
    width = tok_ref.shape[1]
    normed, _ = norm_parts(tok_ref[...].astype(F32))
    hidden = (normed * norms_ref[0:1, :] + norms_ref[1:2, :]).astype(BF16)
    for index, out in enumerate((q_ref, k_ref, v_ref)):
        out[...] = mm(hidden, w_ref[:, index * width : (index + 1) * width]).astype(BF16)
    ht_ref[...] = jnp.transpose(hidden)


def project_tokens(tokens, w_qkv, norms):
    rows, width = tokens.shape
    step = 256
    block = pl.BlockSpec((step, width), lambda i: (i, 0))
    return pl.pallas_call(
        qkv_kernel,
        grid=(rows // step,),
        in_specs=[block, pl.BlockSpec(w_qkv.shape, lambda i: (0, 0)), pl.BlockSpec(norms.shape, lambda i: (0, 0))],
        out_specs=[block, block, block, pl.BlockSpec((width, step), lambda i: (0, i))],
        out_shape=[jax.ShapeDtypeStruct((rows, width), BF16)] * 3 + [jax.ShapeDtypeStruct((width, rows), BF16)],
        compiler_params=pltpu.CompilerParams(vmem_limit_bytes=VMEM_LIMIT),
        cost_estimate=cost(8.0),
        name="project_tokens",
    )(tokens, w_qkv, norms)


def cost(micros):
    return pl.CostEstimate(flops=int(micros * 1e9), bytes_accessed=0, transcendentals=0)


def global_pairs(form, owner_ref, glob_ref, norms_ref, kw_ref, vw_ref, kg_ref, vg_ref, hg_ref, ng_ref, oh_ref):
    count = glob_ref.shape[0]
    match = (owner_ref[...] == form).astype(F32)
    row = lax.broadcasted_iota(jnp.int32, (count, count), 0)
    col = lax.broadcasted_iota(jnp.int32, (count, count), 1)
    upto = (row <= col).astype(F32).astype(BF16)
    rank = mm(jnp.broadcast_to(match, (16, count)).astype(BF16), upto)[0:1]
    slot = lax.broadcasted_iota(jnp.int32, (GLOB_FORM, count), 0).astype(F32) + 1.0
    picked = jnp.where(rank == slot, match, 0.0).astype(BF16)
    oh_ref[0] = picked
    normed, _ = norm_parts(mm(picked, glob_ref[...]))
    ng_ref[0] = normed
    hidden = (normed * norms_ref[0:1, :] + norms_ref[1:2, :]).astype(BF16)
    hg_ref[0] = hidden
    kg_ref[0] = mm(hidden, kw_ref[...]).astype(BF16)
    vg_ref[0] = mm(hidden, vw_ref[...]).astype(BF16)


def fwd_kernel(units_ref, lengths_ref, offset_ref, bias_ref, theta_ref,
               q_ref, k_ref, v_ref, before_ref, after_ref, glob_ref, owner_ref, kw_ref, vw_ref, norms_ref,
               coords_ref, rq_ref, rk_ref,
               ctx_ref, pn_ref, pf_ref, g0_ref, g1_ref, kp_ref, vp_ref, kg_ref, vg_ref, hg_ref, ng_ref, oh_ref,
               ox_ref, oy_ref, dx_ref, dy_ref, s_ref, sf_ref, a_ref, b_ref, *, pairs, per_block):
    t = pl.program_id(0)
    rows_all = k_ref.shape[0]
    offset = offset_ref[0, 0]
    first = offset + t * TILE
    form, low_end, high_end = form_of(units_ref, lengths_ref, first)

    @pl.when(t == 0)
    def _():
        for refs in ((k_ref, kp_ref, kw_ref), (v_ref, vp_ref, vw_ref)):
            own, padded_ref, weight = refs
            padded_ref[RADIUS : RADIUS + rows_all, :] = own[...]
        for halo, start in ((before_ref, 0), (after_ref, RADIUS + rows_all)):
            normed, _ = norm_parts(halo[...].astype(F32))
            hidden = (normed * norms_ref[0:1, :] + norms_ref[1:2, :]).astype(BF16)
            kp_ref[start : start + RADIUS, :] = mm(hidden, kw_ref[...]).astype(BF16)
            vp_ref[start : start + RADIUS, :] = mm(hidden, vw_ref[...]).astype(BF16)

    @pl.when(t % per_block == 0)
    def _():
        global_pairs(form, owner_ref, glob_ref, norms_ref, kw_ref, vw_ref, kg_ref, vg_ref, hg_ref, ng_ref, oh_ref)

    shifted = first - RADIUS
    geometry_into(coords_ref, offset // 128 + t - 1, (low_end - shifted, high_end - shifted), (ox_ref, oy_ref, dx_ref, dy_ref))
    lo16, hi16 = half_masks(BF16)
    lane = lax.broadcasted_iota(jnp.int32, (CH, 128), 1)
    low = lane < 64
    rows = pl.ds(pl.multiple_of(t * TILE, TILE), SPAN)
    root = math.sqrt(0.5 * LOG2E)

    def one_pair(p, carry):
        cols = pl.ds(pl.multiple_of(p * 128, 128), 128)
        qp = q_ref[:, cols]
        kp = kp_ref[rows, cols]
        vp = vp_ref[rows, cols]
        kgp = kg_ref[0, :, cols]
        vgp = vg_ref[0, :, cols]
        widths = [[theta_ref[i, 2 * p + e] * root for i in range(2)] for e in range(2)]
        scales = by_row([LOG2E, LOG2E] + widths[0] + [LOG2E, LOG2E] + widths[1])
        biases = by_row([bias_ref[c, 2 * p + e] for e in range(2) for c in range(4)]) * scales
        s_ref[...] = mm_nt(jnp.concatenate([qp * lo16, qp * hi16], axis=0), kp)
        sf_ref[...] = mm_nt(qp, jnp.concatenate([kgp * lo16, kgp * hi16], axis=0))
        a, b = rich_sums(qp, kp, rq_ref[:, cols], rk_ref[:, cols], scales, biases)
        a_ref[...] = a
        b_ref[...] = b
        for r in range(0, TILE, CH):
            rs = slice(r, r + CH)
            far = sf_ref[rs, :] * (0.125 * LOG2E)
            tops = []
            held = []
            for e in range(2):
                base = 4 * e
                part = [a_ref[rs, base + c : base + c + 1] for c in range(4)]
                line = [b_ref[base + c : base + c + 1, :] for c in range(4)]
                u0 = (part[0] + line[0]) * ox_ref[rs, :]
                u1 = (part[1] + line[1]) * oy_ref[rs, :]
                e0 = jnp.exp2(jnp.minimum(u0, -u0))
                e1 = jnp.exp2(jnp.minimum(u1, -u1))
                f0 = 1.0 + e0
                f1 = 1.0 + e1
                rr = 1.0 / (f0 * f1)
                gx = (widths[e][0] * dx_ref[rs, :] - part[2]) - line[2]
                gy = (widths[e][1] * dy_ref[rs, :] - part[3]) - line[3]
                s = s_ref[e * TILE + r : e * TILE + r + CH, :] * (0.125 * LOG2E)
                s = s + jnp.minimum(u0, 0.0) + jnp.minimum(u1, 0.0) - gx * gx - gy * gy
                top = jnp.maximum(jnp.maximum(s[:, 0:128], s[:, 128:256]), s[:, 256:384])
                here = low if e == 0 else ~low
                top = jnp.maximum(top, jnp.where(here, far, -3e38))
                tops.append(jnp.max(top, axis=1, keepdims=True))
                g0 = jnp.where(u0 >= 0.0, e0, 1.0) * ox_ref[rs, :] * (f1 * rr)
                g1 = jnp.where(u1 >= 0.0, e1, 1.0) * oy_ref[rs, :] * (f0 * rr)
                g0_ref[0, 2 * p + e, rs, :] = g0.astype(BF16)
                g1_ref[0, 2 * p + e, rs, :] = g1.astype(BF16)
                held.append((s, rr))
            pfar = jnp.exp2(far - jnp.where(low, tops[0], tops[1]))
            invs = []
            for e in range(2):
                s, rr = held[e]
                pe = jnp.exp2(s - tops[e]) * rr
                here = low if e == 0 else ~low
                tot = pe[:, 0:128] + pe[:, 128:256] + pe[:, 256:384] + jnp.where(here, pfar, 0.0)
                inv = 1.0 / jnp.sum(tot, axis=1, keepdims=True)
                invs.append(inv)
                pn_ref[0, 2 * p + e, rs, :] = (pe * inv).astype(BF16)
            pf_ref[0, p, rs, :] = (pfar * jnp.where(low, invs[0], invs[1])).astype(BF16)
        ctx = mm(pn_ref[0, 2 * p], vp * lo16) + mm(pn_ref[0, 2 * p + 1], vp * hi16)
        ctx = ctx + mm(pf_ref[0, p], jnp.concatenate([vgp * lo16, vgp * hi16], axis=0))
        ctx_ref[:, cols] = ctx.astype(BF16)
        return carry

    lax.fori_loop(0, pairs, one_pair, 0)


def attn_forward(q, k, v, before, after, every_glob, owner, w_qkv, norms, coords, units, lengths, offset, rich):
    rich_query, rich_key, rich_bias, rich_theta = rich
    rows, width = q.shape
    heads = rich_bias.shape[1]
    pairs = heads // 2
    tiles = rows // TILE
    blocks = rows // QBLOCK
    per_block = tiles // blocks
    padded_rows = rows + 2 * RADIUS
    globs = every_glob.shape[0]
    scalars = pl.BlockSpec(memory_space=pltpu.SMEM)

    def whole(*shape):
        return pl.BlockSpec(shape, lambda t: (0,) * len(shape))

    def block3(*shape):
        return pl.BlockSpec((1,) + shape, lambda t: (t // per_block, 0, 0))

    near = pl.BlockSpec((1, heads, TILE, SPAN), lambda t: (t, 0, 0, 0))
    near_shape = jax.ShapeDtypeStruct((tiles, heads, TILE, SPAN), BF16)
    tile_rows = pl.BlockSpec((TILE, width), lambda t: (t, 0))
    return pl.pallas_call(
        partial(fwd_kernel, pairs=pairs, per_block=per_block),
        grid=(tiles,),
        in_specs=[
            scalars, scalars, scalars, scalars, scalars,
            tile_rows, whole(rows, width), whole(rows, width),
            whole(RADIUS, width), whole(RADIUS, width),
            whole(globs, width), whole(1, globs),
            pl.BlockSpec((width, width), lambda t: (0, 1)),
            pl.BlockSpec((width, width), lambda t: (0, 2)),
            whole(*norms.shape),
            whole(*coords.shape), whole(4, width), whole(4, width),
        ],
        out_specs=[
            tile_rows, near,
            pl.BlockSpec((1, pairs, TILE, 128), lambda t: (t, 0, 0, 0)),
            near, near,
            whole(padded_rows, width), whole(padded_rows, width),
            block3(GLOB_FORM, width), block3(GLOB_FORM, width), block3(GLOB_FORM, width),
            block3(GLOB_FORM, width), block3(GLOB_FORM, globs),
        ],
        out_shape=[
            jax.ShapeDtypeStruct((rows, width), BF16),
            near_shape,
            jax.ShapeDtypeStruct((tiles, pairs, TILE, 128), BF16),
            near_shape, near_shape,
            jax.ShapeDtypeStruct((padded_rows, width), BF16),
            jax.ShapeDtypeStruct((padded_rows, width), BF16),
            jax.ShapeDtypeStruct((blocks, GLOB_FORM, width), BF16),
            jax.ShapeDtypeStruct((blocks, GLOB_FORM, width), BF16),
            jax.ShapeDtypeStruct((blocks, GLOB_FORM, width), BF16),
            jax.ShapeDtypeStruct((blocks, GLOB_FORM, width), F32),
            jax.ShapeDtypeStruct((blocks, GLOB_FORM, globs), BF16),
        ],
        scratch_shapes=[
            pltpu.VMEM((TILE, SPAN), F32), pltpu.VMEM((TILE, SPAN), F32),
            pltpu.VMEM((TILE, SPAN), F32), pltpu.VMEM((TILE, SPAN), F32),
            pltpu.VMEM((2 * TILE, SPAN), F32), pltpu.VMEM((TILE, 128), F32),
            pltpu.VMEM((TILE, 8), F32), pltpu.VMEM((8, SPAN), F32),
        ],
        compiler_params=pltpu.CompilerParams(vmem_limit_bytes=VMEM_LIMIT),
        cost_estimate=cost(65.0),
        name="attn_forward",
    )(units, lengths, offset, rich_bias, rich_theta, q, k, v, before, after, every_glob, owner,
      w_qkv, w_qkv, norms, coords, rich_query, rich_key)


def bwd_kernel(offset_ref, bias_ref, theta_ref,
               q_ref, dc_ref, ctx_ref, k_ref, v_ref, kg_ref, vg_ref, coords_ref, rq_ref, rk_ref,
               pn_ref, pf_ref, g0_ref, g1_ref,
               dq_ref, dk_ref, dv_ref, dkg_ref, dvg_ref, vec_ref,
               dx_ref, dy_ref, dp_ref, dpf_ref, ds_ref, dsf_ref, a_ref, b_ref, dqr_ref, db_ref,
               *, pairs, first_pair, tiles, per_block, edge):
    step = pl.program_id(0)
    t = step * (tiles - 1) if edge else step + 1

    @pl.when(step == 0)
    def _():
        vec_ref[...] = jnp.zeros_like(vec_ref)
        if not edge:
            dk_ref[...] = jnp.zeros_like(dk_ref)
            dv_ref[...] = jnp.zeros_like(dv_ref)
            db_ref[...] = jnp.zeros_like(db_ref)

    if edge:
        fresh = step >= 0
    else:
        fresh = (step == 0) | (t % per_block == 0)

    @pl.when(fresh)
    def _():
        dkg_ref[...] = jnp.zeros_like(dkg_ref)
        dvg_ref[...] = jnp.zeros_like(dvg_ref)

    geometry_into(coords_ref, offset_ref[0, 0] // 128 + t - 1, None, (None, None, dx_ref, dy_ref))
    lo16, hi16 = half_masks(BF16)
    lane = lax.broadcasted_iota(jnp.int32, (CH, 128), 1)
    low = lane < 64
    low64 = lax.broadcasted_iota(jnp.int32, (64, 128), 1) < 64
    lane8 = lax.broadcasted_iota(jnp.int32, (4, 128), 1)
    lane1 = lax.broadcasted_iota(jnp.int32, (1, 128), 1)
    sub = lax.broadcasted_iota(jnp.int32, (128, 1), 0)
    lo16c = (sub < 64).astype(F32).astype(BF16)
    hi16c = (sub >= 64).astype(F32).astype(BF16)
    rows = pl.ds(pl.multiple_of(t * TILE, TILE), SPAN)
    out_rows = pl.ds(pl.multiple_of((t - 1) * TILE, TILE), SPAN)

    def rich_key_parts(p, cols, sums, keys, columns):
        head = 2 * (p + first_pair)
        squares = [theta_ref[i, head + e] * theta_ref[i, head + e] for e in range(2) for i in range(2)]
        scales = by_row([1.0, 1.0, squares[0], squares[1], 1.0, 1.0, squares[2], squares[3]])
        scaled = sums * scales[:, 0:1]
        vectors = jnp.concatenate(split3(rich_rows(rk_ref[:, cols], None)), axis=0)
        parts = split3(scaled)
        left = jnp.concatenate([vectors[0:8]] * 3 + [vectors[8:16]] * 2 + [vectors[16:24]], axis=0)
        left = jnp.transpose(left).astype(BF16)
        right = jnp.concatenate([parts[0], parts[1], parts[2], parts[0], parts[1], parts[0]], axis=0).astype(BF16)
        extra = mm(left, right)
        stacked = jnp.concatenate(parts, axis=0).astype(BF16)
        key24 = mm(stacked, keys)
        key8 = key24[0:8] + key24[8:16] + key24[16:24]
        vec_ref[p, 4:8, :] += jnp.where(lane8 < 64, key8[0:4], key8[4:8])
        totals = jnp.sum(scaled, axis=1, keepdims=True)
        line = jnp.zeros((1, 128), F32)
        for index in range(8):
            line = jnp.where(lane1 == index, totals[index : index + 1, :], line)
        vec_ref[p, 8:9, :] += line
        return extra

    def one_pair(p, carry):
        cols = pl.ds(pl.multiple_of(p * 128, 128), 128)
        head = 2 * (p + first_pair)
        qp = q_ref[:, cols]
        dcp = dc_ref[:, cols]
        kp = k_ref[rows, cols]
        vp = v_ref[rows, cols]
        kgp = kg_ref[0, :, cols]
        vgp = vg_ref[0, :, cols]
        kg2 = jnp.concatenate([kgp * lo16, kgp * hi16], axis=0)
        vg2 = jnp.concatenate([vgp * lo16, vgp * hi16], axis=0)
        dp_ref[...] = mm_nt(jnp.concatenate([dcp * lo16, dcp * hi16], axis=0), vp)
        dpf_ref[...] = mm_nt(dcp, vg2)
        biases = by_row([bias_ref[c, head + e] for e in range(2) for c in range(4)])
        a, b = rich_sums(qp, kp, rq_ref[:, cols], rk_ref[:, cols], None, biases)
        a_ref[...] = a
        b_ref[...] = b
        squares = [[theta_ref[i, head + e] * theta_ref[i, head + e] for i in range(2)] for e in range(2)]
        halves = [jnp.where(lane1 < 64, squares[0][i], squares[1][i]) for i in range(2)]
        lines = [rq_ref[0:1, cols], rq_ref[1:2, cols], rq_ref[2:3, cols] * halves[0], rq_ref[3:4, cols] * halves[1]]
        col_sums = [[jnp.zeros((8, SPAN), F32) for _ in range(4)] for _ in range(2)]
        thetas = [[jnp.zeros((8, 128), F32) for _ in range(2)] for _ in range(2)]
        query_sums = [jnp.zeros((8, 128), F32) for _ in range(4)]
        for r in range(0, TILE, CH):
            rs = slice(r, r + CH)
            prod = dc_ref[rs, cols].astype(F32) * ctx_ref[rs, cols].astype(F32)
            row_sums = []
            dots = []
            for e in range(2):
                here = low if e == 0 else ~low
                base = 4 * e
                dot = jnp.sum(jnp.where(here, prod, 0.0), axis=1, keepdims=True)
                dots.append(dot)
                es = slice(e * TILE + r, e * TILE + r + CH)
                ds = pn_ref[0, 2 * p + e, rs, :].astype(F32) * (dp_ref[es, :] - dot)
                ds_ref[es, :] = ds.astype(BF16)
                t0 = ds * g0_ref[0, 2 * p + e, rs, :].astype(F32)
                t1 = ds * g1_ref[0, 2 * p + e, rs, :].astype(F32)
                gx = (dx_ref[rs, :] - a_ref[rs, base + 2 : base + 3]) - b_ref[base + 2 : base + 3, :]
                gy = (dy_ref[rs, :] - a_ref[rs, base + 3 : base + 4]) - b_ref[base + 3 : base + 4, :]
                tx = ds * gx
                ty = ds * gy
                for i, full in enumerate((tx * gx, ty * gy)):
                    part = full[:, 0:128] + full[:, 128:256] + full[:, 256:384]
                    thetas[e][i] = thetas[e][i] + (part[0:8] + part[8:16])
                sums = []
                for c, full in enumerate((t0, t1, tx, ty)):
                    col_sums[e][c] = col_sums[e][c] + (full[0:8] + full[8:16])
                    sums.append(jnp.sum(full[:, 0:128] + full[:, 128:256] + full[:, 256:384], axis=1, keepdims=True))
                row_sums.append(sums)
            dsf = pf_ref[0, p, rs, :].astype(F32) * (dpf_ref[rs, :] - jnp.where(low, dots[0], dots[1]))
            dsf_ref[rs, :] = dsf.astype(BF16)
            qf = q_ref[rs, cols].astype(F32)
            dqr = jnp.zeros((CH, 128), F32)
            for c in range(4):
                da = jnp.where(low, row_sums[0][c], row_sums[1][c])
                dqr = dqr + da * lines[c]
                part = da * qf
                query_sums[c] = query_sums[c] + (part[0:8] + part[8:16])
            dqr_ref[rs, :] = dqr
        folded = jnp.concatenate([jnp.sum(query_sums[c], axis=0, keepdims=True) for c in range(4)], axis=0)
        scale4 = jnp.concatenate([jnp.ones((2, 128), F32), halves[0], halves[1]], axis=0)
        vec_ref[p, 0:4, :] += folded * scale4
        line = jnp.zeros((1, 128), F32)
        for e in range(2):
            for i in range(2):
                total = jnp.sum(jnp.sum(thetas[e][i], axis=0, keepdims=True), axis=1, keepdims=True)
                line = jnp.where(lane1 == 8 + 2 * e + i, total * (-theta_ref[i, head + e]), line)
        vec_ref[p, 8:9, :] += line
        packed = jnp.concatenate([jnp.sum(col_sums[e][c], axis=0, keepdims=True) for e in range(2) for c in range(4)], axis=0)
        dq = mm(ds_ref[0:TILE, :], kp * lo16) + mm(ds_ref[TILE : 2 * TILE, :], kp * hi16) + mm(dsf_ref[...], kg2)
        dq_ref[:, cols] = (dq * 0.125 + dqr_ref[...]).astype(BF16)
        qT = jnp.transpose(qp)
        dcT = jnp.transpose(dcp)
        dk = mm(jnp.concatenate([qT * lo16c, qT * hi16c], axis=1), ds_ref[...]) * 0.125
        dv = mm(dcT * lo16c, pn_ref[0, 2 * p]) + mm(dcT * hi16c, pn_ref[0, 2 * p + 1])
        if edge:
            dk_ref[0, cols, :] = dk + rich_key_parts(p, cols, packed, kp, rows)
            dv_ref[0, cols, :] = dv
        else:
            dk_ref[cols, out_rows] += dk
            dv_ref[cols, out_rows] += dv
            db_ref[p, :, out_rows] += packed
        dkg2 = mm(jnp.transpose(dsf_ref[...]), qp) * 0.125
        dvg2 = mm(jnp.transpose(pf_ref[0, p]), dcp)
        dkg_ref[0, :, cols] += jnp.where(low64, dkg2[0:64], dkg2[64:128])
        dvg_ref[0, :, cols] += jnp.where(low64, dvg2[0:64], dvg2[64:128])
        return carry

    lax.fori_loop(0, pairs, one_pair, 0)

    if not edge:

        @pl.when(step == pl.num_programs(0) - 1)
        def _():
            own = k_ref.shape[0] - 2 * RADIUS

            def finish(p, carry):
                cols = pl.ds(pl.multiple_of(p * 128, 128), 128)
                keys = k_ref[RADIUS : RADIUS + own, cols]
                dk_ref[cols, :] += rich_key_parts(p, cols, db_ref[p], keys, None)
                return carry

            lax.fori_loop(0, pairs, finish, 0)


def attn_backward(q, dctx, ctx, k_pad, v_pad, kg, vg, coords, offset, rich, kept, first_pair, pairs, edge):
    rich_query, rich_key, rich_bias, rich_theta = rich
    rows, width = q.shape
    tiles = rows // TILE
    blocks = kg.shape[0]
    per_block = tiles // blocks
    part = pairs * 128
    half = first_pair // pairs
    steps = 2 if edge else tiles - 2
    padded_rows = k_pad.shape[0]
    scalars = pl.BlockSpec(memory_space=pltpu.SMEM)

    def tile(i):
        return i * (tiles - 1) if edge else i + 1

    tile_rows = pl.BlockSpec((TILE, part), lambda i: (tile(i), half))
    padded_cols = pl.BlockSpec((padded_rows, part), lambda i: (0, half))
    block3 = pl.BlockSpec((1, GLOB_FORM, part), lambda i: (tile(i) // per_block, 0, half))
    out3 = pl.BlockSpec((1, GLOB_FORM, part), lambda i: (tile(i) // per_block, 0, 0))
    vectors = pl.BlockSpec((4, part), lambda i: (0, half))
    near = pl.BlockSpec((1, 2 * pairs, TILE, SPAN), lambda i: (tile(i), half, 0, 0))
    far = pl.BlockSpec((1, pairs, TILE, 128), lambda i: (tile(i), half, 0, 0))
    if edge:
        key_out = pl.BlockSpec((1, part, SPAN), lambda i: (i, 0, 0))
        key_shape = jax.ShapeDtypeStruct((2, part, SPAN), F32)
    else:
        key_out = pl.BlockSpec((part, rows), lambda i: (0, 0))
        key_shape = jax.ShapeDtypeStruct((part, rows), F32)
    glob_shape = jax.ShapeDtypeStruct((blocks, GLOB_FORM, part), F32)
    return pl.pallas_call(
        partial(bwd_kernel, pairs=pairs, first_pair=first_pair, tiles=tiles, per_block=per_block, edge=edge),
        grid=(steps,),
        in_specs=[
            scalars, scalars, scalars,
            tile_rows, tile_rows, tile_rows, padded_cols, padded_cols, block3, block3,
            pl.BlockSpec(coords.shape, lambda i: (0, 0)), vectors, vectors,
            near, far, near, near,
        ],
        out_specs=[
            pl.BlockSpec((TILE, part), lambda i: (i, 0)),
            key_out, key_out, out3, out3,
            pl.BlockSpec((pairs, 16, 128), lambda i: (0, 0, 0)),
        ],
        out_shape=[
            jax.ShapeDtypeStruct((steps * TILE, part), BF16),
            key_shape, key_shape, glob_shape, glob_shape,
            jax.ShapeDtypeStruct((pairs, 16, 128), F32),
        ],
        scratch_shapes=[
            pltpu.VMEM((TILE, SPAN), F32), pltpu.VMEM((TILE, SPAN), F32),
            pltpu.VMEM((2 * TILE, SPAN), F32), pltpu.VMEM((TILE, 128), F32),
            pltpu.VMEM((2 * TILE, SPAN), BF16), pltpu.VMEM((TILE, 128), BF16),
            pltpu.VMEM((TILE, 8), F32), pltpu.VMEM((8, SPAN), F32),
            pltpu.VMEM((TILE, 128), F32), pltpu.VMEM((pairs, 8, rows), F32),
        ],
        compiler_params=pltpu.CompilerParams(vmem_limit_bytes=VMEM_LIMIT),
        cost_estimate=cost(8.2 * steps * pairs / 6),
        name="attn_backward_edge" if edge else "attn_backward_mid",
    )(offset, rich_bias, rich_theta, q, dctx, ctx, k_pad, v_pad, kg, vg, coords, rich_query, rich_key, *kept)


FF_CHUNK = 384
ROW_CHUNK = 256

def normal_tail(values):
    z = jnp.abs(values) * math.sqrt(0.5)
    t = 1.0 / (1.0 + 0.5 * z)
    poly = jnp.full_like(t, 0.17087277)
    for coef in (-0.82215223, 1.48851587, -1.13520398, 0.27886807, -0.18628806, 0.09678418, 0.37409196, 1.00002368, -1.26551223):
        poly = poly * t + coef
    return 0.5 * t * jnp.exp(poly - z * z)

def gelu_pair(values):
    tail = normal_tail(values)
    phi = jnp.where(values >= 0.0, 1.0 - tail, tail)
    density = jnp.exp(-0.5 * values * values) * (1.0 / math.sqrt(2.0 * math.pi))
    return values * phi, phi + values * density

def ffn_kernel(tok_ref, ctx_ref, ct_ref, wo_ref, wu_ref, wd_ref, norms_ref,
               out_ref, dmid_ref, dctx_ref, wog_ref, wug_ref, wdg_ref, vec_ref,
               mid_ref, h2_ref, h2t_ref, acc_ref, dh_ref, act_ref, dpre_ref, *, rows):
    step = pl.program_id(0)
    last = pl.num_programs(0) - 1

    @pl.when(step == 0)
    def _():
        for r in range(0, rows, ROW_CHUNK):
            rs = slice(r, r + ROW_CHUNK)
            mid = tok_ref[rs, :].astype(F32) + mm(ctx_ref[rs, :], wo_ref[...])
            mid_ref[rs, :] = mid
            normed, _ = norm_parts(mid)
            h2 = (normed * norms_ref[2:3, :] + norms_ref[3:4, :]).astype(BF16)
            h2_ref[rs, :] = h2
            h2t_ref[:, rs] = jnp.transpose(h2)
            acc_ref[rs, :] = jnp.zeros_like(mid)
            dh_ref[rs, :] = jnp.zeros_like(mid)

    for r in range(0, rows, ROW_CHUNK):
        rs = slice(r, r + ROW_CHUNK)
        pre = mm(h2_ref[rs, :], wu_ref[...])
        dact = mm_nt(ct_ref[rs, :], wd_ref[...])
        act, slope = gelu_pair(pre)
        act_ref[rs, :] = act.astype(BF16)
        dpre_ref[rs, :] = (dact * slope).astype(BF16)
        acc_ref[rs, :] += mm(act_ref[rs, :], wd_ref[...])
        dh_ref[rs, :] += mm_nt(dpre_ref[rs, :], wu_ref[...])
    wug_ref[...] = mm(h2t_ref[...], dpre_ref[...]).astype(BF16)
    wdg_ref[...] = mm_tn(act_ref[...], ct_ref[...]).astype(BF16)

    @pl.when(step == last)
    def _():
        gains = jnp.zeros((8, norms_ref.shape[1]), F32)
        shifts = jnp.zeros((8, norms_ref.shape[1]), F32)
        for r in range(0, rows, ROW_CHUNK):
            rs = slice(r, r + ROW_CHUNK)
            mid = mid_ref[rs, :]
            out_ref[rs, :] = (mid + acc_ref[rs, :]).astype(BF16)
            normed, scale = norm_parts(mid)
            dh = dh_ref[rs, :]
            gains = gains + jnp.sum((dh * normed).reshape(ROW_CHUNK // 8, 8, -1), axis=0)
            shifts = shifts + jnp.sum(dh.reshape(ROW_CHUNK // 8, 8, -1), axis=0)
            dmid = ct_ref[rs, :].astype(F32) + norm_pull(dh, normed, scale, norms_ref[2:3, :])
            dmid_ref[rs, :] = dmid
            dattn = dmid.astype(BF16)
            h2_ref[rs, :] = dattn
            dctx_ref[rs, :] = mm_nt(dattn, wo_ref[...]).astype(BF16)
        wog_ref[...] = mm_tn(ctx_ref[...], h2_ref[...]).astype(BF16)
        vec_ref[0:1, :] = jnp.sum(gains, axis=0, keepdims=True)
        vec_ref[1:2, :] = jnp.sum(shifts, axis=0, keepdims=True)

def feed_forward(tokens, context, cotangent, w_out, w_up, w_down, norms):
    rows, width = tokens.shape
    hidden = w_up.shape[1]
    steps = hidden // FF_CHUNK
    whole = lambda *shape: pl.BlockSpec(shape, lambda s: (0,) * len(shape))
    return pl.pallas_call(
        partial(ffn_kernel, rows=rows),
        grid=(steps,),
        in_specs=[
            whole(rows, width), whole(rows, width), whole(rows, width), whole(width, width),
            pl.BlockSpec((width, FF_CHUNK), lambda s: (0, s)),
            pl.BlockSpec((FF_CHUNK, width), lambda s: (s, 0)),
            whole(*norms.shape),
        ],
        out_specs=[
            whole(rows, width), whole(rows, width), whole(rows, width), whole(width, width),
            pl.BlockSpec((width, FF_CHUNK), lambda s: (0, s)),
            pl.BlockSpec((FF_CHUNK, width), lambda s: (s, 0)),
            whole(8, width),
        ],
        out_shape=[
            jax.ShapeDtypeStruct((rows, width), BF16),
            jax.ShapeDtypeStruct((rows, width), F32),
            jax.ShapeDtypeStruct((rows, width), BF16),
            jax.ShapeDtypeStruct((width, width), BF16),
            jax.ShapeDtypeStruct((width, hidden), BF16),
            jax.ShapeDtypeStruct((hidden, width), BF16),
            jax.ShapeDtypeStruct((8, width), F32),
        ],
        scratch_shapes=[
            pltpu.VMEM((rows, width), F32), pltpu.VMEM((rows, width), BF16), pltpu.VMEM((width, rows), BF16),
            pltpu.VMEM((rows, width), F32), pltpu.VMEM((rows, width), F32),
            pltpu.VMEM((rows, FF_CHUNK), BF16), pltpu.VMEM((rows, FF_CHUNK), BF16),
        ],
        compiler_params=pltpu.CompilerParams(vmem_limit_bytes=VMEM_LIMIT),
        cost_estimate=cost(60.0),
        name="feed_forward",
    )(tokens, context, cotangent, w_out, w_up, w_down, norms)


def qkv_back_kernel(*refs, half, final, pairs, kept):
    (ht_ref, hg_ref, w_ref, dqe_ref, dqm_ref, dke_ref, dve_ref, dkm_ref, dvm_ref, before_ref, after_ref,
     dkge_ref, dvge_ref, dkgm_ref, dvgm_ref) = refs[:15]
    refs = refs[15:]
    if final:
        (dh0_ref, dhg0_ref, tok_ref, dmid_ref, norms_ref, oh_ref, ng_ref, second_ref, ve_ref, va_ref, vb_ref) = refs[:11]
        refs = refs[11:]
        grad_ref, vec_ref, tg_ref, gp_ref, dh_ref, dhg_ref, part_ref, dkt_ref, rows_ref = refs
    else:
        grad_ref, dh_ref, dhg_ref, part_ref, dkt_ref = refs
    step = pl.program_id(0)
    rows, part = part_ref.shape
    width = ht_ref.shape[0]
    edge = 128

    @pl.when(step == 0)
    def _():
        part_ref[0:edge, :] = dqe_ref[0:edge, :]
        part_ref[edge : rows - edge, :] = dqm_ref[...]
        part_ref[rows - edge : rows, :] = dqe_ref[edge : 2 * edge, :]

    for index, edge_ref, mid_ref in ((1, dke_ref, dkm_ref), (2, dve_ref, dvm_ref)):

        @pl.when(step == index)
        def _():
            dkt_ref[...] = mid_ref[...].astype(BF16)
            dkt_ref[:, 0:128] = (mid_ref[:, 0:128] + edge_ref[0, :, 128:256] + before_ref[index - 1].astype(F32)).astype(BF16)
            dkt_ref[:, 128:256] = (mid_ref[:, 128:256] + edge_ref[0, :, 256:384]).astype(BF16)
            dkt_ref[:, rows - 256 : rows - 128] = (mid_ref[:, rows - 256 : rows - 128] + edge_ref[1, :, 0:128]).astype(BF16)
            dkt_ref[:, rows - 128 : rows] = (
                mid_ref[:, rows - 128 : rows] + edge_ref[1, :, 128:256] + after_ref[index - 1].astype(F32)
            ).astype(BF16)
            part_ref[...] = jnp.transpose(dkt_ref[...])

    grad = mm(ht_ref[...], part_ref[...])
    moved = mm_nt(part_ref[...], w_ref[...])

    @pl.when(step == 0)
    def _():
        grad_ref[...] = grad.astype(BF16)
        if final:
            dh_ref[...] = dh0_ref[...] + moved
            dhg_ref[...] = dhg0_ref[...]
        else:
            dh_ref[...] = moved
            dhg_ref[...] = jnp.zeros_like(dhg_ref)

    for index, edge_ref, mid_ref in ((1, dkge_ref, dkgm_ref), (2, dvge_ref, dvgm_ref)):

        @pl.when(step == index)
        def _():
            glob = (edge_ref[...] + mid_ref[...]).reshape(-1, part).astype(BF16)
            hg = hg_ref[...].reshape(-1, width)
            grad_ref[...] = (grad + mm_tn(hg, glob)).astype(BF16)
            dh_ref[...] += moved
            dhg_ref[...] += mm_nt(glob, w_ref[...])

    if final:

        @pl.when(step == 2)
        def _():
            gains = jnp.zeros((8, width), F32)
            shifts = jnp.zeros((8, width), F32)
            for r in range(0, rows, 128):
                rs = slice(r, r + 128)
                normed, scale = norm_parts(tok_ref[rs, :].astype(F32))
                dh = dh_ref[rs, :]
                gains = gains + jnp.sum((dh * normed).reshape(16, 8, width), axis=0)
                shifts = shifts + jnp.sum(dh.reshape(16, 8, width), axis=0)
                tg_ref[rs, :] = (dmid_ref[rs, :] + norm_pull(dh, normed, scale, norms_ref[0:1, :])).astype(BF16)
            dhg = dhg_ref[...]
            normed = ng_ref[...].reshape(-1, width)
            rows_ref[...] = jnp.zeros_like(rows_ref)
            rows_ref[0:1, :] = jnp.sum(gains, axis=0, keepdims=True) + jnp.sum(dhg * normed, axis=0, keepdims=True)
            rows_ref[1:2, :] = jnp.sum(shifts, axis=0, keepdims=True) + jnp.sum(dhg, axis=0, keepdims=True)
            rows_ref[2:4, :] = second_ref[0:2, :]
            gp_ref[...] = mm_tn(oh_ref[...].reshape(-1, oh_ref.shape[2]), dhg.astype(BF16)).astype(BF16)
            lines = []
            for p in range(2 * pairs):
                mid = va_ref[p] if p < pairs else vb_ref[p - pairs]
                both = ve_ref[p] + mid
                rows_ref[4:12, p * 128 : p * 128 + 128] = both[0:8]
                lines.append(both[8:9])
            lines.append(jnp.zeros((8 - len(lines), 128), F32))
            lines = jnp.concatenate(split3(jnp.concatenate(lines, axis=0)), axis=0).astype(BF16)
            spot = lax.broadcasted_iota(jnp.int32, (128, width), 0)
            lane = lax.broadcasted_iota(jnp.int32, (128, width), 1)
            spread = mm(lines, (lax.rem(lane, kept) == spot).astype(F32).astype(BF16))
            rows_ref[12:20, :] = spread[0:8] + spread[8:16] + spread[16:24]
            vec_ref[...] = jnp.transpose(rows_ref[...]).astype(BF16)


def qkv_backward(hidden_t, hg, w_qkv, dq, dk, dv, rims, dkg, dvg, half, pairs, kept, last=None):
    width, rows = hidden_t.shape
    part = pairs * 128
    halves = width // part
    final = last is not None

    def whole(*shape):
        return pl.BlockSpec(shape, lambda i: (0,) * len(shape))

    blocks = hg.shape[0]
    edge_keys = pl.BlockSpec((2, part, SPAN), lambda i: (0, half, 0))
    edge_glob = pl.BlockSpec((blocks, GLOB_FORM, part), lambda i: (0, 0, half))
    rim = pl.BlockSpec((2, part, RADIUS), lambda i: (0, half, 0))
    operands = [hidden_t, hg, w_qkv, dq[0], dq[1], dk[0], dv[0], dk[1], dv[1], rims[0], rims[1],
                dkg[0], dvg[0], dkg[1], dvg[1]]
    in_specs = [
        whole(width, rows), whole(blocks, GLOB_FORM, width),
        pl.BlockSpec((width, part), lambda i: (0, halves * i + half)),
        pl.BlockSpec((2 * TILE, part), lambda i: (0, half)), whole(rows - 2 * TILE, part),
        edge_keys, edge_keys, whole(part, rows), whole(part, rows), rim, rim,
        edge_glob, edge_glob, whole(blocks, GLOB_FORM, part), whole(blocks, GLOB_FORM, part),
    ]
    out_specs = [pl.BlockSpec((width, part), lambda i: (0, i))]
    out_shape = [jax.ShapeDtypeStruct((width, 3 * part), BF16)]
    scratch = [pltpu.VMEM((rows, part), BF16), pltpu.VMEM((part, rows), BF16)]
    sums_shape = [(rows, width), (blocks * GLOB_FORM, width)]
    if final:
        operands += list(last)
        in_specs += [whole(*a.shape) for a in last]
        globs = last[5].shape[2]
        out_specs += [whole(width, 128), whole(rows, width), whole(globs, width)]
        out_shape += [
            jax.ShapeDtypeStruct((width, 128), BF16),
            jax.ShapeDtypeStruct((rows, width), BF16),
            jax.ShapeDtypeStruct((globs, width), BF16),
        ]
        scratch = [pltpu.VMEM(s, F32) for s in sums_shape] + scratch + [pltpu.VMEM((128, width), F32)]
    else:
        out_specs += [whole(*s) for s in sums_shape]
        out_shape += [jax.ShapeDtypeStruct(s, F32) for s in sums_shape]
    return pl.pallas_call(
        partial(qkv_back_kernel, half=half, final=final, pairs=pairs, kept=kept),
        grid=(3,),
        in_specs=in_specs,
        out_specs=out_specs,
        out_shape=out_shape,
        scratch_shapes=scratch,
        compiler_params=pltpu.CompilerParams(vmem_limit_bytes=VMEM_LIMIT),
        cost_estimate=cost(15.0 if final else 8.0),
        name="qkv_backward",
    )(*operands)


def swap_on(axis, mask):
    return [(i, i ^ mask) for i in range(lax.axis_size(axis))]


def add_low(kept, received):
    return (kept.astype(F32) + received.astype(F32)).astype(BF16)


def core_halves(grads, place):
    count = lax.axis_size("seq")
    view = grads.reshape(count // 2, 2, grads.shape[0] // count, grads.shape[1])
    send = lax.dynamic_index_in_dim(view, 1 - place % 2, 1, keepdims=False)
    kept = lax.dynamic_index_in_dim(view, place % 2, 1, keepdims=False)
    return kept, send


def core_swap(send):
    return lax.ppermute(send, "seq", swap_on("seq", 1))


def stream_blocks(summed, group_count):
    outer, rows, columns = summed.shape
    return jnp.moveaxis(summed.reshape(outer, group_count, rows // group_count, columns), 1, 0)


def halve_step(blocks, axis, place, bit, width):
    mine = (place >> bit) & 1
    send = lax.dynamic_index_in_dim(blocks, 1 - mine, width, keepdims=False)
    kept = lax.dynamic_index_in_dim(blocks, mine, width, keepdims=False)
    return add_low(kept, lax.ppermute(send, axis, swap_on(axis, 1 << bit)))


def exchange_sum(blocks, axis, place, stride):
    count = blocks.shape[0]
    total = lax.dynamic_index_in_dim(blocks, place, 0, keepdims=False).astype(F32)
    for step in range(1, count):
        send = lax.dynamic_index_in_dim(blocks, place ^ step, 0, keepdims=False)
        total = total + lax.ppermute(send, axis, swap_on(axis, step * stride)).astype(F32)
    return total.astype(BF16)


def exchange_all(piece, axis, place):
    count = lax.axis_size(axis)
    every = [piece] + [lax.ppermute(piece, axis, swap_on(axis, step)) for step in range(1, count)]
    return ordered(jnp.stack(every), place)


def gather_rows(rows, axis, place, bit):
    other = lax.ppermute(rows, axis, swap_on(axis, bit))
    upper = (place & bit) > 0
    return jnp.concatenate([jnp.where(upper, other, rows), jnp.where(upper, rows, other)], axis=0)


def gather_blocks(rows, axis, place, stride):
    count = lax.axis_size(axis) // stride
    every = [rows] + [lax.ppermute(rows, axis, swap_on(axis, step * stride)) for step in range(1, count)]
    return ordered(jnp.stack(every), place).reshape(count * rows.shape[0], rows.shape[1])


def ordered(stacked, place):
    count = stacked.shape[0]
    rest = stacked.shape[1:]
    bit = 1
    while bit < count:
        view = stacked.reshape((count // (2 * bit), 2, bit) + rest)
        stacked = jnp.where((place & bit) > 0, view[:, ::-1], view).reshape((count,) + rest)
        bit *= 2
    return stacked


def tied(*values):
    return lax.optimization_barrier(values)


def body(
    tokens,
    global_states,
    cotangent,
    w_qkv,
    w_out,
    w_up,
    w_down,
    first_gain,
    first_shift,
    second_gain,
    second_shift,
    rich_query,
    rich_key,
    rich_bias,
    rich_theta,
    bucket_units,
    form_lengths,
    coords,
    glob_owner,
):
    row_count = tokens.shape[1]
    model_width = tokens.shape[2]
    place = lax.axis_index("seq")
    group = lax.axis_index("stream")
    seq_count = lax.axis_size("seq")
    group_count = lax.axis_size("stream")
    rich = (rich_query, rich_key, rich_bias, rich_theta)
    offset = (place * row_count).astype(jnp.int32).reshape(1, 1)
    norms = jnp.stack([first_gain, first_shift, second_gain, second_shift])
    up = [(i, i + 1) for i in range(seq_count - 1)]
    down = [(i + 1, i) for i in range(seq_count - 1)]
    pairs = rich_bias.shape[1] // 2
    half_pairs = pairs // 2
    kept_rows = model_width // seq_count

    before = lax.ppermute(tokens[0, row_count - RADIUS :], "seq", up)
    after = lax.ppermute(tokens[0, :RADIUS], "seq", down)
    pair_glob = gather_rows(global_states[0], "seq", place, 1)
    pair_glob, norms, before, after = tied(pair_glob, norms, before, after)
    every_glob = gather_blocks(pair_glob, "seq", place // 2, 2)
    queries, keys, values, hidden_t = project_tokens(tokens[0], w_qkv, norms)
    (context, pn, pf, g0, g1, key_pad, value_pad, glob_keys, glob_values, glob_hidden, glob_normed, picked) = attn_forward(
        queries, keys, values, before, after, every_glob, glob_owner, w_qkv, norms,
        coords[0], bucket_units, form_lengths, offset, rich,
    )
    layer_out, grad_middle, grad_context, grad_w_out, grad_w_up, grad_w_down, second_sums = feed_forward(
        tokens[0], context, cotangent[0], w_out, w_up, w_down, norms
    )

    def attention_back(first_pair, count, edge, grad_context):
        return attn_backward(
            queries, grad_context, context, key_pad, value_pad, glob_keys, glob_values, coords[0], offset, rich,
            (pn, pf, g0, g1), first_pair, count, edge,
        )

    halves = [core_halves(grad, place) for grad in (grad_w_up, grad_w_down, grad_w_out)]
    sends = [half[1] for half in halves]
    grad_context, *sends = tied(grad_context, *sends)
    halves = [(half[0], core_swap(send)) for half, send in zip(halves, sends)]
    dq_e, dk_e, dv_e, dkg_e, dvg_e, vec_e = attention_back(0, pairs, True, grad_context)
    to_before = jnp.stack([dk_e[0, :, :RADIUS], dv_e[0, :, :RADIUS]]).astype(BF16)
    to_after = jnp.stack([dk_e[1, :, 2 * RADIUS :], dv_e[1, :, 2 * RADIUS :]]).astype(BF16)
    rims = (lax.ppermute(to_after, "seq", up), lax.ppermute(to_before, "seq", down))

    (dq_e, *swapped) = tied(dq_e, *[half[1] for half in halves])
    halves = [(half[0], received) for half, received in zip(halves, swapped)]

    sums = [add_low(*half) for half in halves]
    outer = seq_count // 2
    bits = group_count.bit_length() - 1
    pieces = [
        jnp.moveaxis(sums[0].reshape(outer, kept_rows, group_count, -1), 2, 0).reshape(group_count, outer, -1, model_width),
        jnp.moveaxis(sums[1].reshape(outer, group_count, -1, model_width), 1, 0),
        jnp.moveaxis(sums[2].reshape(outer, group_count, -1, model_width), 1, 0),
    ]
    piece_rows = [piece.shape[2] for piece in pieces]
    early = jnp.concatenate(pieces, axis=2).reshape((2,) * bits + (outer, sum(piece_rows), model_width))
    columns = model_width // 2
    early_x, early_y = early[..., :columns], early[..., columns:]
    order_x = list(range(bits))
    order_y = order_x[1:] + order_x[:1]

    def halved(blocks, order, done):
        bit = order[done]
        rest = sorted(order[done:], reverse=True)
        return halve_step(blocks, "stream", group, bit, rest.index(bit))

    early_x, early_y, grad_context, *rims = tied(early_x, early_y, grad_context, *rims)
    early_x = halved(early_x, order_x, 0)
    early_y = halved(early_y, order_y, 0)
    dq_a, dk_a, dv_a, dkg_a, dvg_a, vec_a = attention_back(0, half_pairs, False, grad_context)
    early_x, early_y, dq_a = tied(early_x, early_y, dq_a)
    for done in range(1, bits):
        early_x = halved(early_x, order_x, done)
        early_y = halved(early_y, order_y, done)
    grads_a, grad_hidden, grad_glob_hidden = qkv_backward(
        hidden_t, glob_hidden, w_qkv, (dq_e, dq_a), (dk_e, dk_a), (dv_e, dv_a), rims,
        (dkg_e, dkg_a), (dvg_e, dvg_a), 0, half_pairs, kept_rows,
    )
    kept_a, send_a = core_halves(grads_a, place)
    early = jnp.concatenate([early_x, early_y], axis=-1)
    late_a = stream_blocks(add_low(kept_a, core_swap(send_a)), group_count)
    early, late_a, grad_context = tied(early, late_a, grad_context)
    dq_b, dk_b, dv_b, dkg_b, dvg_b, vec_b = attention_back(half_pairs, half_pairs, False, grad_context)
    early = exchange_sum(early, "seq", place // 2, 2)
    early, dq_b = tied(early, dq_b)
    early = exchange_all(early, "stream", group)
    late_a, dq_b = tied(late_a, dq_b)
    late_a = exchange_sum(late_a, "stream", group, 1)
    late_a = exchange_sum(late_a, "seq", place // 2, 2)
    grads_b, vectors, tokens_grad, glob_part = qkv_backward(
        hidden_t, glob_hidden, w_qkv, (dq_e, dq_b), (dk_e, dk_b), (dv_e, dv_b), rims,
        (dkg_e, dkg_b), (dvg_e, dvg_b), 1, half_pairs, kept_rows,
        (grad_hidden, grad_glob_hidden, tokens[0], grad_middle, norms, picked, glob_normed, second_sums, vec_e, vec_a, vec_b),
    )

    early, late_a, grads_b = tied(early, late_a, grads_b)
    share_a = exchange_all(late_a, "stream", group).reshape(kept_rows, -1).astype(F32)
    kept_b, send_b = core_halves(jnp.concatenate([grads_b, vectors], axis=1), place)
    late_b = stream_blocks(add_low(kept_b, core_swap(send_b)), group_count)
    late_b = exchange_sum(late_b, "stream", group, 1)
    late_b = exchange_sum(late_b, "seq", place // 2, 2)
    share_b = exchange_all(late_b, "stream", group).reshape(kept_rows, -1).astype(F32)
    kept_glob, send_glob = core_halves(glob_part, place)
    glob_blocks = add_low(kept_glob, core_swap(send_glob))
    grad_glob = exchange_sum(glob_blocks, "seq", place // 2, 2).astype(F32)
    own_glob, own_scale = norm_parts(global_states[0].astype(F32))
    glob_grad = norm_pull(grad_glob, own_glob, own_scale, first_gain).astype(BF16)

    part = half_pairs * 128
    share_qkv = jnp.concatenate(
        [share[:, i * part : (i + 1) * part] for i in range(3) for share in (share_a, share_b)], axis=1
    )
    cuts = [0, piece_rows[0], piece_rows[0] + piece_rows[1], sum(piece_rows)]
    early = early.astype(F32)
    share_up = jnp.moveaxis(early[:, : cuts[1]].reshape(group_count, kept_rows, -1), 0, 1).reshape(kept_rows, -1)
    share_down = early[:, cuts[1] : cuts[2]].reshape(-1, model_width)
    share_out = early[:, cuts[2] :].reshape(-1, model_width)
    small = share_b[:, 3 * part :]
    own_vectors = small[:, :12].T
    heads = small[:12, 12 : 12 + pairs].T.reshape(pairs, 12)
    bias_grad = heads[:, :8].reshape(pairs, 2, 4).transpose(2, 0, 1).reshape(rich_bias.shape)
    theta_grad = heads[:, 8:].reshape(pairs, 2, 2).transpose(2, 0, 1).reshape(rich_theta.shape)
    return (
        layer_out[None],
        tokens_grad[None],
        glob_grad[None],
        share_qkv,
        share_out,
        share_up,
        share_down,
        own_vectors[0],
        own_vectors[1],
        own_vectors[2],
        own_vectors[3],
        own_vectors[4:8],
        own_vectors[8:12],
        bias_grad,
        theta_grad,
    )


def solution(mesh):
    return jax.shard_map(
        body,
        mesh=mesh,
        in_specs=(
            P("stream", "seq", None),
            P("stream", "seq", None),
            P("stream", "seq", None),
            P(),
            P(),
            P(),
            P(),
            P(),
            P(),
            P(),
            P(),
            P(),
            P(),
            P(),
            P(),
            P("stream", None),
            P("stream", None),
            P("stream", None, None),
            P("stream", None),
        ),
        out_specs=(
            P("stream", "seq", None),
            P("stream", "seq", None),
            P("stream", "seq", None),
            P("seq", None),
            P("seq", None),
            P("seq", None),
            P("seq", None),
            P("seq"),
            P("seq"),
            P("seq"),
            P("seq"),
            P(None, "seq"),
            P(None, "seq"),
            P(),
            P(),
        ),
        check_vma=False,
    )
```

```python
from functools import partial
import math

import jax
import jax.numpy as jnp
from jax import lax
from jax.experimental import pallas as pl
from jax.experimental.pallas import tpu as pltpu
from jax.sharding import PartitionSpec as P

RADIUS = 128
GLOB_FORM = 64
QBLOCK = 512
TOK_DEV = 1024


EPSILON = 1e-06


TILE = 128
SPAN = 384
LOG2E = math.log2(math.e)
FAR_AWAY = 1e15
CH = 128
UNROLL = 6
BACK_CH = 128
BACK_UNROLL = 3
F32 = jnp.float32
BF16 = jnp.bfloat16
VMEM_LIMIT = 58 * 1024 * 1024


def mm(a, b):
    return lax.dot_general(a, b, (((1,), (0,)), ((), ())), preferred_element_type=F32)


def mm_nt(a, b):
    return lax.dot_general(a, b, (((1,), (1,)), ((), ())), preferred_element_type=F32)


def mm_tn(a, b):
    return lax.dot_general(a, b, (((0,), (0,)), ((), ())), preferred_element_type=F32)


def norm_parts(values):
    centre = jnp.mean(values, axis=-1, keepdims=True)
    centred = values - centre
    spread = jnp.mean(centred * centred, axis=-1, keepdims=True)
    scale = lax.rsqrt(spread + EPSILON)
    return centred * scale, scale


def norm_pull(grad, normed, scale, gain):
    e = grad * gain
    mean_e = jnp.mean(e, axis=-1, keepdims=True)
    mean_en = jnp.mean(e * normed, axis=-1, keepdims=True)
    return scale * (e - mean_e - normed * mean_en)


def split3(values):
    hi = values.astype(BF16).astype(F32)
    rest = values - hi
    mid = rest.astype(BF16).astype(F32)
    return hi, mid, rest - mid


def half_masks(dtype):
    lane = lax.broadcasted_iota(jnp.int32, (1, 128), 1)
    low = (lane < 64).astype(F32)
    return low.astype(dtype), (1.0 - low).astype(dtype)


def by_row(values):
    row = lax.broadcasted_iota(jnp.int32, (8, 128), 0)
    out = jnp.full((8, 128), values[7], F32)
    for index in range(7):
        out = jnp.where(row == index, values[index], out)
    return out


def rich_rows(vectors, scales):
    row = lax.broadcasted_iota(jnp.int32, (8, 128), 0)
    lane = lax.broadcasted_iota(jnp.int32, (8, 128), 1)
    both = jnp.concatenate([vectors, vectors], axis=0)
    both = both if scales is None else both * scales
    return jnp.where((row < 4) == (lane < 64), both, 0.0)


def rich_sums(qp, kp, query_vec, key_vec, scales, bias8):
    rq = jnp.concatenate(split3(rich_rows(query_vec, scales)), axis=1).astype(BF16)
    rk = jnp.concatenate(split3(rich_rows(key_vec, scales)), axis=0).astype(BF16)
    a = mm_nt(jnp.concatenate([qp, qp, qp], axis=1), rq)
    b24 = mm_nt(rk, kp)
    return a, b24[0:8] + b24[8:16] + b24[16:24] + bias8[:, 0:1]


def form_of(units_ref, lengths_ref, row):
    form, low, high, before = 0, 0, lengths_ref[0, 0], 0
    for index in range(1, units_ref.shape[1]):
        before = before + units_ref[0, index - 1]
        start = TOK_DEV // 2 + TOK_DEV * before
        taken = row >= start
        form = jnp.where(taken, index, form)
        low = jnp.where(taken, start, low)
        high = jnp.where(taken, start + lengths_ref[0, index], high)
    return form, low, high


def coord_row(coords_ref, axis, tile_index):
    tile_index = jnp.clip(tile_index, 0, coords_ref.shape[1] // 128 - 1)
    return coords_ref[axis : axis + 1, pl.ds(pl.multiple_of(tile_index * 128, 128), 128)].astype(F32)


def query_columns(coords_ref, axis, tile_index):
    return jnp.transpose(jnp.broadcast_to(coord_row(coords_ref, axis, tile_index), (128, 128)))


def geometry_into(coords_ref, first_tile, span, refs):
    ox_ref, oy_ref, dx_ref, dy_ref = refs
    xq = query_columns(coords_ref, 0, first_tile + 1)
    yq = query_columns(coords_ref, 1, first_tile + 1)
    for lt in range(3):
        xk = coord_row(coords_ref, 0, first_tile + lt)
        yk = coord_row(coords_ref, 1, first_tile + lt)
        out = (slice(None), slice(lt * 128, lt * 128 + 128))
        dx = jnp.log(1.0 + jnp.abs(xq - xk))
        dy = jnp.log(1.0 + jnp.abs(yq - yk))
        if span is not None:
            row = lax.broadcasted_iota(jnp.int32, (128, 128), 0)
            col = lax.broadcasted_iota(jnp.int32, (128, 128), 1) + lt * 128
            near = (col >= row) & (col - row <= 2 * RADIUS)
            dx = jnp.where(near & (col >= span[0]) & (col < span[1]), dx, FAR_AWAY)
            ox_ref[out] = jnp.where(xk > xq, 1.0, -1.0)
            oy_ref[out] = jnp.where(yk > yq, 1.0, -1.0)
        dx_ref[out] = dx
        dy_ref[out] = dy


def qkv_kernel(tok_ref, w_ref, norms_ref, q_ref, k_ref, v_ref, ht_ref):
    width = tok_ref.shape[1]
    normed, _ = norm_parts(tok_ref[...].astype(F32))
    hidden = (normed * norms_ref[0:1, :] + norms_ref[1:2, :]).astype(BF16)
    for index, out in enumerate((q_ref, k_ref, v_ref)):
        out[...] = mm(hidden, w_ref[:, index * width : (index + 1) * width]).astype(BF16)
    ht_ref[...] = jnp.transpose(hidden)


def project_tokens(tokens, w_qkv, norms):
    rows, width = tokens.shape
    step = 256
    block = pl.BlockSpec((step, width), lambda i: (i, 0))
    return pl.pallas_call(
        qkv_kernel,
        grid=(rows // step,),
        in_specs=[block, pl.BlockSpec(w_qkv.shape, lambda i: (0, 0)), pl.BlockSpec(norms.shape, lambda i: (0, 0))],
        out_specs=[block, block, block, pl.BlockSpec((width, step), lambda i: (0, i))],
        out_shape=[jax.ShapeDtypeStruct((rows, width), BF16)] * 3 + [jax.ShapeDtypeStruct((width, rows), BF16)],
        compiler_params=pltpu.CompilerParams(vmem_limit_bytes=VMEM_LIMIT),
        cost_estimate=cost(8.0),
        name="project_tokens",
    )(tokens, w_qkv, norms)


def cost(micros):
    return pl.CostEstimate(flops=int(micros * 1e9), bytes_accessed=0, transcendentals=0)


def global_pairs(form, owner_ref, glob_ref, norms_ref, kw_ref, vw_ref, kg_ref, vg_ref, hg_ref, ng_ref, oh_ref):
    count = glob_ref.shape[0]
    match = (owner_ref[...] == form).astype(F32)
    row = lax.broadcasted_iota(jnp.int32, (count, count), 0)
    col = lax.broadcasted_iota(jnp.int32, (count, count), 1)
    upto = (row <= col).astype(F32).astype(BF16)
    rank = mm(jnp.broadcast_to(match, (16, count)).astype(BF16), upto)[0:1]
    slot = lax.broadcasted_iota(jnp.int32, (GLOB_FORM, count), 0).astype(F32) + 1.0
    picked = jnp.where(rank == slot, match, 0.0).astype(BF16)
    oh_ref[0] = picked
    normed, _ = norm_parts(mm(picked, glob_ref[...]))
    ng_ref[0] = normed
    hidden = (normed * norms_ref[0:1, :] + norms_ref[1:2, :]).astype(BF16)
    hg_ref[0] = hidden
    kg_ref[0] = mm(hidden, kw_ref[...]).astype(BF16)
    vg_ref[0] = mm(hidden, vw_ref[...]).astype(BF16)


def fwd_kernel(units_ref, lengths_ref, offset_ref, bias_ref, theta_ref,
               q_ref, k_ref, v_ref, before_ref, after_ref, glob_ref, owner_ref, kw_ref, vw_ref, norms_ref,
               coords_ref, rq_ref, rk_ref,
               ctx_ref, pn_ref, pf_ref, g0_ref, g1_ref, kp_ref, vp_ref, kg_ref, vg_ref, hg_ref, ng_ref, oh_ref,
               ox_ref, oy_ref, dx_ref, dy_ref, s_ref, sf_ref, a_ref, b_ref, *, pairs, per_block):
    t = pl.program_id(0)
    rows_all = k_ref.shape[0]
    offset = offset_ref[0, 0]
    first = offset + t * TILE
    form, low_end, high_end = form_of(units_ref, lengths_ref, first)

    @pl.when(t == 0)
    def _():
        for refs in ((k_ref, kp_ref, kw_ref), (v_ref, vp_ref, vw_ref)):
            own, padded_ref, weight = refs
            padded_ref[RADIUS : RADIUS + rows_all, :] = own[...]
        for halo, start in ((before_ref, 0), (after_ref, RADIUS + rows_all)):
            normed, _ = norm_parts(halo[...].astype(F32))
            hidden = (normed * norms_ref[0:1, :] + norms_ref[1:2, :]).astype(BF16)
            kp_ref[start : start + RADIUS, :] = mm(hidden, kw_ref[...]).astype(BF16)
            vp_ref[start : start + RADIUS, :] = mm(hidden, vw_ref[...]).astype(BF16)

    @pl.when(t % per_block == 0)
    def _():
        global_pairs(form, owner_ref, glob_ref, norms_ref, kw_ref, vw_ref, kg_ref, vg_ref, hg_ref, ng_ref, oh_ref)

    shifted = first - RADIUS
    geometry_into(coords_ref, offset // 128 + t - 1, (low_end - shifted, high_end - shifted), (ox_ref, oy_ref, dx_ref, dy_ref))
    lo16, hi16 = half_masks(BF16)
    lane = lax.broadcasted_iota(jnp.int32, (CH, 128), 1)
    low = lane < 64
    rows = pl.ds(pl.multiple_of(t * TILE, TILE), SPAN)
    root = math.sqrt(0.5 * LOG2E)

    def widths_of(p):
        return [[theta_ref[i, 2 * p + e] * root for i in range(2)] for e in range(2)]

    def scores(p, slot):
        cols = pl.ds(pl.multiple_of(p * 128, 128), 128)
        qp = q_ref[:, cols]
        kp = kp_ref[rows, cols]
        kgp = kg_ref[0, :, cols]
        widths = widths_of(p)
        scales = by_row([LOG2E, LOG2E] + widths[0] + [LOG2E, LOG2E] + widths[1])
        biases = by_row([bias_ref[c, 2 * p + e] for e in range(2) for c in range(4)]) * scales
        s_ref[slot] = mm_nt(jnp.concatenate([qp * lo16, qp * hi16], axis=0), kp)
        sf_ref[slot] = mm_nt(qp, jnp.concatenate([kgp * lo16, kgp * hi16], axis=0))
        a, b = rich_sums(qp, kp, rq_ref[:, cols], rk_ref[:, cols], scales, biases)
        a_ref[slot] = a
        b_ref[slot] = b

    def weights(p, slot):
        widths = widths_of(p)
        for r in range(0, TILE, CH):
            rs = slice(r, r + CH)
            far = sf_ref[slot, rs, :] * (0.125 * LOG2E)
            tops = []
            held = []
            for e in range(2):
                base = 4 * e
                part = [a_ref[slot, rs, base + c : base + c + 1] for c in range(4)]
                line = [b_ref[slot, base + c : base + c + 1, :] for c in range(4)]
                u0 = (part[0] + line[0]) * ox_ref[rs, :]
                u1 = (part[1] + line[1]) * oy_ref[rs, :]
                e0 = jnp.exp2(jnp.minimum(u0, -u0))
                e1 = jnp.exp2(jnp.minimum(u1, -u1))
                r0 = 1.0 / (1.0 + e0)
                r1 = 1.0 / (1.0 + e1)
                gx = (widths[e][0] * dx_ref[rs, :] - part[2]) - line[2]
                gy = (widths[e][1] * dy_ref[rs, :] - part[3]) - line[3]
                s = s_ref[slot, e * TILE + r : e * TILE + r + CH, :] * (0.125 * LOG2E)
                s = s + jnp.minimum(u0, 0.0) + jnp.minimum(u1, 0.0) - gx * gx - gy * gy
                top = jnp.maximum(jnp.maximum(s[:, 0:128], s[:, 128:256]), s[:, 256:384])
                here = low if e == 0 else ~low
                top = jnp.maximum(top, jnp.where(here, far, -3e38))
                tops.append(jnp.max(top, axis=1, keepdims=True))
                g0 = jnp.where(u0 >= 0.0, e0, 1.0) * (ox_ref[rs, :] * r0)
                g1 = jnp.where(u1 >= 0.0, e1, 1.0) * (oy_ref[rs, :] * r1)
                g0_ref[0, 2 * p + e, rs, :] = g0.astype(BF16)
                g1_ref[0, 2 * p + e, rs, :] = g1.astype(BF16)
                held.append((s, r0 * r1))
            pfar = jnp.exp2(far - jnp.where(low, tops[0], tops[1]))
            invs = []
            for e in range(2):
                s, rr = held[e]
                pe = jnp.exp2(s - tops[e]) * rr
                here = low if e == 0 else ~low
                tot = pe[:, 0:128] + pe[:, 128:256] + pe[:, 256:384] + jnp.where(here, pfar, 0.0)
                inv = 1.0 / jnp.sum(tot, axis=1, keepdims=True)
                invs.append(inv)
                pn_ref[0, 2 * p + e, rs, :] = (pe * inv).astype(BF16)
            pf_ref[0, p, rs, :] = (pfar * jnp.where(low, invs[0], invs[1])).astype(BF16)

    def context(p):
        cols = pl.ds(pl.multiple_of(p * 128, 128), 128)
        vp = vp_ref[rows, cols]
        vgp = vg_ref[0, :, cols]
        ctx = mm(pn_ref[0, 2 * p], vp * lo16) + mm(pn_ref[0, 2 * p + 1], vp * hi16)
        ctx = ctx + mm(pf_ref[0, p], jnp.concatenate([vgp * lo16, vgp * hi16], axis=0))
        ctx_ref[:, cols] = ctx.astype(BF16)

    def group(index, carry):
        first = index * UNROLL
        for u in range(UNROLL):
            scores(first + u, u)
        for u in range(UNROLL):
            weights(first + u, u)
        for u in range(UNROLL):
            context(first + u)
        return carry

    lax.fori_loop(0, pairs // UNROLL, group, 0)


def attn_forward(q, k, v, before, after, every_glob, owner, w_qkv, norms, coords, units, lengths, offset, rich):
    rich_query, rich_key, rich_bias, rich_theta = rich
    rows, width = q.shape
    heads = rich_bias.shape[1]
    pairs = heads // 2
    tiles = rows // TILE
    blocks = rows // QBLOCK
    per_block = tiles // blocks
    padded_rows = rows + 2 * RADIUS
    globs = every_glob.shape[0]
    scalars = pl.BlockSpec(memory_space=pltpu.SMEM)

    def whole(*shape):
        return pl.BlockSpec(shape, lambda t: (0,) * len(shape))

    def block3(*shape):
        return pl.BlockSpec((1,) + shape, lambda t: (t // per_block, 0, 0))

    near = pl.BlockSpec((1, heads, TILE, SPAN), lambda t: (t, 0, 0, 0))
    near_shape = jax.ShapeDtypeStruct((tiles, heads, TILE, SPAN), BF16)
    tile_rows = pl.BlockSpec((TILE, width), lambda t: (t, 0))
    return pl.pallas_call(
        partial(fwd_kernel, pairs=pairs, per_block=per_block),
        grid=(tiles,),
        in_specs=[
            scalars, scalars, scalars, scalars, scalars,
            tile_rows, whole(rows, width), whole(rows, width),
            whole(RADIUS, width), whole(RADIUS, width),
            whole(globs, width), whole(1, globs),
            pl.BlockSpec((width, width), lambda t: (0, 1)),
            pl.BlockSpec((width, width), lambda t: (0, 2)),
            whole(*norms.shape),
            whole(*coords.shape), whole(4, width), whole(4, width),
        ],
        out_specs=[
            tile_rows, near,
            pl.BlockSpec((1, pairs, TILE, 128), lambda t: (t, 0, 0, 0)),
            near, near,
            whole(padded_rows, width), whole(padded_rows, width),
            block3(GLOB_FORM, width), block3(GLOB_FORM, width), block3(GLOB_FORM, width),
            block3(GLOB_FORM, width), block3(GLOB_FORM, globs),
        ],
        out_shape=[
            jax.ShapeDtypeStruct((rows, width), BF16),
            near_shape,
            jax.ShapeDtypeStruct((tiles, pairs, TILE, 128), BF16),
            near_shape, near_shape,
            jax.ShapeDtypeStruct((padded_rows, width), BF16),
            jax.ShapeDtypeStruct((padded_rows, width), BF16),
            jax.ShapeDtypeStruct((blocks, GLOB_FORM, width), BF16),
            jax.ShapeDtypeStruct((blocks, GLOB_FORM, width), BF16),
            jax.ShapeDtypeStruct((blocks, GLOB_FORM, width), BF16),
            jax.ShapeDtypeStruct((blocks, GLOB_FORM, width), F32),
            jax.ShapeDtypeStruct((blocks, GLOB_FORM, globs), BF16),
        ],
        scratch_shapes=[
            pltpu.VMEM((TILE, SPAN), F32), pltpu.VMEM((TILE, SPAN), F32),
            pltpu.VMEM((TILE, SPAN), F32), pltpu.VMEM((TILE, SPAN), F32),
            pltpu.VMEM((UNROLL, 2 * TILE, SPAN), F32), pltpu.VMEM((UNROLL, TILE, 128), F32),
            pltpu.VMEM((UNROLL, TILE, 8), F32), pltpu.VMEM((UNROLL, 8, SPAN), F32),
        ],
        compiler_params=pltpu.CompilerParams(vmem_limit_bytes=VMEM_LIMIT),
        cost_estimate=cost(65.0),
        name="attn_forward",
    )(units, lengths, offset, rich_bias, rich_theta, q, k, v, before, after, every_glob, owner,
      w_qkv, w_qkv, norms, coords, rich_query, rich_key)


def bwd_kernel(offset_ref, bias_ref, theta_ref,
               q_ref, dc_ref, ctx_ref, k_ref, v_ref, kg_ref, vg_ref, coords_ref, rq_ref, rk_ref,
               pn_ref, pf_ref, g0_ref, g1_ref,
               dq_ref, dk_ref, dv_ref, dkg_ref, dvg_ref, vec_ref,
               dx_ref, dy_ref, dp_ref, dpf_ref, ds_ref, dsf_ref, a_ref, b_ref, dqr_ref, db_ref, db_now,
               *, pairs, first_pair, tiles, per_block, edge):
    step = pl.program_id(0)
    t = step * (tiles - 1) if edge else step + 1

    @pl.when(step == 0)
    def _():
        vec_ref[...] = jnp.zeros_like(vec_ref)
        if not edge:
            dk_ref[...] = jnp.zeros_like(dk_ref)
            dv_ref[...] = jnp.zeros_like(dv_ref)
            db_ref[...] = jnp.zeros_like(db_ref)

    if edge:
        fresh = step >= 0
    else:
        fresh = (step == 0) | (t % per_block == 0)

    @pl.when(fresh)
    def _():
        dkg_ref[...] = jnp.zeros_like(dkg_ref)
        dvg_ref[...] = jnp.zeros_like(dvg_ref)

    geometry_into(coords_ref, offset_ref[0, 0] // 128 + t - 1, None, (None, None, dx_ref, dy_ref))
    lo16, hi16 = half_masks(BF16)
    low64 = lax.broadcasted_iota(jnp.int32, (64, 128), 1) < 64
    lane8 = lax.broadcasted_iota(jnp.int32, (4, 128), 1)
    lane1 = lax.broadcasted_iota(jnp.int32, (1, 128), 1)
    sub = lax.broadcasted_iota(jnp.int32, (128, 1), 0)
    lo16c = (sub < 64).astype(F32).astype(BF16)
    hi16c = (sub >= 64).astype(F32).astype(BF16)
    rows = pl.ds(pl.multiple_of(t * TILE, TILE), SPAN)
    out_rows = pl.ds(pl.multiple_of((t - 1) * TILE, TILE), SPAN)

    def rich_key_parts(p, cols, sums, keys, columns):
        head = 2 * (p + first_pair)
        squares = [theta_ref[i, head + e] * theta_ref[i, head + e] for e in range(2) for i in range(2)]
        scales = by_row([1.0, 1.0, squares[0], squares[1], 1.0, 1.0, squares[2], squares[3]])
        scaled = sums * scales[:, 0:1]
        vectors = jnp.concatenate(split3(rich_rows(rk_ref[:, cols], None)), axis=0)
        parts = split3(scaled)
        left = jnp.concatenate([vectors[0:8]] * 3 + [vectors[8:16]] * 2 + [vectors[16:24]], axis=0)
        left = jnp.transpose(left).astype(BF16)
        right = jnp.concatenate([parts[0], parts[1], parts[2], parts[0], parts[1], parts[0]], axis=0).astype(BF16)
        extra = mm(left, right)
        stacked = jnp.concatenate(parts, axis=0).astype(BF16)
        key24 = mm(stacked, keys)
        key8 = key24[0:8] + key24[8:16] + key24[16:24]
        vec_ref[p, 4:8, :] += jnp.where(lane8 < 64, key8[0:4], key8[4:8])
        totals = jnp.sum(scaled, axis=1, keepdims=True)
        line = jnp.zeros((1, 128), F32)
        for index in range(8):
            line = jnp.where(lane1 == index, totals[index : index + 1, :], line)
        vec_ref[p, 8:9, :] += line
        return extra

    low_rows = lax.broadcasted_iota(jnp.int32, (BACK_CH, 128), 1) < 64

    def fold(full):
        return jnp.sum(full.reshape(full.shape[0] // 8, 8, full.shape[1]), axis=0)

    def pair_parts(p):
        cols = pl.ds(pl.multiple_of(p * 128, 128), 128)
        head = 2 * (p + first_pair)
        squares = [[theta_ref[i, head + e] * theta_ref[i, head + e] for i in range(2)] for e in range(2)]
        halves = [jnp.where(lane1 < 64, squares[0][i], squares[1][i]) for i in range(2)]
        return cols, head, halves

    def products(p, slot):
        cols, head, _ = pair_parts(p)
        qp = q_ref[:, cols]
        dcp = dc_ref[:, cols]
        kp = k_ref[rows, cols]
        vgp = vg_ref[0, :, cols]
        dp_ref[slot] = mm_nt(jnp.concatenate([dcp * lo16, dcp * hi16], axis=0), v_ref[rows, cols])
        dpf_ref[slot] = mm_nt(dcp, jnp.concatenate([vgp * lo16, vgp * hi16], axis=0))
        biases = by_row([bias_ref[c, head + e] for e in range(2) for c in range(4)])
        a, b = rich_sums(qp, kp, rq_ref[:, cols], rk_ref[:, cols], None, biases)
        a_ref[slot] = a
        b_ref[slot] = b

    def elements(p, slot):
        cols, head, halves = pair_parts(p)
        lines = [rq_ref[0:1, cols], rq_ref[1:2, cols], rq_ref[2:3, cols] * halves[0], rq_ref[3:4, cols] * halves[1]]
        col_sums = [[jnp.zeros((8, SPAN), F32) for _ in range(4)] for _ in range(2)]
        thetas = [[jnp.zeros((8, 128), F32) for _ in range(2)] for _ in range(2)]
        query_sums = [jnp.zeros((8, 128), F32) for _ in range(4)]
        for r in range(0, TILE, BACK_CH):
            rs = slice(r, r + BACK_CH)
            prod = dc_ref[rs, cols].astype(F32) * ctx_ref[rs, cols].astype(F32)
            row_sums = []
            dots = []
            for e in range(2):
                here = low_rows if e == 0 else ~low_rows
                base = 4 * e
                dot = jnp.sum(jnp.where(here, prod, 0.0), axis=1, keepdims=True)
                dots.append(dot)
                es = slice(e * TILE + r, e * TILE + r + BACK_CH)
                ds = pn_ref[0, 2 * p + e, rs, :].astype(F32) * (dp_ref[slot, es, :] - dot)
                ds_ref[slot, es, :] = ds.astype(BF16)
                t0 = ds * g0_ref[0, 2 * p + e, rs, :].astype(F32)
                t1 = ds * g1_ref[0, 2 * p + e, rs, :].astype(F32)
                gx = (dx_ref[rs, :] - a_ref[slot, rs, base + 2 : base + 3]) - b_ref[slot, base + 2 : base + 3, :]
                gy = (dy_ref[rs, :] - a_ref[slot, rs, base + 3 : base + 4]) - b_ref[slot, base + 3 : base + 4, :]
                tx = ds * gx
                ty = ds * gy
                for i, full in enumerate((tx * gx, ty * gy)):
                    thetas[e][i] = thetas[e][i] + fold(full[:, 0:128] + full[:, 128:256] + full[:, 256:384])
                sums = []
                for c, full in enumerate((t0, t1, tx, ty)):
                    col_sums[e][c] = col_sums[e][c] + fold(full)
                    sums.append(jnp.sum(full[:, 0:128] + full[:, 128:256] + full[:, 256:384], axis=1, keepdims=True))
                row_sums.append(sums)
            dsf = pf_ref[0, p, rs, :].astype(F32) * (dpf_ref[slot, rs, :] - jnp.where(low_rows, dots[0], dots[1]))
            dsf_ref[slot, rs, :] = dsf.astype(BF16)
            qf = q_ref[rs, cols].astype(F32)
            dqr = jnp.zeros((BACK_CH, 128), F32)
            for c in range(4):
                da = jnp.where(low_rows, row_sums[0][c], row_sums[1][c])
                dqr = dqr + da * lines[c]
                query_sums[c] = query_sums[c] + fold(da * qf)
            dqr_ref[slot, rs, :] = dqr
        folded = jnp.concatenate([jnp.sum(query_sums[c], axis=0, keepdims=True) for c in range(4)], axis=0)
        scale4 = jnp.concatenate([jnp.ones((2, 128), F32), halves[0], halves[1]], axis=0)
        vec_ref[p, 0:4, :] += folded * scale4
        line = jnp.zeros((1, 128), F32)
        for e in range(2):
            for i in range(2):
                total = jnp.sum(jnp.sum(thetas[e][i], axis=0, keepdims=True), axis=1, keepdims=True)
                line = jnp.where(lane1 == 8 + 2 * e + i, total * (-theta_ref[i, head + e]), line)
        vec_ref[p, 8:9, :] += line
        db_now[slot] = jnp.concatenate([jnp.sum(col_sums[e][c], axis=0, keepdims=True) for e in range(2) for c in range(4)], axis=0)

    def results(p, slot):
        cols, head, _ = pair_parts(p)
        qp = q_ref[:, cols]
        dcp = dc_ref[:, cols]
        kp = k_ref[rows, cols]
        kgp = kg_ref[0, :, cols]
        packed = db_now[slot]
        dq = mm(ds_ref[slot, 0:TILE, :], kp * lo16) + mm(ds_ref[slot, TILE : 2 * TILE, :], kp * hi16)
        dq = dq + mm(dsf_ref[slot], jnp.concatenate([kgp * lo16, kgp * hi16], axis=0))
        dq_ref[:, cols] = (dq * 0.125 + dqr_ref[slot]).astype(BF16)
        qT = jnp.transpose(qp)
        dcT = jnp.transpose(dcp)
        dk = mm(jnp.concatenate([qT * lo16c, qT * hi16c], axis=1), ds_ref[slot]) * 0.125
        dv = mm(dcT * lo16c, pn_ref[0, 2 * p]) + mm(dcT * hi16c, pn_ref[0, 2 * p + 1])
        if edge:
            dk_ref[0, cols, :] = dk + rich_key_parts(p, cols, packed, kp, rows)
            dv_ref[0, cols, :] = dv
        else:
            dk_ref[cols, out_rows] += dk
            dv_ref[cols, out_rows] += dv
            db_ref[p, :, out_rows] += packed
        dkg2 = mm(jnp.transpose(dsf_ref[slot]), qp) * 0.125
        dvg2 = mm(jnp.transpose(pf_ref[0, p]), dcp)
        dkg_ref[0, :, cols] += jnp.where(low64, dkg2[0:64], dkg2[64:128])
        dvg_ref[0, :, cols] += jnp.where(low64, dvg2[0:64], dvg2[64:128])

    def group(index, carry):
        first = index * BACK_UNROLL
        for stage in (products, elements, results):
            for u in range(BACK_UNROLL):
                stage(first + u, u)
        return carry

    lax.fori_loop(0, pairs // BACK_UNROLL, group, 0)

    if not edge:

        @pl.when(step == pl.num_programs(0) - 1)
        def _():
            own = k_ref.shape[0] - 2 * RADIUS

            def finish(p, carry):
                cols = pl.ds(pl.multiple_of(p * 128, 128), 128)
                keys = k_ref[RADIUS : RADIUS + own, cols]
                dk_ref[cols, :] += rich_key_parts(p, cols, db_ref[p], keys, None)
                return carry

            lax.fori_loop(0, pairs, finish, 0)


def attn_backward(q, dctx, ctx, k_pad, v_pad, kg, vg, coords, offset, rich, kept, first_pair, pairs, edge):
    rich_query, rich_key, rich_bias, rich_theta = rich
    rows, width = q.shape
    tiles = rows // TILE
    blocks = kg.shape[0]
    per_block = tiles // blocks
    part = pairs * 128
    half = first_pair // pairs
    steps = 2 if edge else tiles - 2
    padded_rows = k_pad.shape[0]
    scalars = pl.BlockSpec(memory_space=pltpu.SMEM)

    def tile(i):
        return i * (tiles - 1) if edge else i + 1

    tile_rows = pl.BlockSpec((TILE, part), lambda i: (tile(i), half))
    padded_cols = pl.BlockSpec((padded_rows, part), lambda i: (0, half))
    block3 = pl.BlockSpec((1, GLOB_FORM, part), lambda i: (tile(i) // per_block, 0, half))
    out3 = pl.BlockSpec((1, GLOB_FORM, part), lambda i: (tile(i) // per_block, 0, 0))
    vectors = pl.BlockSpec((4, part), lambda i: (0, half))
    near = pl.BlockSpec((1, 2 * pairs, TILE, SPAN), lambda i: (tile(i), half, 0, 0))
    far = pl.BlockSpec((1, pairs, TILE, 128), lambda i: (tile(i), half, 0, 0))
    if edge:
        key_out = pl.BlockSpec((1, part, SPAN), lambda i: (i, 0, 0))
        key_shape = jax.ShapeDtypeStruct((2, part, SPAN), F32)
    else:
        key_out = pl.BlockSpec((part, rows), lambda i: (0, 0))
        key_shape = jax.ShapeDtypeStruct((part, rows), F32)
    glob_shape = jax.ShapeDtypeStruct((blocks, GLOB_FORM, part), F32)
    return pl.pallas_call(
        partial(bwd_kernel, pairs=pairs, first_pair=first_pair, tiles=tiles, per_block=per_block, edge=edge),
        grid=(steps,),
        in_specs=[
            scalars, scalars, scalars,
            tile_rows, tile_rows, tile_rows, padded_cols, padded_cols, block3, block3,
            pl.BlockSpec(coords.shape, lambda i: (0, 0)), vectors, vectors,
            near, far, near, near,
        ],
        out_specs=[
            pl.BlockSpec((TILE, part), lambda i: (i, 0)),
            key_out, key_out, out3, out3,
            pl.BlockSpec((pairs, 16, 128), lambda i: (0, 0, 0)),
        ],
        out_shape=[
            jax.ShapeDtypeStruct((steps * TILE, part), BF16),
            key_shape, key_shape, glob_shape, glob_shape,
            jax.ShapeDtypeStruct((pairs, 16, 128), F32),
        ],
        scratch_shapes=[
            pltpu.VMEM((TILE, SPAN), F32), pltpu.VMEM((TILE, SPAN), F32),
            pltpu.VMEM((BACK_UNROLL, 2 * TILE, SPAN), F32), pltpu.VMEM((BACK_UNROLL, TILE, 128), F32),
            pltpu.VMEM((BACK_UNROLL, 2 * TILE, SPAN), BF16), pltpu.VMEM((BACK_UNROLL, TILE, 128), BF16),
            pltpu.VMEM((BACK_UNROLL, TILE, 8), F32), pltpu.VMEM((BACK_UNROLL, 8, SPAN), F32),
            pltpu.VMEM((BACK_UNROLL, TILE, 128), F32), pltpu.VMEM((pairs, 8, rows), F32),
            pltpu.VMEM((BACK_UNROLL, 8, SPAN), F32),
        ],
        compiler_params=pltpu.CompilerParams(vmem_limit_bytes=VMEM_LIMIT),
        cost_estimate=cost(8.2 * steps * pairs / 6),
        name="attn_backward_edge" if edge else "attn_backward_mid",
    )(offset, rich_bias, rich_theta, q, dctx, ctx, k_pad, v_pad, kg, vg, coords, rich_query, rich_key, *kept)


FF_CHUNK = 512
ROW_CHUNK = 256

TAIL_SLOPE = 0.35
TAIL = (0.0987331438, 0.0987265523, 0.092954664, 0.0773361877, 0.0814717893, -0.00727472285, 0.100604539, -0.0425525649)


def gelu_pair(values):
    t = 1.0 / (1.0 + (TAIL_SLOPE * math.sqrt(0.5)) * jnp.abs(values))
    poly = TAIL[-1] * t + TAIL[-2]
    for coef in TAIL[-3::-1]:
        poly = poly * t + coef
    bell = jnp.exp2((values * values) * (-0.5 * LOG2E))
    tail = t * poly * bell
    phi = jnp.where(values >= 0.0, 1.0 - tail, tail)
    return values * phi, phi + (values * bell) * (1.0 / math.sqrt(2.0 * math.pi))


def ffn_kernel(tok_ref, ctx_ref, ct_ref, wo_ref, wu_ref, wd_ref, norms_ref,
               out_ref, dmid_ref, dctx_ref, wog_ref, wug_ref, wdg_ref, vec_ref,
               mid_ref, h2_ref, h2t_ref, acc_ref, dh_ref, act_ref, dpre_ref, *, rows):
    step = pl.program_id(0)
    last = pl.num_programs(0) - 1

    @pl.when(step == 0)
    def _():
        for r in range(0, rows, ROW_CHUNK):
            rs = slice(r, r + ROW_CHUNK)
            mid = tok_ref[rs, :].astype(F32) + mm(ctx_ref[rs, :], wo_ref[...])
            mid_ref[rs, :] = mid
            normed, _ = norm_parts(mid)
            h2 = (normed * norms_ref[2:3, :] + norms_ref[3:4, :]).astype(BF16)
            h2_ref[rs, :] = h2
            h2t_ref[:, rs] = jnp.transpose(h2)
            acc_ref[rs, :] = jnp.zeros_like(mid)
            dh_ref[rs, :] = jnp.zeros_like(mid)

    def second(rs):
        acc_ref[rs, :] += mm(act_ref[rs, :], wd_ref[...])
        dh_ref[rs, :] += mm_nt(dpre_ref[rs, :], wu_ref[...])

    spans = [slice(r, r + ROW_CHUNK) for r in range(0, rows, ROW_CHUNK)]

    def first(rs):
        return mm(h2_ref[rs, :], wu_ref[...]), mm_nt(ct_ref[rs, :], wd_ref[...])

    ahead = first(spans[0])
    for index, rs in enumerate(spans):
        pre, dact = ahead
        if index + 1 < len(spans):
            ahead = first(spans[index + 1])
        act, slope = gelu_pair(pre)
        act_ref[rs, :] = act.astype(BF16)
        dpre_ref[rs, :] = (dact * slope).astype(BF16)
        if index > 0:
            second(spans[index - 1])
    second(spans[-1])
    wug_ref[...] = mm(h2t_ref[...], dpre_ref[...]).astype(BF16)
    wdg_ref[...] = mm_tn(act_ref[...], ct_ref[...]).astype(BF16)

    @pl.when(step == last)
    def _():
        gains = jnp.zeros((8, norms_ref.shape[1]), F32)
        shifts = jnp.zeros((8, norms_ref.shape[1]), F32)
        for r in range(0, rows, ROW_CHUNK):
            rs = slice(r, r + ROW_CHUNK)
            mid = mid_ref[rs, :]
            out_ref[rs, :] = (mid + acc_ref[rs, :]).astype(BF16)
            normed, scale = norm_parts(mid)
            dh = dh_ref[rs, :]
            gains = gains + jnp.sum((dh * normed).reshape(ROW_CHUNK // 8, 8, -1), axis=0)
            shifts = shifts + jnp.sum(dh.reshape(ROW_CHUNK // 8, 8, -1), axis=0)
            dmid = ct_ref[rs, :].astype(F32) + norm_pull(dh, normed, scale, norms_ref[2:3, :])
            dmid_ref[rs, :] = dmid
            dattn = dmid.astype(BF16)
            h2_ref[rs, :] = dattn
            dctx_ref[rs, :] = mm_nt(dattn, wo_ref[...]).astype(BF16)
        wog_ref[...] = mm_tn(ctx_ref[...], h2_ref[...]).astype(BF16)
        vec_ref[0:1, :] = jnp.sum(gains, axis=0, keepdims=True)
        vec_ref[1:2, :] = jnp.sum(shifts, axis=0, keepdims=True)

def feed_forward(tokens, context, cotangent, w_out, w_up, w_down, norms):
    rows, width = tokens.shape
    hidden = w_up.shape[1]
    steps = hidden // FF_CHUNK
    whole = lambda *shape: pl.BlockSpec(shape, lambda s: (0,) * len(shape))
    return pl.pallas_call(
        partial(ffn_kernel, rows=rows),
        grid=(steps,),
        in_specs=[
            whole(rows, width), whole(rows, width), whole(rows, width), whole(width, width),
            pl.BlockSpec((width, FF_CHUNK), lambda s: (0, s)),
            pl.BlockSpec((FF_CHUNK, width), lambda s: (s, 0)),
            whole(*norms.shape),
        ],
        out_specs=[
            whole(rows, width), whole(rows, width), whole(rows, width), whole(width, width),
            pl.BlockSpec((width, FF_CHUNK), lambda s: (0, s)),
            pl.BlockSpec((FF_CHUNK, width), lambda s: (s, 0)),
            whole(8, width),
        ],
        out_shape=[
            jax.ShapeDtypeStruct((rows, width), BF16),
            jax.ShapeDtypeStruct((rows, width), F32),
            jax.ShapeDtypeStruct((rows, width), BF16),
            jax.ShapeDtypeStruct((width, width), BF16),
            jax.ShapeDtypeStruct((width, hidden), BF16),
            jax.ShapeDtypeStruct((hidden, width), BF16),
            jax.ShapeDtypeStruct((8, width), F32),
        ],
        scratch_shapes=[
            pltpu.VMEM((rows, width), F32), pltpu.VMEM((rows, width), BF16), pltpu.VMEM((width, rows), BF16),
            pltpu.VMEM((rows, width), F32), pltpu.VMEM((rows, width), F32),
            pltpu.VMEM((rows, FF_CHUNK), BF16), pltpu.VMEM((rows, FF_CHUNK), BF16),
        ],
        compiler_params=pltpu.CompilerParams(vmem_limit_bytes=VMEM_LIMIT),
        cost_estimate=cost(60.0),
        name="feed_forward",
    )(tokens, context, cotangent, w_out, w_up, w_down, norms)


def qkv_back_kernel(*refs, half, final, pairs, kept):
    (ht_ref, hg_ref, w_ref, dqe_ref, dqm_ref, dke_ref, dve_ref, dkm_ref, dvm_ref, before_ref, after_ref,
     dkge_ref, dvge_ref, dkgm_ref, dvgm_ref) = refs[:15]
    refs = refs[15:]
    if final:
        (dh0_ref, dhg0_ref, tok_ref, dmid_ref, norms_ref, oh_ref, ng_ref, second_ref, ve_ref, va_ref, vb_ref) = refs[:11]
        refs = refs[11:]
        grad_ref, vec_ref, tg_ref, gp_ref, dh_ref, dhg_ref, part_ref, dkt_ref, rows_ref = refs
    else:
        grad_ref, dh_ref, dhg_ref, part_ref, dkt_ref = refs
    step = pl.program_id(0)
    rows, part = part_ref.shape
    width = ht_ref.shape[0]
    edge = 128

    @pl.when(step == 0)
    def _():
        part_ref[0:edge, :] = dqe_ref[0:edge, :]
        part_ref[edge : rows - edge, :] = dqm_ref[...]
        part_ref[rows - edge : rows, :] = dqe_ref[edge : 2 * edge, :]

    for index, edge_ref, mid_ref in ((1, dke_ref, dkm_ref), (2, dve_ref, dvm_ref)):

        @pl.when(step == index)
        def _():
            dkt_ref[...] = mid_ref[...].astype(BF16)
            dkt_ref[:, 0:128] = (mid_ref[:, 0:128] + edge_ref[0, :, 128:256] + before_ref[index - 1].astype(F32)).astype(BF16)
            dkt_ref[:, 128:256] = (mid_ref[:, 128:256] + edge_ref[0, :, 256:384]).astype(BF16)
            dkt_ref[:, rows - 256 : rows - 128] = (mid_ref[:, rows - 256 : rows - 128] + edge_ref[1, :, 0:128]).astype(BF16)
            dkt_ref[:, rows - 128 : rows] = (
                mid_ref[:, rows - 128 : rows] + edge_ref[1, :, 128:256] + after_ref[index - 1].astype(F32)
            ).astype(BF16)
            part_ref[...] = jnp.transpose(dkt_ref[...])

    grad = mm(ht_ref[...], part_ref[...])
    moved = mm_nt(part_ref[...], w_ref[...])

    @pl.when(step == 0)
    def _():
        grad_ref[...] = grad.astype(BF16)
        if final:
            dh_ref[...] = dh0_ref[...] + moved
            dhg_ref[...] = dhg0_ref[...]
        else:
            dh_ref[...] = moved
            dhg_ref[...] = jnp.zeros_like(dhg_ref)

    for index, edge_ref, mid_ref in ((1, dkge_ref, dkgm_ref), (2, dvge_ref, dvgm_ref)):

        @pl.when(step == index)
        def _():
            glob = (edge_ref[...] + mid_ref[...]).reshape(-1, part).astype(BF16)
            hg = hg_ref[...].reshape(-1, width)
            grad_ref[...] = (grad + mm_tn(hg, glob)).astype(BF16)
            dh_ref[...] += moved
            dhg_ref[...] += mm_nt(glob, w_ref[...])

    if final:

        @pl.when(step == 2)
        def _():
            gains = jnp.zeros((8, width), F32)
            shifts = jnp.zeros((8, width), F32)
            for r in range(0, rows, 128):
                rs = slice(r, r + 128)
                normed, scale = norm_parts(tok_ref[rs, :].astype(F32))
                dh = dh_ref[rs, :]
                gains = gains + jnp.sum((dh * normed).reshape(16, 8, width), axis=0)
                shifts = shifts + jnp.sum(dh.reshape(16, 8, width), axis=0)
                tg_ref[rs, :] = (dmid_ref[rs, :] + norm_pull(dh, normed, scale, norms_ref[0:1, :])).astype(BF16)
            dhg = dhg_ref[...]
            normed = ng_ref[...].reshape(-1, width)
            rows_ref[...] = jnp.zeros_like(rows_ref)
            rows_ref[0:1, :] = jnp.sum(gains, axis=0, keepdims=True) + jnp.sum(dhg * normed, axis=0, keepdims=True)
            rows_ref[1:2, :] = jnp.sum(shifts, axis=0, keepdims=True) + jnp.sum(dhg, axis=0, keepdims=True)
            rows_ref[2:4, :] = second_ref[0:2, :]
            gp_ref[...] = mm_tn(oh_ref[...].reshape(-1, oh_ref.shape[2]), dhg.astype(BF16)).astype(BF16)
            lines = []
            for p in range(2 * pairs):
                mid = va_ref[p] if p < pairs else vb_ref[p - pairs]
                both = ve_ref[p] + mid
                rows_ref[4:12, p * 128 : p * 128 + 128] = both[0:8]
                lines.append(both[8:9])
            lines.append(jnp.zeros((8 - len(lines), 128), F32))
            lines = jnp.concatenate(split3(jnp.concatenate(lines, axis=0)), axis=0).astype(BF16)
            spot = lax.broadcasted_iota(jnp.int32, (128, width), 0)
            lane = lax.broadcasted_iota(jnp.int32, (128, width), 1)
            spread = mm(lines, (lax.rem(lane, kept) == spot).astype(F32).astype(BF16))
            rows_ref[12:20, :] = spread[0:8] + spread[8:16] + spread[16:24]
            vec_ref[...] = jnp.transpose(rows_ref[...]).astype(BF16)


def qkv_backward(hidden_t, hg, w_qkv, dq, dk, dv, rims, dkg, dvg, half, pairs, kept, last=None):
    width, rows = hidden_t.shape
    part = pairs * 128
    halves = width // part
    final = last is not None

    def whole(*shape):
        return pl.BlockSpec(shape, lambda i: (0,) * len(shape))

    blocks = hg.shape[0]
    edge_keys = pl.BlockSpec((2, part, SPAN), lambda i: (0, half, 0))
    edge_glob = pl.BlockSpec((blocks, GLOB_FORM, part), lambda i: (0, 0, half))
    rim = pl.BlockSpec((2, part, RADIUS), lambda i: (0, half, 0))
    operands = [hidden_t, hg, w_qkv, dq[0], dq[1], dk[0], dv[0], dk[1], dv[1], rims[0], rims[1],
                dkg[0], dvg[0], dkg[1], dvg[1]]
    in_specs = [
        whole(width, rows), whole(blocks, GLOB_FORM, width),
        pl.BlockSpec((width, part), lambda i: (0, halves * i + half)),
        pl.BlockSpec((2 * TILE, part), lambda i: (0, half)), whole(rows - 2 * TILE, part),
        edge_keys, edge_keys, whole(part, rows), whole(part, rows), rim, rim,
        edge_glob, edge_glob, whole(blocks, GLOB_FORM, part), whole(blocks, GLOB_FORM, part),
    ]
    out_specs = [pl.BlockSpec((width, part), lambda i: (0, i))]
    out_shape = [jax.ShapeDtypeStruct((width, 3 * part), BF16)]
    scratch = [pltpu.VMEM((rows, part), BF16), pltpu.VMEM((part, rows), BF16)]
    sums_shape = [(rows, width), (blocks * GLOB_FORM, width)]
    if final:
        operands += list(last)
        in_specs += [whole(*a.shape) for a in last]
        globs = last[5].shape[2]
        out_specs += [whole(width, 128), whole(rows, width), whole(globs, width)]
        out_shape += [
            jax.ShapeDtypeStruct((width, 128), BF16),
            jax.ShapeDtypeStruct((rows, width), BF16),
            jax.ShapeDtypeStruct((globs, width), BF16),
        ]
        scratch = [pltpu.VMEM(s, F32) for s in sums_shape] + scratch + [pltpu.VMEM((128, width), F32)]
    else:
        out_specs += [whole(*s) for s in sums_shape]
        out_shape += [jax.ShapeDtypeStruct(s, F32) for s in sums_shape]
    return pl.pallas_call(
        partial(qkv_back_kernel, half=half, final=final, pairs=pairs, kept=kept),
        grid=(3,),
        in_specs=in_specs,
        out_specs=out_specs,
        out_shape=out_shape,
        scratch_shapes=scratch,
        compiler_params=pltpu.CompilerParams(vmem_limit_bytes=VMEM_LIMIT),
        cost_estimate=cost(15.0 if final else 8.0),
        name="qkv_backward",
    )(*operands)


def swap_on(axis, mask):
    return [(i, i ^ mask) for i in range(lax.axis_size(axis))]


def add_low(kept, received):
    return (kept.astype(F32) + received.astype(F32)).astype(BF16)


def core_halves(grads, place):
    count = lax.axis_size("seq")
    view = grads.reshape(count // 2, 2, grads.shape[0] // count, grads.shape[1])
    send = lax.dynamic_index_in_dim(view, 1 - place % 2, 1, keepdims=False)
    kept = lax.dynamic_index_in_dim(view, place % 2, 1, keepdims=False)
    return kept, send


def core_swap(send):
    return lax.ppermute(send, "seq", swap_on("seq", 1))


def stream_blocks(summed, group_count):
    outer, rows, columns = summed.shape
    return jnp.moveaxis(summed.reshape(outer, group_count, rows // group_count, columns), 1, 0)


def halve_step(blocks, axis, place, bit, width):
    mine = (place >> bit) & 1
    send = lax.dynamic_index_in_dim(blocks, 1 - mine, width, keepdims=False)
    kept = lax.dynamic_index_in_dim(blocks, mine, width, keepdims=False)
    return add_low(kept, lax.ppermute(send, axis, swap_on(axis, 1 << bit)))


def exchange_sum(blocks, axis, place, stride):
    count = blocks.shape[0]
    total = lax.dynamic_index_in_dim(blocks, place, 0, keepdims=False).astype(F32)
    for step in range(1, count):
        send = lax.dynamic_index_in_dim(blocks, place ^ step, 0, keepdims=False)
        total = total + lax.ppermute(send, axis, swap_on(axis, step * stride)).astype(F32)
    return total.astype(BF16)


def exchange_all(piece, axis, place):
    count = lax.axis_size(axis)
    every = [piece] + [lax.ppermute(piece, axis, swap_on(axis, step)) for step in range(1, count)]
    return ordered(jnp.stack(every), place)


def gather_rows(rows, axis, place, bit):
    other = lax.ppermute(rows, axis, swap_on(axis, bit))
    upper = (place & bit) > 0
    return jnp.concatenate([jnp.where(upper, other, rows), jnp.where(upper, rows, other)], axis=0)


def gather_blocks(rows, axis, place, stride):
    count = lax.axis_size(axis) // stride
    every = [rows] + [lax.ppermute(rows, axis, swap_on(axis, step * stride)) for step in range(1, count)]
    return ordered(jnp.stack(every), place).reshape(count * rows.shape[0], rows.shape[1])


def ordered(stacked, place):
    count = stacked.shape[0]
    rest = stacked.shape[1:]
    bit = 1
    while bit < count:
        view = stacked.reshape((count // (2 * bit), 2, bit) + rest)
        stacked = jnp.where((place & bit) > 0, view[:, ::-1], view).reshape((count,) + rest)
        bit *= 2
    return stacked


def tied(*values):
    return lax.optimization_barrier(values)


def body(
    tokens,
    global_states,
    cotangent,
    w_qkv,
    w_out,
    w_up,
    w_down,
    first_gain,
    first_shift,
    second_gain,
    second_shift,
    rich_query,
    rich_key,
    rich_bias,
    rich_theta,
    bucket_units,
    form_lengths,
    coords,
    glob_owner,
):
    row_count = tokens.shape[1]
    model_width = tokens.shape[2]
    place = lax.axis_index("seq")
    group = lax.axis_index("stream")
    seq_count = lax.axis_size("seq")
    group_count = lax.axis_size("stream")
    rich = (rich_query, rich_key, rich_bias, rich_theta)
    offset = (place * row_count).astype(jnp.int32).reshape(1, 1)
    norms = jnp.stack([first_gain, first_shift, second_gain, second_shift])
    up = [(i, i + 1) for i in range(seq_count - 1)]
    down = [(i + 1, i) for i in range(seq_count - 1)]
    pairs = rich_bias.shape[1] // 2
    half_pairs = pairs // 2
    kept_rows = model_width // seq_count

    before = lax.ppermute(tokens[0, row_count - RADIUS :], "seq", up)
    after = lax.ppermute(tokens[0, :RADIUS], "seq", down)
    pair_glob = gather_rows(global_states[0], "seq", place, 1)
    pair_glob, norms, before, after = tied(pair_glob, norms, before, after)
    every_glob = gather_blocks(pair_glob, "seq", place // 2, 2)
    queries, keys, values, hidden_t = project_tokens(tokens[0], w_qkv, norms)
    (context, pn, pf, g0, g1, key_pad, value_pad, glob_keys, glob_values, glob_hidden, glob_normed, picked) = attn_forward(
        queries, keys, values, before, after, every_glob, glob_owner, w_qkv, norms,
        coords[0], bucket_units, form_lengths, offset, rich,
    )
    layer_out, grad_middle, grad_context, grad_w_out, grad_w_up, grad_w_down, second_sums = feed_forward(
        tokens[0], context, cotangent[0], w_out, w_up, w_down, norms
    )

    def attention_back(first_pair, count, edge, grad_context):
        return attn_backward(
            queries, grad_context, context, key_pad, value_pad, glob_keys, glob_values, coords[0], offset, rich,
            (pn, pf, g0, g1), first_pair, count, edge,
        )

    halves = [core_halves(grad, place) for grad in (grad_w_up, grad_w_down, grad_w_out)]
    sends = [half[1] for half in halves]
    grad_context, *sends = tied(grad_context, *sends)
    halves = [(half[0], core_swap(send)) for half, send in zip(halves, sends)]
    dq_e, dk_e, dv_e, dkg_e, dvg_e, vec_e = attention_back(0, pairs, True, grad_context)
    to_before = jnp.stack([dk_e[0, :, :RADIUS], dv_e[0, :, :RADIUS]]).astype(BF16)
    to_after = jnp.stack([dk_e[1, :, 2 * RADIUS :], dv_e[1, :, 2 * RADIUS :]]).astype(BF16)
    rims = (lax.ppermute(to_after, "seq", up), lax.ppermute(to_before, "seq", down))

    (dq_e, *swapped) = tied(dq_e, *[half[1] for half in halves])
    halves = [(half[0], received) for half, received in zip(halves, swapped)]

    sums = [add_low(*half) for half in halves]
    outer = seq_count // 2
    bits = group_count.bit_length() - 1
    pieces = [
        jnp.moveaxis(sums[0].reshape(outer, kept_rows, group_count, -1), 2, 0).reshape(group_count, outer, -1, model_width),
        jnp.moveaxis(sums[1].reshape(outer, group_count, -1, model_width), 1, 0),
        jnp.moveaxis(sums[2].reshape(outer, group_count, -1, model_width), 1, 0),
    ]
    piece_rows = [piece.shape[2] for piece in pieces]
    early = jnp.concatenate(pieces, axis=2).reshape((2,) * bits + (outer, sum(piece_rows), model_width))
    columns = model_width // 2
    early_x, early_y = early[..., :columns], early[..., columns:]
    order_x = list(range(bits))
    order_y = order_x[1:] + order_x[:1]

    def halved(blocks, order, done):
        bit = order[done]
        rest = sorted(order[done:], reverse=True)
        return halve_step(blocks, "stream", group, bit, rest.index(bit))

    early_x, early_y, grad_context, *rims = tied(early_x, early_y, grad_context, *rims)
    early_x = halved(early_x, order_x, 0)
    early_y = halved(early_y, order_y, 0)
    dq_a, dk_a, dv_a, dkg_a, dvg_a, vec_a = attention_back(0, half_pairs, False, grad_context)
    early_x, early_y, dq_a = tied(early_x, early_y, dq_a)
    for done in range(1, bits):
        early_x = halved(early_x, order_x, done)
        early_y = halved(early_y, order_y, done)
    grads_a, grad_hidden, grad_glob_hidden = qkv_backward(
        hidden_t, glob_hidden, w_qkv, (dq_e, dq_a), (dk_e, dk_a), (dv_e, dv_a), rims,
        (dkg_e, dkg_a), (dvg_e, dvg_a), 0, half_pairs, kept_rows,
    )
    kept_a, send_a = core_halves(grads_a, place)
    early = jnp.concatenate([early_x, early_y], axis=-1)
    late_a = stream_blocks(add_low(kept_a, core_swap(send_a)), group_count)
    early, late_a, grad_context = tied(early, late_a, grad_context)
    dq_b, dk_b, dv_b, dkg_b, dvg_b, vec_b = attention_back(half_pairs, half_pairs, False, grad_context)
    early = exchange_sum(early, "seq", place // 2, 2)
    early, dq_b = tied(early, dq_b)
    early = exchange_all(early, "stream", group)
    late_a, dq_b = tied(late_a, dq_b)
    late_a = exchange_sum(late_a, "stream", group, 1)
    late_a = exchange_sum(late_a, "seq", place // 2, 2)
    grads_b, vectors, tokens_grad, glob_part = qkv_backward(
        hidden_t, glob_hidden, w_qkv, (dq_e, dq_b), (dk_e, dk_b), (dv_e, dv_b), rims,
        (dkg_e, dkg_b), (dvg_e, dvg_b), 1, half_pairs, kept_rows,
        (grad_hidden, grad_glob_hidden, tokens[0], grad_middle, norms, picked, glob_normed, second_sums, vec_e, vec_a, vec_b),
    )

    early, late_a, grads_b = tied(early, late_a, grads_b)
    share_a = exchange_all(late_a, "stream", group).reshape(kept_rows, -1).astype(F32)
    kept_b, send_b = core_halves(jnp.concatenate([grads_b, vectors], axis=1), place)
    late_b = stream_blocks(add_low(kept_b, core_swap(send_b)), group_count)
    late_b = exchange_sum(late_b, "stream", group, 1)
    late_b = exchange_sum(late_b, "seq", place // 2, 2)
    share_b = exchange_all(late_b, "stream", group).reshape(kept_rows, -1).astype(F32)
    kept_glob, send_glob = core_halves(glob_part, place)
    glob_blocks = add_low(kept_glob, core_swap(send_glob))
    grad_glob = exchange_sum(glob_blocks, "seq", place // 2, 2).astype(F32)
    own_glob, own_scale = norm_parts(global_states[0].astype(F32))
    glob_grad = norm_pull(grad_glob, own_glob, own_scale, first_gain).astype(BF16)

    part = half_pairs * 128
    share_qkv = jnp.concatenate(
        [share[:, i * part : (i + 1) * part] for i in range(3) for share in (share_a, share_b)], axis=1
    )
    cuts = [0, piece_rows[0], piece_rows[0] + piece_rows[1], sum(piece_rows)]
    early = early.astype(F32)
    share_up = jnp.moveaxis(early[:, : cuts[1]].reshape(group_count, kept_rows, -1), 0, 1).reshape(kept_rows, -1)
    share_down = early[:, cuts[1] : cuts[2]].reshape(-1, model_width)
    share_out = early[:, cuts[2] :].reshape(-1, model_width)
    small = share_b[:, 3 * part :]
    own_vectors = small[:, :12].T
    heads = small[:12, 12 : 12 + pairs].T.reshape(pairs, 12)
    bias_grad = heads[:, :8].reshape(pairs, 2, 4).transpose(2, 0, 1).reshape(rich_bias.shape)
    theta_grad = heads[:, 8:].reshape(pairs, 2, 2).transpose(2, 0, 1).reshape(rich_theta.shape)
    return (
        layer_out[None],
        tokens_grad[None],
        glob_grad[None],
        share_qkv,
        share_out,
        share_up,
        share_down,
        own_vectors[0],
        own_vectors[1],
        own_vectors[2],
        own_vectors[3],
        own_vectors[4:8],
        own_vectors[8:12],
        bias_grad,
        theta_grad,
    )


def solution(mesh):
    return jax.shard_map(
        body,
        mesh=mesh,
        in_specs=(
            P("stream", "seq", None),
            P("stream", "seq", None),
            P("stream", "seq", None),
            P(),
            P(),
            P(),
            P(),
            P(),
            P(),
            P(),
            P(),
            P(),
            P(),
            P(),
            P(),
            P("stream", None),
            P("stream", None),
            P("stream", None, None),
            P("stream", None),
        ),
        out_specs=(
            P("stream", "seq", None),
            P("stream", "seq", None),
            P("stream", "seq", None),
            P("seq", None),
            P("seq", None),
            P("seq", None),
            P("seq", None),
            P("seq"),
            P("seq"),
            P("seq"),
            P("seq"),
            P(None, "seq"),
            P(None, "seq"),
            P(),
            P(),
        ),
        check_vma=False,
    )
```

```python
from functools import partial
import math

import jax
import jax.numpy as jnp
from jax import lax
from jax.experimental import pallas as pl
from jax.experimental.pallas import tpu as pltpu
from jax.sharding import PartitionSpec as P

RADIUS = 128
GLOB_FORM = 64
QBLOCK = 512
TOK_DEV = 1024


EPSILON = 1e-06


TILE = 128
SPAN = 384
LOG2E = math.log2(math.e)
FAR_AWAY = 1e15
CH = 128
UNROLL = 6
BACK_CH = 128
BACK_UNROLL = 3
F32 = jnp.float32
BF16 = jnp.bfloat16
VMEM_LIMIT = 58 * 1024 * 1024


def mm(a, b):
    return lax.dot_general(a, b, (((1,), (0,)), ((), ())), preferred_element_type=F32)


def mm_nt(a, b):
    return lax.dot_general(a, b, (((1,), (1,)), ((), ())), preferred_element_type=F32)


def mm_tn(a, b):
    return lax.dot_general(a, b, (((0,), (0,)), ((), ())), preferred_element_type=F32)


def norm_parts(values):
    centre = jnp.mean(values, axis=-1, keepdims=True)
    centred = values - centre
    spread = jnp.mean(centred * centred, axis=-1, keepdims=True)
    scale = lax.rsqrt(spread + EPSILON)
    return centred * scale, scale


def norm_pull(grad, normed, scale, gain):
    e = grad * gain
    mean_e = jnp.mean(e, axis=-1, keepdims=True)
    mean_en = jnp.mean(e * normed, axis=-1, keepdims=True)
    return scale * (e - mean_e - normed * mean_en)


def split3(values):
    hi = values.astype(BF16).astype(F32)
    rest = values - hi
    mid = rest.astype(BF16).astype(F32)
    return hi, mid, rest - mid


def half_masks(dtype):
    lane = lax.broadcasted_iota(jnp.int32, (1, 128), 1)
    low = (lane < 64).astype(F32)
    return low.astype(dtype), (1.0 - low).astype(dtype)


def by_row(values):
    row = lax.broadcasted_iota(jnp.int32, (8, 128), 0)
    out = jnp.full((8, 128), values[7], F32)
    for index in range(7):
        out = jnp.where(row == index, values[index], out)
    return out


def rich_rows(vectors, scales):
    row = lax.broadcasted_iota(jnp.int32, (8, 128), 0)
    lane = lax.broadcasted_iota(jnp.int32, (8, 128), 1)
    both = jnp.concatenate([vectors, vectors], axis=0)
    both = both if scales is None else both * scales
    return jnp.where((row < 4) == (lane < 64), both, 0.0)


def rich_sums(qp, kp, query_vec, key_vec, scales, bias8):
    rq = jnp.concatenate(split3(rich_rows(query_vec, scales)), axis=1).astype(BF16)
    rk = jnp.concatenate(split3(rich_rows(key_vec, scales)), axis=0).astype(BF16)
    a = mm_nt(jnp.concatenate([qp, qp, qp], axis=1), rq)
    b24 = mm_nt(rk, kp)
    return a, b24[0:8] + b24[8:16] + b24[16:24] + bias8[:, 0:1]


def form_of(units_ref, lengths_ref, row):
    form, low, high, before = 0, 0, lengths_ref[0, 0], 0
    for index in range(1, units_ref.shape[1]):
        before = before + units_ref[0, index - 1]
        start = TOK_DEV // 2 + TOK_DEV * before
        taken = row >= start
        form = jnp.where(taken, index, form)
        low = jnp.where(taken, start, low)
        high = jnp.where(taken, start + lengths_ref[0, index], high)
    return form, low, high


def coord_row(coords_ref, axis, tile_index):
    tile_index = jnp.clip(tile_index, 0, coords_ref.shape[1] // 128 - 1)
    return coords_ref[axis : axis + 1, pl.ds(pl.multiple_of(tile_index * 128, 128), 128)].astype(F32)


def query_columns(coords_ref, axis, tile_index):
    return jnp.transpose(jnp.broadcast_to(coord_row(coords_ref, axis, tile_index), (128, 128)))


def geometry_into(coords_ref, first_tile, span, refs):
    ox_ref, oy_ref, dx_ref, dy_ref = refs
    xq = query_columns(coords_ref, 0, first_tile + 1)
    yq = query_columns(coords_ref, 1, first_tile + 1)
    for lt in range(3):
        xk = coord_row(coords_ref, 0, first_tile + lt)
        yk = coord_row(coords_ref, 1, first_tile + lt)
        out = (slice(None), slice(lt * 128, lt * 128 + 128))
        dx = jnp.log(1.0 + jnp.abs(xq - xk))
        dy = jnp.log(1.0 + jnp.abs(yq - yk))
        if span is not None:
            row = lax.broadcasted_iota(jnp.int32, (128, 128), 0)
            col = lax.broadcasted_iota(jnp.int32, (128, 128), 1) + lt * 128
            near = (col >= row) & (col - row <= 2 * RADIUS)
            dx = jnp.where(near & (col >= span[0]) & (col < span[1]), dx, FAR_AWAY)
            ox_ref[out] = jnp.where(xk > xq, 1.0, -1.0)
            oy_ref[out] = jnp.where(yk > yq, 1.0, -1.0)
        dx_ref[out] = dx
        dy_ref[out] = dy


def qkv_kernel(tok_ref, w_ref, norms_ref, q_ref, k_ref, v_ref, ht_ref):
    width = tok_ref.shape[1]
    normed, _ = norm_parts(tok_ref[...].astype(F32))
    hidden = (normed * norms_ref[0:1, :] + norms_ref[1:2, :]).astype(BF16)
    for index, out in enumerate((q_ref, k_ref, v_ref)):
        out[...] = mm(hidden, w_ref[:, index * width : (index + 1) * width]).astype(BF16)
    ht_ref[...] = jnp.transpose(hidden)


def project_tokens(tokens, w_qkv, norms):
    rows, width = tokens.shape
    step = 256
    block = pl.BlockSpec((step, width), lambda i: (i, 0))
    return pl.pallas_call(
        qkv_kernel,
        grid=(rows // step,),
        in_specs=[block, pl.BlockSpec(w_qkv.shape, lambda i: (0, 0)), pl.BlockSpec(norms.shape, lambda i: (0, 0))],
        out_specs=[block, block, block, pl.BlockSpec((width, step), lambda i: (0, i))],
        out_shape=[jax.ShapeDtypeStruct((rows, width), BF16)] * 3 + [jax.ShapeDtypeStruct((width, rows), BF16)],
        compiler_params=pltpu.CompilerParams(vmem_limit_bytes=VMEM_LIMIT),
        cost_estimate=cost(8.0),
        name="project_tokens",
    )(tokens, w_qkv, norms)


def cost(micros):
    return pl.CostEstimate(flops=int(micros * 1e9), bytes_accessed=0, transcendentals=0)


def global_pairs(form, owner_ref, glob_ref, norms_ref, kw_ref, vw_ref, kg_ref, vg_ref, hg_ref, ng_ref, oh_ref):
    count = glob_ref.shape[0]
    match = (owner_ref[...] == form).astype(F32)
    row = lax.broadcasted_iota(jnp.int32, (count, count), 0)
    col = lax.broadcasted_iota(jnp.int32, (count, count), 1)
    upto = (row <= col).astype(F32).astype(BF16)
    rank = mm(jnp.broadcast_to(match, (16, count)).astype(BF16), upto)[0:1]
    slot = lax.broadcasted_iota(jnp.int32, (GLOB_FORM, count), 0).astype(F32) + 1.0
    picked = jnp.where(rank == slot, match, 0.0).astype(BF16)
    oh_ref[0] = picked
    normed, _ = norm_parts(mm(picked, glob_ref[...]))
    ng_ref[0] = normed
    hidden = (normed * norms_ref[0:1, :] + norms_ref[1:2, :]).astype(BF16)
    hg_ref[0] = hidden
    kg_ref[0] = mm(hidden, kw_ref[...]).astype(BF16)
    vg_ref[0] = mm(hidden, vw_ref[...]).astype(BF16)


def fwd_kernel(units_ref, lengths_ref, offset_ref, bias_ref, theta_ref,
               q_ref, k_ref, v_ref, before_ref, after_ref, glob_ref, owner_ref, kw_ref, vw_ref, norms_ref,
               coords_ref, rq_ref, rk_ref,
               ctx_ref, pn_ref, pf_ref, g0_ref, g1_ref, kp_ref, vp_ref, kg_ref, vg_ref, hg_ref, ng_ref, oh_ref,
               ox_ref, oy_ref, dx_ref, dy_ref, s_ref, sf_ref, a_ref, b_ref, *, pairs, per_block):
    t = pl.program_id(0)
    rows_all = k_ref.shape[0]
    offset = offset_ref[0, 0]
    first = offset + t * TILE
    form, low_end, high_end = form_of(units_ref, lengths_ref, first)

    @pl.when(t == 0)
    def _():
        for refs in ((k_ref, kp_ref, kw_ref), (v_ref, vp_ref, vw_ref)):
            own, padded_ref, weight = refs
            padded_ref[RADIUS : RADIUS + rows_all, :] = own[...]
        for halo, start in ((before_ref, 0), (after_ref, RADIUS + rows_all)):
            normed, _ = norm_parts(halo[...].astype(F32))
            hidden = (normed * norms_ref[0:1, :] + norms_ref[1:2, :]).astype(BF16)
            kp_ref[start : start + RADIUS, :] = mm(hidden, kw_ref[...]).astype(BF16)
            vp_ref[start : start + RADIUS, :] = mm(hidden, vw_ref[...]).astype(BF16)

    @pl.when(t % per_block == 0)
    def _():
        global_pairs(form, owner_ref, glob_ref, norms_ref, kw_ref, vw_ref, kg_ref, vg_ref, hg_ref, ng_ref, oh_ref)

    shifted = first - RADIUS
    geometry_into(coords_ref, offset // 128 + t - 1, (low_end - shifted, high_end - shifted), (ox_ref, oy_ref, dx_ref, dy_ref))
    lo16, hi16 = half_masks(BF16)
    lane = lax.broadcasted_iota(jnp.int32, (CH, 128), 1)
    low = lane < 64
    rows = pl.ds(pl.multiple_of(t * TILE, TILE), SPAN)
    root = math.sqrt(0.5 * LOG2E)

    def widths_of(p):
        return [[theta_ref[i, 2 * p + e] * root for i in range(2)] for e in range(2)]

    def scores(p, slot):
        cols = pl.ds(pl.multiple_of(p * 128, 128), 128)
        qp = q_ref[:, cols]
        kp = kp_ref[rows, cols]
        kgp = kg_ref[0, :, cols]
        widths = widths_of(p)
        scales = by_row([LOG2E, LOG2E] + widths[0] + [LOG2E, LOG2E] + widths[1])
        biases = by_row([bias_ref[c, 2 * p + e] for e in range(2) for c in range(4)]) * scales
        s_ref[slot] = mm_nt(jnp.concatenate([qp * lo16, qp * hi16], axis=0), kp)
        sf_ref[slot] = mm_nt(qp, jnp.concatenate([kgp * lo16, kgp * hi16], axis=0))
        a, b = rich_sums(qp, kp, rq_ref[:, cols], rk_ref[:, cols], scales, biases)
        a_ref[slot] = a
        b_ref[slot] = b

    def weights(p, slot):
        widths = widths_of(p)
        for r in range(0, TILE, CH):
            rs = slice(r, r + CH)
            far = sf_ref[slot, rs, :] * (0.125 * LOG2E)
            tops = []
            held = []
            for e in range(2):
                base = 4 * e
                part = [a_ref[slot, rs, base + c : base + c + 1] for c in range(4)]
                line = [b_ref[slot, base + c : base + c + 1, :] for c in range(4)]
                u0 = (part[0] + line[0]) * ox_ref[rs, :]
                u1 = (part[1] + line[1]) * oy_ref[rs, :]
                e0 = jnp.exp2(jnp.minimum(u0, -u0))
                e1 = jnp.exp2(jnp.minimum(u1, -u1))
                r0 = 1.0 / (1.0 + e0)
                r1 = 1.0 / (1.0 + e1)
                gx = (widths[e][0] * dx_ref[rs, :] - part[2]) - line[2]
                gy = (widths[e][1] * dy_ref[rs, :] - part[3]) - line[3]
                s = s_ref[slot, e * TILE + r : e * TILE + r + CH, :] * (0.125 * LOG2E)
                s = s + jnp.minimum(u0, 0.0) + jnp.minimum(u1, 0.0) - gx * gx - gy * gy
                top = jnp.maximum(jnp.maximum(s[:, 0:128], s[:, 128:256]), s[:, 256:384])
                here = low if e == 0 else ~low
                top = jnp.maximum(top, jnp.where(here, far, -3e38))
                tops.append(jnp.max(top, axis=1, keepdims=True))
                g0 = jnp.where(u0 >= 0.0, e0, 1.0) * (ox_ref[rs, :] * r0)
                g1 = jnp.where(u1 >= 0.0, e1, 1.0) * (oy_ref[rs, :] * r1)
                g0_ref[0, 2 * p + e, rs, :] = g0.astype(BF16)
                g1_ref[0, 2 * p + e, rs, :] = g1.astype(BF16)
                held.append((s, r0 * r1))
            pfar = jnp.exp2(far - jnp.where(low, tops[0], tops[1]))
            invs = []
            for e in range(2):
                s, rr = held[e]
                pe = jnp.exp2(s - tops[e]) * rr
                here = low if e == 0 else ~low
                tot = pe[:, 0:128] + pe[:, 128:256] + pe[:, 256:384] + jnp.where(here, pfar, 0.0)
                inv = 1.0 / jnp.sum(tot, axis=1, keepdims=True)
                invs.append(inv)
                pn_ref[0, 2 * p + e, rs, :] = (pe * inv).astype(BF16)
            pf_ref[0, p, rs, :] = (pfar * jnp.where(low, invs[0], invs[1])).astype(BF16)

    def context(p):
        cols = pl.ds(pl.multiple_of(p * 128, 128), 128)
        vp = vp_ref[rows, cols]
        vgp = vg_ref[0, :, cols]
        ctx = mm(pn_ref[0, 2 * p], vp * lo16) + mm(pn_ref[0, 2 * p + 1], vp * hi16)
        ctx = ctx + mm(pf_ref[0, p], jnp.concatenate([vgp * lo16, vgp * hi16], axis=0))
        ctx_ref[:, cols] = ctx.astype(BF16)

    def group(index, carry):
        first = index * UNROLL
        for u in range(UNROLL):
            scores(first + u, u)
        for u in range(UNROLL):
            weights(first + u, u)
        for u in range(UNROLL):
            context(first + u)
        return carry

    lax.fori_loop(0, pairs // UNROLL, group, 0)


def attn_forward(q, k, v, before, after, every_glob, owner, w_qkv, norms, coords, units, lengths, offset, rich):
    rich_query, rich_key, rich_bias, rich_theta = rich
    rows, width = q.shape
    heads = rich_bias.shape[1]
    pairs = heads // 2
    tiles = rows // TILE
    blocks = rows // QBLOCK
    per_block = tiles // blocks
    padded_rows = rows + 2 * RADIUS
    globs = every_glob.shape[0]
    scalars = pl.BlockSpec(memory_space=pltpu.SMEM)

    def whole(*shape):
        return pl.BlockSpec(shape, lambda t: (0,) * len(shape))

    def block3(*shape):
        return pl.BlockSpec((1,) + shape, lambda t: (t // per_block, 0, 0))

    near = pl.BlockSpec((1, heads, TILE, SPAN), lambda t: (t, 0, 0, 0))
    near_shape = jax.ShapeDtypeStruct((tiles, heads, TILE, SPAN), BF16)
    tile_rows = pl.BlockSpec((TILE, width), lambda t: (t, 0))
    return pl.pallas_call(
        partial(fwd_kernel, pairs=pairs, per_block=per_block),
        grid=(tiles,),
        in_specs=[
            scalars, scalars, scalars, scalars, scalars,
            tile_rows, whole(rows, width), whole(rows, width),
            whole(RADIUS, width), whole(RADIUS, width),
            whole(globs, width), whole(1, globs),
            pl.BlockSpec((width, width), lambda t: (0, 1)),
            pl.BlockSpec((width, width), lambda t: (0, 2)),
            whole(*norms.shape),
            whole(*coords.shape), whole(4, width), whole(4, width),
        ],
        out_specs=[
            tile_rows, near,
            pl.BlockSpec((1, pairs, TILE, 128), lambda t: (t, 0, 0, 0)),
            near, near,
            whole(padded_rows, width), whole(padded_rows, width),
            block3(GLOB_FORM, width), block3(GLOB_FORM, width), block3(GLOB_FORM, width),
            block3(GLOB_FORM, width), block3(GLOB_FORM, globs),
        ],
        out_shape=[
            jax.ShapeDtypeStruct((rows, width), BF16),
            near_shape,
            jax.ShapeDtypeStruct((tiles, pairs, TILE, 128), BF16),
            near_shape, near_shape,
            jax.ShapeDtypeStruct((padded_rows, width), BF16),
            jax.ShapeDtypeStruct((padded_rows, width), BF16),
            jax.ShapeDtypeStruct((blocks, GLOB_FORM, width), BF16),
            jax.ShapeDtypeStruct((blocks, GLOB_FORM, width), BF16),
            jax.ShapeDtypeStruct((blocks, GLOB_FORM, width), BF16),
            jax.ShapeDtypeStruct((blocks, GLOB_FORM, width), F32),
            jax.ShapeDtypeStruct((blocks, GLOB_FORM, globs), BF16),
        ],
        scratch_shapes=[
            pltpu.VMEM((TILE, SPAN), F32), pltpu.VMEM((TILE, SPAN), F32),
            pltpu.VMEM((TILE, SPAN), F32), pltpu.VMEM((TILE, SPAN), F32),
            pltpu.VMEM((UNROLL, 2 * TILE, SPAN), F32), pltpu.VMEM((UNROLL, TILE, 128), F32),
            pltpu.VMEM((UNROLL, TILE, 8), F32), pltpu.VMEM((UNROLL, 8, SPAN), F32),
        ],
        compiler_params=pltpu.CompilerParams(vmem_limit_bytes=VMEM_LIMIT),
        cost_estimate=cost(65.0),
        name="attn_forward",
    )(units, lengths, offset, rich_bias, rich_theta, q, k, v, before, after, every_glob, owner,
      w_qkv, w_qkv, norms, coords, rich_query, rich_key)


def bwd_kernel(offset_ref, bias_ref, theta_ref,
               q_ref, dc_ref, ctx_ref, k_ref, v_ref, kg_ref, vg_ref, coords_ref, rq_ref, rk_ref,
               pn_ref, pf_ref, g0_ref, g1_ref,
               dq_ref, dk_ref, dv_ref, dkg_ref, dvg_ref, vec_ref,
               dx_ref, dy_ref, dp_ref, dpf_ref, ds_ref, dsf_ref, a_ref, b_ref, dqr_ref, db_ref, db_now,
               *, pairs, first_pair, tiles, per_block, edge):
    step = pl.program_id(0)
    t = step * (tiles - 1) if edge else step + 1

    @pl.when(step == 0)
    def _():
        vec_ref[...] = jnp.zeros_like(vec_ref)
        if not edge:
            dk_ref[...] = jnp.zeros_like(dk_ref)
            dv_ref[...] = jnp.zeros_like(dv_ref)
            db_ref[...] = jnp.zeros_like(db_ref)

    if edge:
        fresh = step >= 0
    else:
        fresh = (step == 0) | (t % per_block == 0)

    @pl.when(fresh)
    def _():
        dkg_ref[...] = jnp.zeros_like(dkg_ref)
        dvg_ref[...] = jnp.zeros_like(dvg_ref)

    geometry_into(coords_ref, offset_ref[0, 0] // 128 + t - 1, None, (None, None, dx_ref, dy_ref))
    lo16, hi16 = half_masks(BF16)
    low64 = lax.broadcasted_iota(jnp.int32, (64, 128), 1) < 64
    lane8 = lax.broadcasted_iota(jnp.int32, (4, 128), 1)
    lane1 = lax.broadcasted_iota(jnp.int32, (1, 128), 1)
    sub = lax.broadcasted_iota(jnp.int32, (128, 1), 0)
    lo16c = (sub < 64).astype(F32).astype(BF16)
    hi16c = (sub >= 64).astype(F32).astype(BF16)
    rows = pl.ds(pl.multiple_of(t * TILE, TILE), SPAN)
    out_rows = pl.ds(pl.multiple_of((t - 1) * TILE, TILE), SPAN)

    def rich_key_parts(p, cols, sums, keys, columns):
        head = 2 * (p + first_pair)
        squares = [theta_ref[i, head + e] * theta_ref[i, head + e] for e in range(2) for i in range(2)]
        scales = by_row([1.0, 1.0, squares[0], squares[1], 1.0, 1.0, squares[2], squares[3]])
        scaled = sums * scales[:, 0:1]
        vectors = jnp.concatenate(split3(rich_rows(rk_ref[:, cols], None)), axis=0)
        parts = split3(scaled)
        left = jnp.concatenate([vectors[0:8]] * 3 + [vectors[8:16]] * 2 + [vectors[16:24]], axis=0)
        left = jnp.transpose(left).astype(BF16)
        right = jnp.concatenate([parts[0], parts[1], parts[2], parts[0], parts[1], parts[0]], axis=0).astype(BF16)
        extra = mm(left, right)
        stacked = jnp.concatenate(parts, axis=0).astype(BF16)
        key24 = mm(stacked, keys)
        key8 = key24[0:8] + key24[8:16] + key24[16:24]
        vec_ref[p, 4:8, :] += jnp.where(lane8 < 64, key8[0:4], key8[4:8])
        totals = jnp.sum(scaled, axis=1, keepdims=True)
        line = jnp.zeros((1, 128), F32)
        for index in range(8):
            line = jnp.where(lane1 == index, totals[index : index + 1, :], line)
        vec_ref[p, 8:9, :] += line
        return extra

    low_rows = lax.broadcasted_iota(jnp.int32, (BACK_CH, 128), 1) < 64

    def fold(full):
        return jnp.sum(full.reshape(full.shape[0] // 8, 8, full.shape[1]), axis=0)

    def pair_parts(p):
        cols = pl.ds(pl.multiple_of(p * 128, 128), 128)
        head = 2 * (p + first_pair)
        squares = [[theta_ref[i, head + e] * theta_ref[i, head + e] for i in range(2)] for e in range(2)]
        halves = [jnp.where(lane1 < 64, squares[0][i], squares[1][i]) for i in range(2)]
        return cols, head, halves

    def products(p, slot):
        cols, head, _ = pair_parts(p)
        qp = q_ref[:, cols]
        dcp = dc_ref[:, cols]
        kp = k_ref[rows, cols]
        vgp = vg_ref[0, :, cols]
        dp_ref[slot] = mm_nt(jnp.concatenate([dcp * lo16, dcp * hi16], axis=0), v_ref[rows, cols])
        dpf_ref[slot] = mm_nt(dcp, jnp.concatenate([vgp * lo16, vgp * hi16], axis=0))
        biases = by_row([bias_ref[c, head + e] for e in range(2) for c in range(4)])
        a, b = rich_sums(qp, kp, rq_ref[:, cols], rk_ref[:, cols], None, biases)
        a_ref[slot] = a
        b_ref[slot] = b

    def elements(p, slot):
        cols, head, halves = pair_parts(p)
        lines = [rq_ref[0:1, cols], rq_ref[1:2, cols], rq_ref[2:3, cols] * halves[0], rq_ref[3:4, cols] * halves[1]]
        col_sums = [[jnp.zeros((8, SPAN), F32) for _ in range(4)] for _ in range(2)]
        thetas = [[jnp.zeros((8, 128), F32) for _ in range(2)] for _ in range(2)]
        query_sums = [jnp.zeros((8, 128), F32) for _ in range(4)]
        for r in range(0, TILE, BACK_CH):
            rs = slice(r, r + BACK_CH)
            prod = dc_ref[rs, cols].astype(F32) * ctx_ref[rs, cols].astype(F32)
            row_sums = []
            dots = []
            for e in range(2):
                here = low_rows if e == 0 else ~low_rows
                base = 4 * e
                dot = jnp.sum(jnp.where(here, prod, 0.0), axis=1, keepdims=True)
                dots.append(dot)
                es = slice(e * TILE + r, e * TILE + r + BACK_CH)
                ds = pn_ref[0, 2 * p + e, rs, :].astype(F32) * (dp_ref[slot, es, :] - dot)
                ds_ref[slot, es, :] = ds.astype(BF16)
                t0 = ds * g0_ref[0, 2 * p + e, rs, :].astype(F32)
                t1 = ds * g1_ref[0, 2 * p + e, rs, :].astype(F32)
                gx = (dx_ref[rs, :] - a_ref[slot, rs, base + 2 : base + 3]) - b_ref[slot, base + 2 : base + 3, :]
                gy = (dy_ref[rs, :] - a_ref[slot, rs, base + 3 : base + 4]) - b_ref[slot, base + 3 : base + 4, :]
                tx = ds * gx
                ty = ds * gy
                for i, full in enumerate((tx * gx, ty * gy)):
                    thetas[e][i] = thetas[e][i] + fold(full[:, 0:128] + full[:, 128:256] + full[:, 256:384])
                sums = []
                for c, full in enumerate((t0, t1, tx, ty)):
                    col_sums[e][c] = col_sums[e][c] + fold(full)
                    sums.append(jnp.sum(full[:, 0:128] + full[:, 128:256] + full[:, 256:384], axis=1, keepdims=True))
                row_sums.append(sums)
            dsf = pf_ref[0, p, rs, :].astype(F32) * (dpf_ref[slot, rs, :] - jnp.where(low_rows, dots[0], dots[1]))
            dsf_ref[slot, rs, :] = dsf.astype(BF16)
            qf = q_ref[rs, cols].astype(F32)
            dqr = jnp.zeros((BACK_CH, 128), F32)
            for c in range(4):
                da = jnp.where(low_rows, row_sums[0][c], row_sums[1][c])
                dqr = dqr + da * lines[c]
                query_sums[c] = query_sums[c] + fold(da * qf)
            dqr_ref[slot, rs, :] = dqr
        folded = jnp.concatenate([jnp.sum(query_sums[c], axis=0, keepdims=True) for c in range(4)], axis=0)
        scale4 = jnp.concatenate([jnp.ones((2, 128), F32), halves[0], halves[1]], axis=0)
        vec_ref[p, 0:4, :] += folded * scale4
        line = jnp.zeros((1, 128), F32)
        for e in range(2):
            for i in range(2):
                total = jnp.sum(jnp.sum(thetas[e][i], axis=0, keepdims=True), axis=1, keepdims=True)
                line = jnp.where(lane1 == 8 + 2 * e + i, total * (-theta_ref[i, head + e]), line)
        vec_ref[p, 8:9, :] += line
        db_now[slot] = jnp.concatenate([jnp.sum(col_sums[e][c], axis=0, keepdims=True) for e in range(2) for c in range(4)], axis=0)

    def results(p, slot):
        cols, head, _ = pair_parts(p)
        qp = q_ref[:, cols]
        dcp = dc_ref[:, cols]
        kp = k_ref[rows, cols]
        kgp = kg_ref[0, :, cols]
        packed = db_now[slot]
        dq = mm(ds_ref[slot, 0:TILE, :], kp * lo16) + mm(ds_ref[slot, TILE : 2 * TILE, :], kp * hi16)
        dq = dq + mm(dsf_ref[slot], jnp.concatenate([kgp * lo16, kgp * hi16], axis=0))
        dq_ref[:, cols] = (dq * 0.125 + dqr_ref[slot]).astype(BF16)
        qT = jnp.transpose(qp)
        dcT = jnp.transpose(dcp)
        dk = mm(jnp.concatenate([qT * lo16c, qT * hi16c], axis=1), ds_ref[slot]) * 0.125
        dv = mm(dcT * lo16c, pn_ref[0, 2 * p]) + mm(dcT * hi16c, pn_ref[0, 2 * p + 1])
        if edge:
            dk_ref[0, cols, :] = dk + rich_key_parts(p, cols, packed, kp, rows)
            dv_ref[0, cols, :] = dv
        else:
            dk_ref[cols, out_rows] += dk
            dv_ref[cols, out_rows] += dv
            db_ref[p, :, out_rows] += packed
        dkg2 = mm(jnp.transpose(dsf_ref[slot]), qp) * 0.125
        dvg2 = mm(jnp.transpose(pf_ref[0, p]), dcp)
        dkg_ref[0, :, cols] += jnp.where(low64, dkg2[0:64], dkg2[64:128])
        dvg_ref[0, :, cols] += jnp.where(low64, dvg2[0:64], dvg2[64:128])

    def group(index, carry):
        first = index * BACK_UNROLL
        for stage in (products, elements, results):
            for u in range(BACK_UNROLL):
                stage(first + u, u)
        return carry

    lax.fori_loop(0, pairs // BACK_UNROLL, group, 0)

    if not edge:

        @pl.when(step == pl.num_programs(0) - 1)
        def _():
            own = k_ref.shape[0] - 2 * RADIUS

            def finish(p, carry):
                cols = pl.ds(pl.multiple_of(p * 128, 128), 128)
                keys = k_ref[RADIUS : RADIUS + own, cols]
                dk_ref[cols, :] += rich_key_parts(p, cols, db_ref[p], keys, None)
                return carry

            lax.fori_loop(0, pairs, finish, 0)


def attn_backward(q, dctx, ctx, k_pad, v_pad, kg, vg, coords, offset, rich, kept, first_pair, pairs, edge):
    rich_query, rich_key, rich_bias, rich_theta = rich
    rows, width = q.shape
    tiles = rows // TILE
    blocks = kg.shape[0]
    per_block = tiles // blocks
    part = pairs * 128
    half = first_pair // pairs
    steps = 2 if edge else tiles - 2
    padded_rows = k_pad.shape[0]
    scalars = pl.BlockSpec(memory_space=pltpu.SMEM)

    def tile(i):
        return i * (tiles - 1) if edge else i + 1

    tile_rows = pl.BlockSpec((TILE, part), lambda i: (tile(i), half))
    padded_cols = pl.BlockSpec((padded_rows, part), lambda i: (0, half))
    block3 = pl.BlockSpec((1, GLOB_FORM, part), lambda i: (tile(i) // per_block, 0, half))
    out3 = pl.BlockSpec((1, GLOB_FORM, part), lambda i: (tile(i) // per_block, 0, 0))
    vectors = pl.BlockSpec((4, part), lambda i: (0, half))
    near = pl.BlockSpec((1, 2 * pairs, TILE, SPAN), lambda i: (tile(i), half, 0, 0))
    far = pl.BlockSpec((1, pairs, TILE, 128), lambda i: (tile(i), half, 0, 0))
    if edge:
        key_out = pl.BlockSpec((1, part, SPAN), lambda i: (i, 0, 0))
        key_shape = jax.ShapeDtypeStruct((2, part, SPAN), F32)
    else:
        key_out = pl.BlockSpec((part, rows), lambda i: (0, 0))
        key_shape = jax.ShapeDtypeStruct((part, rows), F32)
    glob_shape = jax.ShapeDtypeStruct((blocks, GLOB_FORM, part), F32)
    return pl.pallas_call(
        partial(bwd_kernel, pairs=pairs, first_pair=first_pair, tiles=tiles, per_block=per_block, edge=edge),
        grid=(steps,),
        in_specs=[
            scalars, scalars, scalars,
            tile_rows, tile_rows, tile_rows, padded_cols, padded_cols, block3, block3,
            pl.BlockSpec(coords.shape, lambda i: (0, 0)), vectors, vectors,
            near, far, near, near,
        ],
        out_specs=[
            pl.BlockSpec((TILE, part), lambda i: (i, 0)),
            key_out, key_out, out3, out3,
            pl.BlockSpec((pairs, 16, 128), lambda i: (0, 0, 0)),
        ],
        out_shape=[
            jax.ShapeDtypeStruct((steps * TILE, part), BF16),
            key_shape, key_shape, glob_shape, glob_shape,
            jax.ShapeDtypeStruct((pairs, 16, 128), F32),
        ],
        scratch_shapes=[
            pltpu.VMEM((TILE, SPAN), F32), pltpu.VMEM((TILE, SPAN), F32),
            pltpu.VMEM((BACK_UNROLL, 2 * TILE, SPAN), F32), pltpu.VMEM((BACK_UNROLL, TILE, 128), F32),
            pltpu.VMEM((BACK_UNROLL, 2 * TILE, SPAN), BF16), pltpu.VMEM((BACK_UNROLL, TILE, 128), BF16),
            pltpu.VMEM((BACK_UNROLL, TILE, 8), F32), pltpu.VMEM((BACK_UNROLL, 8, SPAN), F32),
            pltpu.VMEM((BACK_UNROLL, TILE, 128), F32), pltpu.VMEM((pairs, 8, rows), F32),
            pltpu.VMEM((BACK_UNROLL, 8, SPAN), F32),
        ],
        compiler_params=pltpu.CompilerParams(vmem_limit_bytes=VMEM_LIMIT),
        cost_estimate=cost(8.2 * steps * pairs / 6),
        name="attn_backward_edge" if edge else "attn_backward_mid",
    )(offset, rich_bias, rich_theta, q, dctx, ctx, k_pad, v_pad, kg, vg, coords, rich_query, rich_key, *kept)


FF_CHUNK = 512
ROW_CHUNK = 256

TAIL_SLOPE = 0.35
TAIL = (0.0987331438, 0.0987265523, 0.092954664, 0.0773361877, 0.0814717893, -0.00727472285, 0.100604539, -0.0425525649)


def gelu_pair(values):
    t = 1.0 / (1.0 + (TAIL_SLOPE * math.sqrt(0.5)) * jnp.abs(values))
    poly = TAIL[-1] * t + TAIL[-2]
    for coef in TAIL[-3::-1]:
        poly = poly * t + coef
    bell = jnp.exp2((values * values) * (-0.5 * LOG2E))
    tail = t * poly * bell
    phi = jnp.where(values >= 0.0, 1.0 - tail, tail)
    return values * phi, phi + (values * bell) * (1.0 / math.sqrt(2.0 * math.pi))


def ffn_kernel(tok_ref, ctx_ref, ct_ref, wo_ref, wu_ref, wd_ref, norms_ref,
               out_ref, dmid_ref, dctx_ref, wog_ref, wug_ref, wdg_ref, vec_ref,
               mid_ref, h2_ref, h2t_ref, acc_ref, dh_ref, act_ref, dpre_ref, *, rows):
    step = pl.program_id(0)
    last = pl.num_programs(0) - 1

    @pl.when(step == 0)
    def _():
        for r in range(0, rows, ROW_CHUNK):
            rs = slice(r, r + ROW_CHUNK)
            mid = tok_ref[rs, :].astype(F32) + mm(ctx_ref[rs, :], wo_ref[...])
            mid_ref[rs, :] = mid
            normed, _ = norm_parts(mid)
            h2 = (normed * norms_ref[2:3, :] + norms_ref[3:4, :]).astype(BF16)
            h2_ref[rs, :] = h2
            h2t_ref[:, rs] = jnp.transpose(h2)
            acc_ref[rs, :] = jnp.zeros_like(mid)
            dh_ref[rs, :] = jnp.zeros_like(mid)

    def second(rs):
        acc_ref[rs, :] += mm(act_ref[rs, :], wd_ref[...])
        dh_ref[rs, :] += mm_nt(dpre_ref[rs, :], wu_ref[...])

    spans = [slice(r, r + ROW_CHUNK) for r in range(0, rows, ROW_CHUNK)]

    def first(rs):
        return mm(h2_ref[rs, :], wu_ref[...]), mm_nt(ct_ref[rs, :], wd_ref[...])

    ahead = first(spans[0])
    for index, rs in enumerate(spans):
        pre, dact = ahead
        if index + 1 < len(spans):
            ahead = first(spans[index + 1])
        act, slope = gelu_pair(pre)
        act_ref[rs, :] = act.astype(BF16)
        dpre_ref[rs, :] = (dact * slope).astype(BF16)
        if index > 0:
            second(spans[index - 1])
    second(spans[-1])
    wug_ref[...] = mm(h2t_ref[...], dpre_ref[...]).astype(BF16)
    wdg_ref[...] = mm_tn(act_ref[...], ct_ref[...]).astype(BF16)

    @pl.when(step == last)
    def _():
        gains = jnp.zeros((8, norms_ref.shape[1]), F32)
        shifts = jnp.zeros((8, norms_ref.shape[1]), F32)
        for r in range(0, rows, ROW_CHUNK):
            rs = slice(r, r + ROW_CHUNK)
            mid = mid_ref[rs, :]
            out_ref[rs, :] = (mid + acc_ref[rs, :]).astype(BF16)
            normed, scale = norm_parts(mid)
            dh = dh_ref[rs, :]
            gains = gains + jnp.sum((dh * normed).reshape(ROW_CHUNK // 8, 8, -1), axis=0)
            shifts = shifts + jnp.sum(dh.reshape(ROW_CHUNK // 8, 8, -1), axis=0)
            dmid = ct_ref[rs, :].astype(F32) + norm_pull(dh, normed, scale, norms_ref[2:3, :])
            dmid_ref[rs, :] = dmid
            dattn = dmid.astype(BF16)
            h2_ref[rs, :] = dattn
            dctx_ref[rs, :] = mm_nt(dattn, wo_ref[...]).astype(BF16)
        wog_ref[...] = mm_tn(ctx_ref[...], h2_ref[...]).astype(BF16)
        vec_ref[0:1, :] = jnp.sum(gains, axis=0, keepdims=True)
        vec_ref[1:2, :] = jnp.sum(shifts, axis=0, keepdims=True)

def feed_forward(tokens, context, cotangent, w_out, w_up, w_down, norms):
    rows, width = tokens.shape
    hidden = w_up.shape[1]
    steps = hidden // FF_CHUNK
    whole = lambda *shape: pl.BlockSpec(shape, lambda s: (0,) * len(shape))
    return pl.pallas_call(
        partial(ffn_kernel, rows=rows),
        grid=(steps,),
        in_specs=[
            whole(rows, width), whole(rows, width), whole(rows, width), whole(width, width),
            pl.BlockSpec((width, FF_CHUNK), lambda s: (0, s)),
            pl.BlockSpec((FF_CHUNK, width), lambda s: (s, 0)),
            whole(*norms.shape),
        ],
        out_specs=[
            whole(rows, width), whole(rows, width), whole(rows, width), whole(width, width),
            pl.BlockSpec((width, FF_CHUNK), lambda s: (0, s)),
            pl.BlockSpec((FF_CHUNK, width), lambda s: (s, 0)),
            whole(8, width),
        ],
        out_shape=[
            jax.ShapeDtypeStruct((rows, width), BF16),
            jax.ShapeDtypeStruct((rows, width), F32),
            jax.ShapeDtypeStruct((rows, width), BF16),
            jax.ShapeDtypeStruct((width, width), BF16),
            jax.ShapeDtypeStruct((width, hidden), BF16),
            jax.ShapeDtypeStruct((hidden, width), BF16),
            jax.ShapeDtypeStruct((8, width), F32),
        ],
        scratch_shapes=[
            pltpu.VMEM((rows, width), F32), pltpu.VMEM((rows, width), BF16), pltpu.VMEM((width, rows), BF16),
            pltpu.VMEM((rows, width), F32), pltpu.VMEM((rows, width), F32),
            pltpu.VMEM((rows, FF_CHUNK), BF16), pltpu.VMEM((rows, FF_CHUNK), BF16),
        ],
        compiler_params=pltpu.CompilerParams(vmem_limit_bytes=VMEM_LIMIT),
        cost_estimate=cost(60.0),
        name="feed_forward",
    )(tokens, context, cotangent, w_out, w_up, w_down, norms)


def qkv_grad_kernel(ht_ref, hg_ref, dqe_ref, dqm_ref, dke_ref, dve_ref, dkm_ref, dvm_ref, before_ref, after_ref,
                    dkge_ref, dvge_ref, dkgm_ref, dvgm_ref, grad_ref, part_ref, glob_ref, dkt_ref):
    step = pl.program_id(0)
    rows, part = part_ref.shape
    width = ht_ref.shape[0]
    edge = 128

    @pl.when(step == 0)
    def _():
        part_ref[0:edge, :] = dqe_ref[0:edge, :]
        part_ref[edge : rows - edge, :] = dqm_ref[...]
        part_ref[rows - edge : rows, :] = dqe_ref[edge : 2 * edge, :]
        grad_ref[...] = mm(ht_ref[...], part_ref[...]).astype(BF16)

    sources = ((1, dke_ref, dkm_ref, dkge_ref, dkgm_ref), (2, dve_ref, dvm_ref, dvge_ref, dvgm_ref))
    for index, edge_ref, mid_ref, edge_glob, mid_glob in sources:

        @pl.when(step == index)
        def _():
            dkt_ref[...] = mid_ref[...].astype(BF16)
            dkt_ref[:, 0:128] = (mid_ref[:, 0:128] + edge_ref[0, :, 128:256] + before_ref[index - 1].astype(F32)).astype(BF16)
            dkt_ref[:, 128:256] = (mid_ref[:, 128:256] + edge_ref[0, :, 256:384]).astype(BF16)
            dkt_ref[:, rows - 256 : rows - 128] = (mid_ref[:, rows - 256 : rows - 128] + edge_ref[1, :, 0:128]).astype(BF16)
            dkt_ref[:, rows - 128 : rows] = (
                mid_ref[:, rows - 128 : rows] + edge_ref[1, :, 128:256] + after_ref[index - 1].astype(F32)
            ).astype(BF16)
            part_ref[...] = jnp.transpose(dkt_ref[...])
            glob = (edge_glob[...] + mid_glob[...]).reshape(-1, part).astype(BF16)
            glob_ref[...] = glob
            hg = hg_ref[...].reshape(-1, width)
            grad_ref[...] = (mm(ht_ref[...], part_ref[...]) + mm_tn(hg, glob)).astype(BF16)


def qkv_grad(hidden_t, hg, dq, dk, dv, rims, dkg, dvg, half, pairs):
    width, rows = hidden_t.shape
    part = pairs * 128
    blocks = hg.shape[0]

    def whole(*shape):
        return pl.BlockSpec(shape, lambda i: (0,) * len(shape))

    edge_keys = pl.BlockSpec((2, part, SPAN), lambda i: (0, half, 0))
    edge_glob = pl.BlockSpec((blocks, GLOB_FORM, part), lambda i: (0, 0, half))
    rim = pl.BlockSpec((2, part, RADIUS), lambda i: (0, half, 0))
    mid_glob = whole(blocks, GLOB_FORM, part)
    return pl.pallas_call(
        qkv_grad_kernel,
        grid=(3,),
        in_specs=[
            whole(width, rows), whole(blocks, GLOB_FORM, width),
            pl.BlockSpec((2 * TILE, part), lambda i: (0, half)), whole(rows - 2 * TILE, part),
            edge_keys, edge_keys, whole(part, rows), whole(part, rows), rim, rim,
            edge_glob, edge_glob, mid_glob, mid_glob,
        ],
        out_specs=[
            pl.BlockSpec((width, part), lambda i: (0, i)),
            pl.BlockSpec((rows, part), lambda i: (0, i)),
            pl.BlockSpec((blocks * GLOB_FORM, part), lambda i: (0, jnp.maximum(i - 1, 0))),
        ],
        out_shape=[
            jax.ShapeDtypeStruct((width, 3 * part), BF16),
            jax.ShapeDtypeStruct((rows, 3 * part), BF16),
            jax.ShapeDtypeStruct((blocks * GLOB_FORM, 2 * part), BF16),
        ],
        scratch_shapes=[pltpu.VMEM((part, rows), BF16)],
        compiler_params=pltpu.CompilerParams(vmem_limit_bytes=VMEM_LIMIT),
        cost_estimate=cost(20.0),
        name="qkv_grad",
    )(hidden_t, hg, dq[0], dq[1], dk[0], dv[0], dk[1], dv[1], rims[0], rims[1], dkg[0], dvg[0], dkg[1], dvg[1])


def token_grad_kernel(pa_ref, pb_ref, tok_ref, dmid_ref, w_ref, norms_ref, ga_ref, gb_ref, oh_ref, ng_ref, second_ref,
                      ve_ref, va_ref, vb_ref, tg_ref, gp_ref, vec_ref, both_ref, gains_ref, shifts_ref, *, pairs, kept):
    step = pl.program_id(0)
    width = tok_ref.shape[1]
    part = pairs * 128

    @pl.when(step == 0)
    def _():
        gains_ref[...] = jnp.zeros_like(gains_ref)
        shifts_ref[...] = jnp.zeros_like(shifts_ref)

    for index in range(3):
        both_ref[:, index * width : index * width + part] = pa_ref[:, index * part : (index + 1) * part]
        both_ref[:, index * width + part : (index + 1) * width] = pb_ref[:, index * part : (index + 1) * part]
    dh = mm_nt(both_ref[...], w_ref[...])
    normed, scale = norm_parts(tok_ref[...].astype(F32))
    count = dh.shape[0] // 8
    gains_ref[...] += jnp.sum((dh * normed).reshape(count, 8, width), axis=0)
    shifts_ref[...] += jnp.sum(dh.reshape(count, 8, width), axis=0)
    tg_ref[...] = (dmid_ref[...] + norm_pull(dh, normed, scale, norms_ref[0:1, :])).astype(BF16)

    @pl.when(step == pl.num_programs(0) - 1)
    def _():
        dhg = jnp.zeros((ga_ref.shape[0], width), F32)
        for index in range(2):
            for half, ref in ((0, ga_ref), (1, gb_ref)):
                start = (index + 1) * width + half * part
                dhg = dhg + mm_nt(ref[:, index * part : (index + 1) * part], w_ref[:, start : start + part])
        glob_normed = ng_ref[...].reshape(-1, width)
        rows_all = [
            jnp.sum(gains_ref[...], axis=0, keepdims=True) + jnp.sum(dhg * glob_normed, axis=0, keepdims=True),
            jnp.sum(shifts_ref[...], axis=0, keepdims=True) + jnp.sum(dhg, axis=0, keepdims=True),
        ]
        vec_ref[0:1, :] = rows_all[0]
        vec_ref[1:2, :] = rows_all[1]
        vec_ref[2:4, :] = second_ref[0:2, :]
        gp_ref[...] = mm_tn(oh_ref[...].reshape(-1, oh_ref.shape[2]), dhg.astype(BF16)).astype(BF16)
        lines = []
        for p in range(2 * pairs):
            mid = va_ref[p] if p < pairs else vb_ref[p - pairs]
            both = ve_ref[p] + mid
            vec_ref[4:12, p * 128 : p * 128 + 128] = both[0:8]
            lines.append(both[8:9])
        lines.append(jnp.zeros((8 - len(lines), 128), F32))
        lines = jnp.concatenate(split3(jnp.concatenate(lines, axis=0)), axis=0).astype(BF16)
        spot = lax.broadcasted_iota(jnp.int32, (128, width), 0)
        lane = lax.broadcasted_iota(jnp.int32, (128, width), 1)
        spread = mm(lines, (lax.rem(lane, kept) == spot).astype(F32).astype(BF16))
        vec_ref[12:20, :] = spread[0:8] + spread[8:16] + spread[16:24]
        vec_ref[20:24, :] = jnp.zeros((4, width), F32)


def token_grad(parts, globs, tokens, grad_middle, w_qkv, norms, picked, glob_normed, second_sums, vecs, pairs, kept):
    rows, width = tokens.shape
    step = 256
    count = picked.shape[2]

    def whole(*shape):
        return pl.BlockSpec(shape, lambda i: (0,) * len(shape))

    def block(columns):
        return pl.BlockSpec((step, columns), lambda i: (i, 0))

    return pl.pallas_call(
        partial(token_grad_kernel, pairs=pairs, kept=kept),
        grid=(rows // step,),
        in_specs=[
            block(parts[0].shape[1]), block(parts[1].shape[1]), block(width), block(width), whole(*w_qkv.shape),
            whole(*norms.shape), whole(*globs[0].shape), whole(*globs[1].shape), whole(*picked.shape),
            whole(*glob_normed.shape), whole(*second_sums.shape),
        ] + [whole(*v.shape) for v in vecs],
        out_specs=[block(width), whole(count, width), whole(24, width)],
        out_shape=[
            jax.ShapeDtypeStruct((rows, width), BF16),
            jax.ShapeDtypeStruct((count, width), BF16),
            jax.ShapeDtypeStruct((24, width), F32),
        ],
        scratch_shapes=[pltpu.VMEM((step, 3 * width), BF16), pltpu.VMEM((8, width), F32), pltpu.VMEM((8, width), F32)],
        compiler_params=pltpu.CompilerParams(vmem_limit_bytes=VMEM_LIMIT),
        cost_estimate=cost(40.0),
        name="token_grad",
    )(*parts, tokens, grad_middle, w_qkv, norms, *globs, picked, glob_normed, second_sums, *vecs)


def swap_on(axis, mask):
    return [(i, i ^ mask) for i in range(lax.axis_size(axis))]


def add_low(kept, received):
    return (kept.astype(F32) + received.astype(F32)).astype(BF16)


def core_halves(grads, place):
    count = lax.axis_size("seq")
    view = grads.reshape(count // 2, 2, grads.shape[0] // count, grads.shape[1])
    send = lax.dynamic_index_in_dim(view, 1 - place % 2, 1, keepdims=False)
    kept = lax.dynamic_index_in_dim(view, place % 2, 1, keepdims=False)
    return kept, send


def core_swap(send):
    return lax.ppermute(send, "seq", swap_on("seq", 1))


def stream_blocks(summed, group_count):
    outer, rows, columns = summed.shape
    return jnp.moveaxis(summed.reshape(outer, group_count, rows // group_count, columns), 1, 0)


def halve_step(blocks, axis, place, bit, width):
    mine = (place >> bit) & 1
    send = lax.dynamic_index_in_dim(blocks, 1 - mine, width, keepdims=False)
    kept = lax.dynamic_index_in_dim(blocks, mine, width, keepdims=False)
    return kept, lax.ppermute(send, axis, swap_on(axis, 1 << bit))


def exchange_parts(blocks, axis, place, stride):
    parts = [lax.dynamic_index_in_dim(blocks, place, 0, keepdims=False)]
    for step in range(1, blocks.shape[0]):
        send = lax.dynamic_index_in_dim(blocks, place ^ step, 0, keepdims=False)
        parts.append(lax.ppermute(send, axis, swap_on(axis, step * stride)))
    return parts


def summed_low(parts):
    total = parts[0].astype(F32)
    for part in parts[1:]:
        total = total + part.astype(F32)
    return total.astype(BF16)


def gather_rows(rows, axis, place, bit):
    other = lax.ppermute(rows, axis, swap_on(axis, bit))
    upper = (place & bit) > 0
    return jnp.concatenate([jnp.where(upper, other, rows), jnp.where(upper, rows, other)], axis=0)


def gather_blocks(rows, axis, place, stride):
    count = lax.axis_size(axis) // stride
    every = [rows] + [lax.ppermute(rows, axis, swap_on(axis, step * stride)) for step in range(1, count)]
    return ordered(jnp.stack(every), place).reshape(count * rows.shape[0], rows.shape[1])


def ordered(stacked, place):
    count = stacked.shape[0]
    rest = stacked.shape[1:]
    bit = 1
    while bit < count:
        view = stacked.reshape((count // (2 * bit), 2, bit) + rest)
        stacked = jnp.where((place & bit) > 0, view[:, ::-1], view).reshape((count,) + rest)
        bit *= 2
    return stacked


def tied(*values):
    return lax.optimization_barrier(values)


def flat_rows(array, width):
    rows, columns = array.shape
    if columns % width == 0:
        return jnp.concatenate([array[:, i : i + width] for i in range(0, columns, width)], axis=0)
    return array.reshape(-1, width)


def flat_blocks(array, width):
    count, columns = array.shape[0], array.shape[-1]
    array = array.reshape(count, -1, columns)
    if columns % width == 0:
        return jnp.concatenate([array[:, :, i : i + width] for i in range(0, columns, width)], axis=1)
    return array.reshape(count, -1, width)


def unflat_rows(stacked, rows, columns):
    count, width = stacked.shape[0], stacked.shape[2]
    if columns % width == 0:
        return jnp.concatenate([stacked[:, i * rows : (i + 1) * rows] for i in range(columns // width)], axis=2)
    return stacked.reshape(count, rows, columns)


def pad_rows(blocks, width):
    count = blocks.shape[0]
    flat = blocks.reshape(count, -1)
    size = -(-flat.shape[1] // (16 * width)) * 16 * width
    return jnp.pad(flat, ((0, 0), (0, size - flat.shape[1]))).reshape(count, -1, width)


def exchange_raw(piece, axis):
    count = lax.axis_size(axis)
    return [piece] + [lax.ppermute(piece, axis, swap_on(axis, step)) for step in range(1, count)]


def body(
    tokens,
    global_states,
    cotangent,
    w_qkv,
    w_out,
    w_up,
    w_down,
    first_gain,
    first_shift,
    second_gain,
    second_shift,
    rich_query,
    rich_key,
    rich_bias,
    rich_theta,
    bucket_units,
    form_lengths,
    coords,
    glob_owner,
):
    row_count = tokens.shape[1]
    model_width = tokens.shape[2]
    place = lax.axis_index("seq")
    group = lax.axis_index("stream")
    seq_count = lax.axis_size("seq")
    group_count = lax.axis_size("stream")
    rich = (rich_query, rich_key, rich_bias, rich_theta)
    offset = (place * row_count).astype(jnp.int32).reshape(1, 1)
    norms = jnp.stack([first_gain, first_shift, second_gain, second_shift])
    up = [(i, i + 1) for i in range(seq_count - 1)]
    down = [(i + 1, i) for i in range(seq_count - 1)]
    pairs = rich_bias.shape[1] // 2
    half_pairs = pairs // 2
    kept_rows = model_width // seq_count

    before = lax.ppermute(tokens[0, row_count - RADIUS :], "seq", up)
    after = lax.ppermute(tokens[0, :RADIUS], "seq", down)
    pair_glob = gather_rows(global_states[0], "seq", place, 1)
    pair_glob, norms, before, after = tied(pair_glob, norms, before, after)
    every_glob = gather_blocks(pair_glob, "seq", place // 2, 2)
    queries, keys, values, hidden_t = project_tokens(tokens[0], w_qkv, norms)
    (context, pn, pf, g0, g1, key_pad, value_pad, glob_keys, glob_values, glob_hidden, glob_normed, picked) = attn_forward(
        queries, keys, values, before, after, every_glob, glob_owner, w_qkv, norms,
        coords[0], bucket_units, form_lengths, offset, rich,
    )
    layer_out, grad_middle, grad_context, grad_w_out, grad_w_up, grad_w_down, second_sums = feed_forward(
        tokens[0], context, cotangent[0], w_out, w_up, w_down, norms
    )

    def attention_back(first_pair, count, edge, grad_context):
        return attn_backward(
            queries, grad_context, context, key_pad, value_pad, glob_keys, glob_values, coords[0], offset, rich,
            (pn, pf, g0, g1), first_pair, count, edge,
        )

    halves = [core_halves(grad, place) for grad in (grad_w_up, grad_w_down, grad_w_out)]
    sends = [half[1] for half in halves]
    grad_context, *sends = tied(grad_context, *sends)
    halves = [(half[0], core_swap(send)) for half, send in zip(halves, sends)]
    dq_e, dk_e, dv_e, dkg_e, dvg_e, vec_e = attention_back(0, pairs, True, grad_context)
    to_before = jnp.stack([dk_e[0, :, :RADIUS], dv_e[0, :, :RADIUS]]).astype(BF16)
    to_after = jnp.stack([dk_e[1, :, 2 * RADIUS :], dv_e[1, :, 2 * RADIUS :]]).astype(BF16)
    rims = (lax.ppermute(to_after, "seq", up), lax.ppermute(to_before, "seq", down))

    (dq_e, *swapped) = tied(dq_e, *[half[1] for half in halves])
    halves = [(half[0], received) for half, received in zip(halves, swapped)]

    sums = [add_low(*half) for half in halves]
    outer = seq_count // 2
    bits = group_count.bit_length() - 1
    pieces = [
        jnp.moveaxis(sums[0].reshape(outer, kept_rows, group_count, -1), 2, 0).reshape(group_count, outer, -1, model_width),
        jnp.moveaxis(sums[1].reshape(outer, group_count, -1, model_width), 1, 0),
        jnp.moveaxis(sums[2].reshape(outer, group_count, -1, model_width), 1, 0),
    ]
    piece_rows = [piece.shape[2] for piece in pieces]
    early = jnp.concatenate(pieces, axis=2).reshape((2,) * bits + (outer, sum(piece_rows), model_width))
    columns = model_width // 2
    early_x, early_y = early[..., :columns], early[..., columns:]
    order_x = list(range(bits))
    order_y = order_x[1:] + order_x[:1]

    def halved(blocks, order, done):
        bit = order[done]
        rest = sorted(order[done:], reverse=True)
        return halve_step(blocks, "stream", group, bit, rest.index(bit))

    early_x, early_y, grad_context, *rims = tied(early_x, early_y, grad_context, *rims)
    (keep_x, got_x), (keep_y, got_y) = halved(early_x, order_x, 0), halved(early_y, order_y, 0)
    dq_a, dk_a, dv_a, dkg_a, dvg_a, vec_a = attention_back(0, half_pairs, False, grad_context)
    grads_a, part_a, glob_a = qkv_grad(
        hidden_t, glob_hidden, (dq_e, dq_a), (dk_e, dk_a), (dv_e, dv_a), rims, (dkg_e, dkg_a), (dvg_e, dvg_a), 0, half_pairs
    )
    got_x, got_y, grads_a = tied(got_x, got_y, grads_a)
    early_x, early_y = add_low(keep_x, got_x), add_low(keep_y, got_y)
    kept_a, send_a = core_halves(grads_a, place)
    split = (2,) * bits + (outer, kept_rows // group_count, -1)
    late_a = stream_blocks(add_low(kept_a, core_swap(send_a)), group_count).reshape(split)
    early_x, early_y, late_a, grad_context = tied(early_x, early_y, late_a, grad_context)
    for done in range(1, bits):
        (keep_x, got_x), (keep_y, got_y) = halved(early_x, order_x, done), halved(early_y, order_y, done)
        early_x, early_y = (keep_x, got_x), (keep_y, got_y)
        if done + 1 < bits:
            early_x, early_y = add_low(*early_x), add_low(*early_y)
    keep_a, got_a = halved(late_a, order_x, 0)
    dq_b, dk_b, dv_b, dkg_b, dvg_b, vec_b = attention_back(half_pairs, half_pairs, False, grad_context)
    got_x, got_y, got_a, dq_b = tied(early_x[1], early_y[1], got_a, dq_b)
    early = jnp.concatenate([add_low(early_x[0], got_x), add_low(early_y[0], got_y)], axis=-1)
    late_a = add_low(keep_a, got_a)
    early, late_a, dq_b = tied(early, late_a, dq_b)
    early = exchange_parts(early, "seq", place // 2, 2)
    for done in range(1, bits):
        late_a = halved(late_a, order_x, done)
        if done + 1 < bits:
            late_a = add_low(*late_a)
    grads_b, part_b, glob_b = qkv_grad(
        hidden_t, glob_hidden, (dq_e, dq_b), (dk_e, dk_b), (dv_e, dv_b), rims, (dkg_e, dkg_b), (dvg_e, dvg_b), 1, half_pairs
    )
    kept_b, send_b = core_halves(grads_b, place)
    got_a, got_b = tied(late_a[1], core_swap(send_b))
    late_a = add_low(late_a[0], got_a)
    late_b = stream_blocks(add_low(kept_b, got_b), group_count).reshape(split)
    late_a, late_b, part_b = tied(late_a, late_b, part_b)
    keep_b, got_b = halved(late_b, order_x, 0)
    tokens_grad, glob_part, vectors = token_grad(
        (part_a, part_b), (glob_a, glob_b), tokens[0], grad_middle, w_qkv, norms, picked, glob_normed, second_sums,
        (vec_e, vec_a, vec_b), half_pairs, kept_rows,
    )
    got_b, glob_part, *received = tied(got_b, glob_part, *early[1:])
    early = summed_low([early[0]] + received)
    late_b = add_low(keep_b, got_b)
    for done in range(1, bits):
        late_b = add_low(*halved(late_b, order_x, done))
    gathered = exchange_raw(early, "stream")
    vec_rows = jnp.moveaxis(vectors.reshape(24, outer, 2 * kept_rows), 1, 0).astype(BF16)
    vec_flat = pad_rows(vec_rows, model_width)
    glob_blocks = glob_part.reshape(outer, -1, model_width)
    late = jnp.concatenate([late_a, late_b], axis=2)
    columns = late.shape[2]
    late_flat = flat_blocks(late, model_width)
    counts = [late_flat.shape[1], glob_blocks.shape[1], vec_flat.shape[1]]
    summed = exchange_parts(jnp.concatenate([late_flat, glob_blocks, vec_flat], axis=1), "seq", place // 2, 2)
    summed = tied(*summed, *gathered)
    gathered = ordered(jnp.stack(summed[outer:]), group)
    summed = summed_low(summed[:outer])
    late_piece = summed[: counts[0]]
    glob_piece = summed[counts[0] : counts[0] + counts[1]].reshape(2, -1, model_width)
    vec_piece = summed[counts[0] + counts[1] :]
    glob_send = lax.dynamic_index_in_dim(glob_piece, 1 - place % 2, 0, keepdims=False)
    glob_kept = lax.dynamic_index_in_dim(glob_piece, place % 2, 0, keepdims=False)
    every = exchange_raw(jnp.concatenate([late_piece, vec_piece], axis=0), "stream")
    glob_got = core_swap(glob_send)
    vec_sum = sum(rows[counts[0] :].astype(F32) for rows in every)
    vec_sum = vec_sum.reshape(-1)[: 24 * 2 * kept_rows].reshape(24, 2, kept_rows)
    vec_send = lax.dynamic_index_in_dim(vec_sum, 1 - place % 2, 1, keepdims=False)
    vec_own = lax.dynamic_index_in_dim(vec_sum, place % 2, 1, keepdims=False) + core_swap(vec_send)
    late = ordered(jnp.stack([rows[: counts[0]] for rows in every]), group)
    late = unflat_rows(late, kept_rows // group_count, columns).reshape(kept_rows, columns).astype(F32)
    grad_glob = glob_kept.astype(F32) + glob_got.astype(F32)
    own_glob, own_scale = norm_parts(global_states[0].astype(F32))
    glob_grad = norm_pull(grad_glob, own_glob, own_scale, first_gain).astype(BF16)

    part = half_pairs * 128
    share_qkv = jnp.concatenate(
        [late[:, (half * 3 + i) * part : (half * 3 + i + 1) * part] for i in range(3) for half in range(2)], axis=1
    )
    early = gathered.astype(F32)
    cuts = [0, piece_rows[0], piece_rows[0] + piece_rows[1], sum(piece_rows)]
    share_up = jnp.moveaxis(early[:, : cuts[1]].reshape(group_count, kept_rows, -1), 0, 1).reshape(kept_rows, -1)
    share_down = early[:, cuts[1] : cuts[2]].reshape(-1, model_width)
    share_out = early[:, cuts[2] :].reshape(-1, model_width)
    own_vectors = vec_own[:12]
    heads = vec_own[12 : 12 + pairs, :12]
    bias_grad = heads[:, :8].reshape(pairs, 2, 4).transpose(2, 0, 1).reshape(rich_bias.shape)
    theta_grad = heads[:, 8:].reshape(pairs, 2, 2).transpose(2, 0, 1).reshape(rich_theta.shape)
    return (
        layer_out[None],
        tokens_grad[None],
        glob_grad[None],
        share_qkv,
        share_out,
        share_up,
        share_down,
        own_vectors[0],
        own_vectors[1],
        own_vectors[2],
        own_vectors[3],
        own_vectors[4:8],
        own_vectors[8:12],
        bias_grad,
        theta_grad,
    )


def solution(mesh):
    return jax.shard_map(
        body,
        mesh=mesh,
        in_specs=(
            P("stream", "seq", None),
            P("stream", "seq", None),
            P("stream", "seq", None),
            P(),
            P(),
            P(),
            P(),
            P(),
            P(),
            P(),
            P(),
            P(),
            P(),
            P(),
            P(),
            P("stream", None),
            P("stream", None),
            P("stream", None, None),
            P("stream", None),
        ),
        out_specs=(
            P("stream", "seq", None),
            P("stream", "seq", None),
            P("stream", "seq", None),
            P("seq", None),
            P("seq", None),
            P("seq", None),
            P("seq", None),
            P("seq"),
            P("seq"),
            P("seq"),
            P("seq"),
            P(None, "seq"),
            P(None, "seq"),
            P(),
            P(),
        ),
        check_vma=False,
    )
```

```python
from functools import partial
import math

import jax
import jax.numpy as jnp
from jax import lax
from jax.experimental import pallas as pl
from jax.experimental.pallas import tpu as pltpu
from jax.sharding import PartitionSpec as P

RADIUS = 128
GLOB_FORM = 64
QBLOCK = 512
TOK_DEV = 1024


EPSILON = 1e-06


TILE = 128
SPAN = 384
LOG2E = math.log2(math.e)
FAR_AWAY = 1e15
CH = 128
UNROLL = 6
BACK_CH = 128
BACK_UNROLL = 3
F32 = jnp.float32
BF16 = jnp.bfloat16
VMEM_LIMIT = 58 * 1024 * 1024


def mm(a, b):
    return lax.dot_general(a, b, (((1,), (0,)), ((), ())), preferred_element_type=F32)


def mm_nt(a, b):
    return lax.dot_general(a, b, (((1,), (1,)), ((), ())), preferred_element_type=F32)


def mm_tn(a, b):
    return lax.dot_general(a, b, (((0,), (0,)), ((), ())), preferred_element_type=F32)


def norm_parts(values):
    centre = jnp.mean(values, axis=-1, keepdims=True)
    centred = values - centre
    spread = jnp.mean(centred * centred, axis=-1, keepdims=True)
    scale = lax.rsqrt(spread + EPSILON)
    return centred * scale, scale


def norm_pull(grad, normed, scale, gain):
    e = grad * gain
    mean_e = jnp.mean(e, axis=-1, keepdims=True)
    mean_en = jnp.mean(e * normed, axis=-1, keepdims=True)
    return scale * (e - mean_e - normed * mean_en)


def split3(values):
    hi = values.astype(BF16).astype(F32)
    rest = values - hi
    mid = rest.astype(BF16).astype(F32)
    return hi, mid, rest - mid


def half_masks(dtype):
    lane = lax.broadcasted_iota(jnp.int32, (1, 128), 1)
    low = (lane < 64).astype(F32)
    return low.astype(dtype), (1.0 - low).astype(dtype)


def by_row(values):
    row = lax.broadcasted_iota(jnp.int32, (8, 128), 0)
    out = jnp.full((8, 128), values[7], F32)
    for index in range(7):
        out = jnp.where(row == index, values[index], out)
    return out


def rich_rows(vectors, scales):
    row = lax.broadcasted_iota(jnp.int32, (8, 128), 0)
    lane = lax.broadcasted_iota(jnp.int32, (8, 128), 1)
    both = jnp.concatenate([vectors, vectors], axis=0)
    both = both if scales is None else both * scales
    return jnp.where((row < 4) == (lane < 64), both, 0.0)


def rich_sums(qp, kp, query_vec, key_vec, scales, bias8):
    rq = jnp.concatenate(split3(rich_rows(query_vec, scales)), axis=1).astype(BF16)
    rk = jnp.concatenate(split3(rich_rows(key_vec, scales)), axis=0).astype(BF16)
    a = mm_nt(jnp.concatenate([qp, qp, qp], axis=1), rq)
    b24 = mm_nt(rk, kp)
    return a, b24[0:8] + b24[8:16] + b24[16:24] + bias8[:, 0:1]


def form_of(units_ref, lengths_ref, row):
    form, low, high, before = 0, 0, lengths_ref[0, 0], 0
    for index in range(1, units_ref.shape[1]):
        before = before + units_ref[0, index - 1]
        start = TOK_DEV // 2 + TOK_DEV * before
        taken = row >= start
        form = jnp.where(taken, index, form)
        low = jnp.where(taken, start, low)
        high = jnp.where(taken, start + lengths_ref[0, index], high)
    return form, low, high


def coord_row(coords_ref, axis, tile_index):
    tile_index = jnp.clip(tile_index, 0, coords_ref.shape[1] // 128 - 1)
    return coords_ref[axis : axis + 1, pl.ds(pl.multiple_of(tile_index * 128, 128), 128)].astype(F32)


def query_columns(coords_ref, axis, tile_index):
    return jnp.transpose(jnp.broadcast_to(coord_row(coords_ref, axis, tile_index), (128, 128)))


def geometry_into(coords_ref, first_tile, span, refs):
    ox_ref, oy_ref, dx_ref, dy_ref = refs
    xq = query_columns(coords_ref, 0, first_tile + 1)
    yq = query_columns(coords_ref, 1, first_tile + 1)
    for lt in range(3):
        xk = coord_row(coords_ref, 0, first_tile + lt)
        yk = coord_row(coords_ref, 1, first_tile + lt)
        out = (slice(None), slice(lt * 128, lt * 128 + 128))
        dx = jnp.log(1.0 + jnp.abs(xq - xk))
        dy = jnp.log(1.0 + jnp.abs(yq - yk))
        if span is not None:
            row = lax.broadcasted_iota(jnp.int32, (128, 128), 0)
            col = lax.broadcasted_iota(jnp.int32, (128, 128), 1) + lt * 128
            near = (col >= row) & (col - row <= 2 * RADIUS)
            dx = jnp.where(near & (col >= span[0]) & (col < span[1]), dx, FAR_AWAY)
            ox_ref[out] = jnp.where(xk > xq, 1.0, -1.0)
            oy_ref[out] = jnp.where(yk > yq, 1.0, -1.0)
        dx_ref[out] = dx
        dy_ref[out] = dy


def qkv_kernel(tok_ref, w_ref, norms_ref, q_ref, k_ref, v_ref, ht_ref):
    width = tok_ref.shape[1]
    normed, _ = norm_parts(tok_ref[...].astype(F32))
    hidden = (normed * norms_ref[0:1, :] + norms_ref[1:2, :]).astype(BF16)
    for index, out in enumerate((q_ref, k_ref, v_ref)):
        out[...] = mm(hidden, w_ref[:, index * width : (index + 1) * width]).astype(BF16)
    ht_ref[...] = jnp.transpose(hidden)


def project_tokens(tokens, w_qkv, norms):
    rows, width = tokens.shape
    step = 256
    block = pl.BlockSpec((step, width), lambda i: (i, 0))
    return pl.pallas_call(
        qkv_kernel,
        grid=(rows // step,),
        in_specs=[block, pl.BlockSpec(w_qkv.shape, lambda i: (0, 0)), pl.BlockSpec(norms.shape, lambda i: (0, 0))],
        out_specs=[block, block, block, pl.BlockSpec((width, step), lambda i: (0, i))],
        out_shape=[jax.ShapeDtypeStruct((rows, width), BF16)] * 3 + [jax.ShapeDtypeStruct((width, rows), BF16)],
        compiler_params=pltpu.CompilerParams(vmem_limit_bytes=VMEM_LIMIT),
        cost_estimate=cost(8.0),
        name="project_tokens",
    )(tokens, w_qkv, norms)


def cost(micros):
    return pl.CostEstimate(flops=int(micros * 1e9), bytes_accessed=0, transcendentals=0)


def global_pairs(form, owner_ref, glob_ref, norms_ref, kw_ref, vw_ref, kg_ref, vg_ref, hg_ref, ng_ref, oh_ref):
    count = glob_ref.shape[0]
    match = (owner_ref[...] == form).astype(F32)
    row = lax.broadcasted_iota(jnp.int32, (count, count), 0)
    col = lax.broadcasted_iota(jnp.int32, (count, count), 1)
    upto = (row <= col).astype(F32).astype(BF16)
    rank = mm(jnp.broadcast_to(match, (16, count)).astype(BF16), upto)[0:1]
    slot = lax.broadcasted_iota(jnp.int32, (GLOB_FORM, count), 0).astype(F32) + 1.0
    picked = jnp.where(rank == slot, match, 0.0).astype(BF16)
    oh_ref[0] = picked
    normed, _ = norm_parts(mm(picked, glob_ref[...]))
    ng_ref[0] = normed
    hidden = (normed * norms_ref[0:1, :] + norms_ref[1:2, :]).astype(BF16)
    hg_ref[0] = hidden
    kg_ref[0] = mm(hidden, kw_ref[...]).astype(BF16)
    vg_ref[0] = mm(hidden, vw_ref[...]).astype(BF16)


def fwd_kernel(units_ref, lengths_ref, offset_ref, bias_ref, theta_ref,
               q_ref, k_ref, v_ref, before_ref, after_ref, glob_ref, owner_ref, kw_ref, vw_ref, norms_ref,
               coords_ref, rq_ref, rk_ref,
               ctx_ref, pn_ref, pf_ref, g0_ref, g1_ref, kp_ref, vp_ref, kg_ref, vg_ref, hg_ref, ng_ref, oh_ref,
               ox_ref, oy_ref, dx_ref, dy_ref, s_ref, sf_ref, a_ref, b_ref, *, pairs, per_block):
    t = pl.program_id(0)
    rows_all = k_ref.shape[0]
    offset = offset_ref[0, 0]
    first = offset + t * TILE
    form, low_end, high_end = form_of(units_ref, lengths_ref, first)

    @pl.when(t == 0)
    def _():
        for refs in ((k_ref, kp_ref, kw_ref), (v_ref, vp_ref, vw_ref)):
            own, padded_ref, weight = refs
            padded_ref[RADIUS : RADIUS + rows_all, :] = own[...]
        for halo, start in ((before_ref, 0), (after_ref, RADIUS + rows_all)):
            normed, _ = norm_parts(halo[...].astype(F32))
            hidden = (normed * norms_ref[0:1, :] + norms_ref[1:2, :]).astype(BF16)
            kp_ref[start : start + RADIUS, :] = mm(hidden, kw_ref[...]).astype(BF16)
            vp_ref[start : start + RADIUS, :] = mm(hidden, vw_ref[...]).astype(BF16)

    @pl.when(t % per_block == 0)
    def _():
        global_pairs(form, owner_ref, glob_ref, norms_ref, kw_ref, vw_ref, kg_ref, vg_ref, hg_ref, ng_ref, oh_ref)

    shifted = first - RADIUS
    geometry_into(coords_ref, offset // 128 + t - 1, (low_end - shifted, high_end - shifted), (ox_ref, oy_ref, dx_ref, dy_ref))
    lo16, hi16 = half_masks(BF16)
    lane = lax.broadcasted_iota(jnp.int32, (CH, 128), 1)
    low = lane < 64
    rows = pl.ds(pl.multiple_of(t * TILE, TILE), SPAN)
    root = math.sqrt(0.5 * LOG2E)

    def widths_of(p):
        return [[theta_ref[i, 2 * p + e] * root for i in range(2)] for e in range(2)]

    def scores(p, slot):
        cols = pl.ds(pl.multiple_of(p * 128, 128), 128)
        qp = q_ref[:, cols]
        kp = kp_ref[rows, cols]
        kgp = kg_ref[0, :, cols]
        widths = widths_of(p)
        scales = by_row([LOG2E, LOG2E] + widths[0] + [LOG2E, LOG2E] + widths[1])
        biases = by_row([bias_ref[c, 2 * p + e] for e in range(2) for c in range(4)]) * scales
        s_ref[slot] = mm_nt(jnp.concatenate([qp * lo16, qp * hi16], axis=0), kp)
        sf_ref[slot] = mm_nt(qp, jnp.concatenate([kgp * lo16, kgp * hi16], axis=0))
        a, b = rich_sums(qp, kp, rq_ref[:, cols], rk_ref[:, cols], scales, biases)
        a_ref[slot] = a
        b_ref[slot] = b

    def weights(p, slot):
        widths = widths_of(p)
        for r in range(0, TILE, CH):
            rs = slice(r, r + CH)
            far = sf_ref[slot, rs, :] * (0.125 * LOG2E)
            tops = []
            held = []
            for e in range(2):
                base = 4 * e
                part = [a_ref[slot, rs, base + c : base + c + 1] for c in range(4)]
                line = [b_ref[slot, base + c : base + c + 1, :] for c in range(4)]
                u0 = (part[0] + line[0]) * ox_ref[rs, :]
                u1 = (part[1] + line[1]) * oy_ref[rs, :]
                e0 = jnp.exp2(jnp.minimum(u0, -u0))
                e1 = jnp.exp2(jnp.minimum(u1, -u1))
                r0 = 1.0 / (1.0 + e0)
                r1 = 1.0 / (1.0 + e1)
                gx = (widths[e][0] * dx_ref[rs, :] - part[2]) - line[2]
                gy = (widths[e][1] * dy_ref[rs, :] - part[3]) - line[3]
                s = s_ref[slot, e * TILE + r : e * TILE + r + CH, :] * (0.125 * LOG2E)
                s = s + jnp.minimum(u0, 0.0) + jnp.minimum(u1, 0.0) - gx * gx - gy * gy
                top = jnp.maximum(jnp.maximum(s[:, 0:128], s[:, 128:256]), s[:, 256:384])
                here = low if e == 0 else ~low
                top = jnp.maximum(top, jnp.where(here, far, -3e38))
                tops.append(jnp.max(top, axis=1, keepdims=True))
                g0 = jnp.where(u0 >= 0.0, e0, 1.0) * (ox_ref[rs, :] * r0)
                g1 = jnp.where(u1 >= 0.0, e1, 1.0) * (oy_ref[rs, :] * r1)
                g0_ref[0, 2 * p + e, rs, :] = g0.astype(BF16)
                g1_ref[0, 2 * p + e, rs, :] = g1.astype(BF16)
                held.append((s, r0 * r1))
            pfar = jnp.exp2(far - jnp.where(low, tops[0], tops[1]))
            invs = []
            for e in range(2):
                s, rr = held[e]
                pe = jnp.exp2(s - tops[e]) * rr
                here = low if e == 0 else ~low
                tot = pe[:, 0:128] + pe[:, 128:256] + pe[:, 256:384] + jnp.where(here, pfar, 0.0)
                inv = 1.0 / jnp.sum(tot, axis=1, keepdims=True)
                invs.append(inv)
                pn_ref[0, 2 * p + e, rs, :] = (pe * inv).astype(BF16)
            pf_ref[0, p, rs, :] = (pfar * jnp.where(low, invs[0], invs[1])).astype(BF16)

    def context(p):
        cols = pl.ds(pl.multiple_of(p * 128, 128), 128)
        vp = vp_ref[rows, cols]
        vgp = vg_ref[0, :, cols]
        ctx = mm(pn_ref[0, 2 * p], vp * lo16) + mm(pn_ref[0, 2 * p + 1], vp * hi16)
        ctx = ctx + mm(pf_ref[0, p], jnp.concatenate([vgp * lo16, vgp * hi16], axis=0))
        ctx_ref[:, cols] = ctx.astype(BF16)

    def group(index, carry):
        first = index * UNROLL
        for u in range(UNROLL):
            scores(first + u, u)
        for u in range(UNROLL):
            weights(first + u, u)
        for u in range(UNROLL):
            context(first + u)
        return carry

    lax.fori_loop(0, pairs // UNROLL, group, 0)


def attn_forward(q, k, v, before, after, every_glob, owner, w_qkv, norms, coords, units, lengths, offset, rich):
    rich_query, rich_key, rich_bias, rich_theta = rich
    rows, width = q.shape
    heads = rich_bias.shape[1]
    pairs = heads // 2
    tiles = rows // TILE
    blocks = rows // QBLOCK
    per_block = tiles // blocks
    padded_rows = rows + 2 * RADIUS
    globs = every_glob.shape[0]
    scalars = pl.BlockSpec(memory_space=pltpu.SMEM)

    def whole(*shape):
        return pl.BlockSpec(shape, lambda t: (0,) * len(shape))

    def block3(*shape):
        return pl.BlockSpec((1,) + shape, lambda t: (t // per_block, 0, 0))

    near = pl.BlockSpec((1, heads, TILE, SPAN), lambda t: (t, 0, 0, 0))
    near_shape = jax.ShapeDtypeStruct((tiles, heads, TILE, SPAN), BF16)
    tile_rows = pl.BlockSpec((TILE, width), lambda t: (t, 0))
    return pl.pallas_call(
        partial(fwd_kernel, pairs=pairs, per_block=per_block),
        grid=(tiles,),
        in_specs=[
            scalars, scalars, scalars, scalars, scalars,
            tile_rows, whole(rows, width), whole(rows, width),
            whole(RADIUS, width), whole(RADIUS, width),
            whole(globs, width), whole(1, globs),
            pl.BlockSpec((width, width), lambda t: (0, 1)),
            pl.BlockSpec((width, width), lambda t: (0, 2)),
            whole(*norms.shape),
            whole(*coords.shape), whole(4, width), whole(4, width),
        ],
        out_specs=[
            tile_rows, near,
            pl.BlockSpec((1, pairs, TILE, 128), lambda t: (t, 0, 0, 0)),
            near, near,
            whole(padded_rows, width), whole(padded_rows, width),
            block3(GLOB_FORM, width), block3(GLOB_FORM, width), block3(GLOB_FORM, width),
            block3(GLOB_FORM, width), block3(GLOB_FORM, globs),
        ],
        out_shape=[
            jax.ShapeDtypeStruct((rows, width), BF16),
            near_shape,
            jax.ShapeDtypeStruct((tiles, pairs, TILE, 128), BF16),
            near_shape, near_shape,
            jax.ShapeDtypeStruct((padded_rows, width), BF16),
            jax.ShapeDtypeStruct((padded_rows, width), BF16),
            jax.ShapeDtypeStruct((blocks, GLOB_FORM, width), BF16),
            jax.ShapeDtypeStruct((blocks, GLOB_FORM, width), BF16),
            jax.ShapeDtypeStruct((blocks, GLOB_FORM, width), BF16),
            jax.ShapeDtypeStruct((blocks, GLOB_FORM, width), F32),
            jax.ShapeDtypeStruct((blocks, GLOB_FORM, globs), BF16),
        ],
        scratch_shapes=[
            pltpu.VMEM((TILE, SPAN), F32), pltpu.VMEM((TILE, SPAN), F32),
            pltpu.VMEM((TILE, SPAN), F32), pltpu.VMEM((TILE, SPAN), F32),
            pltpu.VMEM((UNROLL, 2 * TILE, SPAN), F32), pltpu.VMEM((UNROLL, TILE, 128), F32),
            pltpu.VMEM((UNROLL, TILE, 8), F32), pltpu.VMEM((UNROLL, 8, SPAN), F32),
        ],
        compiler_params=pltpu.CompilerParams(vmem_limit_bytes=VMEM_LIMIT),
        cost_estimate=cost(65.0),
        name="attn_forward",
    )(units, lengths, offset, rich_bias, rich_theta, q, k, v, before, after, every_glob, owner,
      w_qkv, w_qkv, norms, coords, rich_query, rich_key)


def bwd_kernel(offset_ref, bias_ref, theta_ref,
               q_ref, dc_ref, ctx_ref, k_ref, v_ref, kg_ref, vg_ref, coords_ref, rq_ref, rk_ref,
               pn_ref, pf_ref, g0_ref, g1_ref,
               dq_ref, dk_ref, dv_ref, dkg_ref, dvg_ref, vec_ref, rim_ref,
               dx_ref, dy_ref, dp_ref, dpf_ref, ds_ref, dsf_ref, a_ref, b_ref, dqr_ref, db_ref, db_now,
               *, pairs, first_pair, tiles, per_block, edge):
    step = pl.program_id(0)
    t = step * (tiles - 1) if edge else step + 1

    @pl.when(step == 0)
    def _():
        vec_ref[...] = jnp.zeros_like(vec_ref)
        if not edge:
            rim_ref[...] = jnp.zeros_like(rim_ref)
            dk_ref[...] = jnp.zeros_like(dk_ref)
            dv_ref[...] = jnp.zeros_like(dv_ref)
            db_ref[...] = jnp.zeros_like(db_ref)

    if edge:
        fresh = step >= 0
    else:
        fresh = (step == 0) | (t % per_block == 0)

    @pl.when(fresh)
    def _():
        dkg_ref[...] = jnp.zeros_like(dkg_ref)
        dvg_ref[...] = jnp.zeros_like(dvg_ref)

    geometry_into(coords_ref, offset_ref[0, 0] // 128 + t - 1, None, (None, None, dx_ref, dy_ref))
    lo16, hi16 = half_masks(BF16)
    low64 = lax.broadcasted_iota(jnp.int32, (64, 128), 1) < 64
    lane8 = lax.broadcasted_iota(jnp.int32, (4, 128), 1)
    lane1 = lax.broadcasted_iota(jnp.int32, (1, 128), 1)
    sub = lax.broadcasted_iota(jnp.int32, (128, 1), 0)
    lo16c = (sub < 64).astype(F32).astype(BF16)
    hi16c = (sub >= 64).astype(F32).astype(BF16)
    rows = pl.ds(pl.multiple_of(t * TILE, TILE), SPAN)
    out_rows = pl.ds(pl.multiple_of((t - 1) * TILE, TILE), SPAN)

    def rich_key_parts(p, cols, sums, keys, columns):
        head = 2 * (p + first_pair)
        squares = [theta_ref[i, head + e] * theta_ref[i, head + e] for e in range(2) for i in range(2)]
        scales = by_row([1.0, 1.0, squares[0], squares[1], 1.0, 1.0, squares[2], squares[3]])
        scaled = sums * scales[:, 0:1]
        vectors = jnp.concatenate(split3(rich_rows(rk_ref[:, cols], None)), axis=0)
        parts = split3(scaled)
        left = jnp.concatenate([vectors[0:8]] * 3 + [vectors[8:16]] * 2 + [vectors[16:24]], axis=0)
        left = jnp.transpose(left).astype(BF16)
        right = jnp.concatenate([parts[0], parts[1], parts[2], parts[0], parts[1], parts[0]], axis=0).astype(BF16)
        extra = mm(left, right)
        stacked = jnp.concatenate(parts, axis=0).astype(BF16)
        key24 = mm(stacked, keys)
        key8 = key24[0:8] + key24[8:16] + key24[16:24]
        vec_ref[p, 4:8, :] += jnp.where(lane8 < 64, key8[0:4], key8[4:8])
        totals = jnp.sum(scaled, axis=1, keepdims=True)
        line = jnp.zeros((1, 128), F32)
        for index in range(8):
            line = jnp.where(lane1 == index, totals[index : index + 1, :], line)
        vec_ref[p, 8:9, :] += line
        return extra

    low_rows = lax.broadcasted_iota(jnp.int32, (BACK_CH, 128), 1) < 64

    def fold(full):
        return jnp.sum(full.reshape(full.shape[0] // 8, 8, full.shape[1]), axis=0)

    def pair_parts(p):
        cols = pl.ds(pl.multiple_of(p * 128, 128), 128)
        head = 2 * (p + first_pair)
        squares = [[theta_ref[i, head + e] * theta_ref[i, head + e] for i in range(2)] for e in range(2)]
        halves = [jnp.where(lane1 < 64, squares[0][i], squares[1][i]) for i in range(2)]
        return cols, head, halves

    def products(p, slot):
        cols, head, _ = pair_parts(p)
        qp = q_ref[:, cols]
        dcp = dc_ref[:, cols]
        kp = k_ref[rows, cols]
        vgp = vg_ref[0, :, cols]
        dp_ref[slot] = mm_nt(jnp.concatenate([dcp * lo16, dcp * hi16], axis=0), v_ref[rows, cols])
        dpf_ref[slot] = mm_nt(dcp, jnp.concatenate([vgp * lo16, vgp * hi16], axis=0))
        biases = by_row([bias_ref[c, head + e] for e in range(2) for c in range(4)])
        a, b = rich_sums(qp, kp, rq_ref[:, cols], rk_ref[:, cols], None, biases)
        a_ref[slot] = a
        b_ref[slot] = b

    def elements(p, slot):
        cols, head, halves = pair_parts(p)
        lines = [rq_ref[0:1, cols], rq_ref[1:2, cols], rq_ref[2:3, cols] * halves[0], rq_ref[3:4, cols] * halves[1]]
        col_sums = [[jnp.zeros((8, SPAN), F32) for _ in range(4)] for _ in range(2)]
        thetas = [[jnp.zeros((8, 128), F32) for _ in range(2)] for _ in range(2)]
        query_sums = [jnp.zeros((8, 128), F32) for _ in range(4)]
        for r in range(0, TILE, BACK_CH):
            rs = slice(r, r + BACK_CH)
            prod = dc_ref[rs, cols].astype(F32) * ctx_ref[rs, cols].astype(F32)
            row_sums = []
            dots = []
            for e in range(2):
                here = low_rows if e == 0 else ~low_rows
                base = 4 * e
                dot = jnp.sum(jnp.where(here, prod, 0.0), axis=1, keepdims=True)
                dots.append(dot)
                es = slice(e * TILE + r, e * TILE + r + BACK_CH)
                ds = pn_ref[0, 2 * p + e, rs, :].astype(F32) * (dp_ref[slot, es, :] - dot)
                ds_ref[slot, es, :] = ds.astype(BF16)
                t0 = ds * g0_ref[0, 2 * p + e, rs, :].astype(F32)
                t1 = ds * g1_ref[0, 2 * p + e, rs, :].astype(F32)
                gx = (dx_ref[rs, :] - a_ref[slot, rs, base + 2 : base + 3]) - b_ref[slot, base + 2 : base + 3, :]
                gy = (dy_ref[rs, :] - a_ref[slot, rs, base + 3 : base + 4]) - b_ref[slot, base + 3 : base + 4, :]
                tx = ds * gx
                ty = ds * gy
                for i, full in enumerate((tx * gx, ty * gy)):
                    thetas[e][i] = thetas[e][i] + fold(full[:, 0:128] + full[:, 128:256] + full[:, 256:384])
                sums = []
                for c, full in enumerate((t0, t1, tx, ty)):
                    col_sums[e][c] = col_sums[e][c] + fold(full)
                    sums.append(jnp.sum(full[:, 0:128] + full[:, 128:256] + full[:, 256:384], axis=1, keepdims=True))
                row_sums.append(sums)
            dsf = pf_ref[0, p, rs, :].astype(F32) * (dpf_ref[slot, rs, :] - jnp.where(low_rows, dots[0], dots[1]))
            dsf_ref[slot, rs, :] = dsf.astype(BF16)
            qf = q_ref[rs, cols].astype(F32)
            dqr = jnp.zeros((BACK_CH, 128), F32)
            for c in range(4):
                da = jnp.where(low_rows, row_sums[0][c], row_sums[1][c])
                dqr = dqr + da * lines[c]
                query_sums[c] = query_sums[c] + fold(da * qf)
            dqr_ref[slot, rs, :] = dqr
        folded = jnp.concatenate([jnp.sum(query_sums[c], axis=0, keepdims=True) for c in range(4)], axis=0)
        scale4 = jnp.concatenate([jnp.ones((2, 128), F32), halves[0], halves[1]], axis=0)
        vec_ref[p, 0:4, :] += folded * scale4
        line = jnp.zeros((1, 128), F32)
        for e in range(2):
            for i in range(2):
                total = jnp.sum(jnp.sum(thetas[e][i], axis=0, keepdims=True), axis=1, keepdims=True)
                line = jnp.where(lane1 == 8 + 2 * e + i, total * (-theta_ref[i, head + e]), line)
        vec_ref[p, 8:9, :] += line
        db_now[slot] = jnp.concatenate([jnp.sum(col_sums[e][c], axis=0, keepdims=True) for e in range(2) for c in range(4)], axis=0)

    def results(p, slot):
        cols, head, _ = pair_parts(p)
        qp = q_ref[:, cols]
        dcp = dc_ref[:, cols]
        kp = k_ref[rows, cols]
        kgp = kg_ref[0, :, cols]
        packed = db_now[slot]
        dq = mm(ds_ref[slot, 0:TILE, :], kp * lo16) + mm(ds_ref[slot, TILE : 2 * TILE, :], kp * hi16)
        dq = dq + mm(dsf_ref[slot], jnp.concatenate([kgp * lo16, kgp * hi16], axis=0))
        dq_ref[:, cols] = (dq * 0.125 + dqr_ref[slot]).astype(BF16)
        qT = jnp.transpose(qp)
        dcT = jnp.transpose(dcp)
        dk = mm(jnp.concatenate([qT * lo16c, qT * hi16c], axis=1), ds_ref[slot]) * 0.125
        dv = mm(dcT * lo16c, pn_ref[0, 2 * p]) + mm(dcT * hi16c, pn_ref[0, 2 * p + 1])
        if edge:
            dk = dk + rich_key_parts(p, cols, packed, kp, rows)
            dk_ref[0, cols, :] = dk
            dv_ref[0, cols, :] = dv
            for index, full in enumerate((dk, dv)):
                rim = jnp.where(step == 0, full[:, 0:RADIUS], full[:, SPAN - RADIUS : SPAN])
                rim_ref[0, index, cols, :] = rim.astype(BF16)
        else:
            dk_ref[cols, out_rows] += dk
            dv_ref[cols, out_rows] += dv
            db_ref[p, :, out_rows] += packed
        dkg2 = mm(jnp.transpose(dsf_ref[slot]), qp) * 0.125
        dvg2 = mm(jnp.transpose(pf_ref[0, p]), dcp)
        dkg_ref[0, :, cols] += jnp.where(low64, dkg2[0:64], dkg2[64:128])
        dvg_ref[0, :, cols] += jnp.where(low64, dvg2[0:64], dvg2[64:128])

    def group(index, carry):
        first = index * BACK_UNROLL
        for stage in (products, elements, results):
            for u in range(BACK_UNROLL):
                stage(first + u, u)
        return carry

    lax.fori_loop(0, pairs // BACK_UNROLL, group, 0)

    if not edge:

        @pl.when(step == pl.num_programs(0) - 1)
        def _():
            own = k_ref.shape[0] - 2 * RADIUS

            def finish(p, carry):
                cols = pl.ds(pl.multiple_of(p * 128, 128), 128)
                keys = k_ref[RADIUS : RADIUS + own, cols]
                dk_ref[cols, :] += rich_key_parts(p, cols, db_ref[p], keys, None)
                return carry

            lax.fori_loop(0, pairs, finish, 0)


def attn_backward(q, dctx, ctx, k_pad, v_pad, kg, vg, coords, offset, rich, kept, first_pair, pairs, edge):
    rich_query, rich_key, rich_bias, rich_theta = rich
    rows, width = q.shape
    tiles = rows // TILE
    blocks = kg.shape[0]
    per_block = tiles // blocks
    part = pairs * 128
    half = first_pair // pairs
    steps = 2 if edge else tiles - 2
    padded_rows = k_pad.shape[0]
    scalars = pl.BlockSpec(memory_space=pltpu.SMEM)

    def tile(i):
        return i * (tiles - 1) if edge else i + 1

    tile_rows = pl.BlockSpec((TILE, part), lambda i: (tile(i), half))
    padded_cols = pl.BlockSpec((padded_rows, part), lambda i: (0, half))
    block3 = pl.BlockSpec((1, GLOB_FORM, part), lambda i: (tile(i) // per_block, 0, half))
    out3 = pl.BlockSpec((1, GLOB_FORM, part), lambda i: (tile(i) // per_block, 0, 0))
    vectors = pl.BlockSpec((4, part), lambda i: (0, half))
    near = pl.BlockSpec((1, 2 * pairs, TILE, SPAN), lambda i: (tile(i), half, 0, 0))
    far = pl.BlockSpec((1, pairs, TILE, 128), lambda i: (tile(i), half, 0, 0))
    if edge:
        key_out = pl.BlockSpec((1, part, SPAN), lambda i: (i, 0, 0))
        key_shape = jax.ShapeDtypeStruct((2, part, SPAN), F32)
        rim_out = pl.BlockSpec((1, 2, part, RADIUS), lambda i: (i, 0, 0, 0))
        rim_shape = jax.ShapeDtypeStruct((2, 2, part, RADIUS), BF16)
    else:
        key_out = pl.BlockSpec((part, rows), lambda i: (0, 0))
        key_shape = jax.ShapeDtypeStruct((part, rows), F32)
        rim_out = pl.BlockSpec((1, 2, 16, RADIUS), lambda i: (0, 0, 0, 0))
        rim_shape = jax.ShapeDtypeStruct((1, 2, 16, RADIUS), BF16)
    glob_shape = jax.ShapeDtypeStruct((blocks, GLOB_FORM, part), F32)
    return pl.pallas_call(
        partial(bwd_kernel, pairs=pairs, first_pair=first_pair, tiles=tiles, per_block=per_block, edge=edge),
        grid=(steps,),
        in_specs=[
            scalars, scalars, scalars,
            tile_rows, tile_rows, tile_rows, padded_cols, padded_cols, block3, block3,
            pl.BlockSpec(coords.shape, lambda i: (0, 0)), vectors, vectors,
            near, far, near, near,
        ],
        out_specs=[
            pl.BlockSpec((TILE, part), lambda i: (i, 0)),
            key_out, key_out, out3, out3,
            pl.BlockSpec((pairs, 16, 128), lambda i: (0, 0, 0)),
            rim_out,
        ],
        out_shape=[
            jax.ShapeDtypeStruct((steps * TILE, part), BF16),
            key_shape, key_shape, glob_shape, glob_shape,
            jax.ShapeDtypeStruct((pairs, 16, 128), F32),
            rim_shape,
        ],
        scratch_shapes=[
            pltpu.VMEM((TILE, SPAN), F32), pltpu.VMEM((TILE, SPAN), F32),
            pltpu.VMEM((BACK_UNROLL, 2 * TILE, SPAN), F32), pltpu.VMEM((BACK_UNROLL, TILE, 128), F32),
            pltpu.VMEM((BACK_UNROLL, 2 * TILE, SPAN), BF16), pltpu.VMEM((BACK_UNROLL, TILE, 128), BF16),
            pltpu.VMEM((BACK_UNROLL, TILE, 8), F32), pltpu.VMEM((BACK_UNROLL, 8, SPAN), F32),
            pltpu.VMEM((BACK_UNROLL, TILE, 128), F32), pltpu.VMEM((pairs, 8, rows), F32),
            pltpu.VMEM((BACK_UNROLL, 8, SPAN), F32),
        ],
        compiler_params=pltpu.CompilerParams(vmem_limit_bytes=VMEM_LIMIT),
        cost_estimate=cost(8.2 * steps * pairs / 6),
        name="attn_backward_edge" if edge else "attn_backward_mid",
    )(offset, rich_bias, rich_theta, q, dctx, ctx, k_pad, v_pad, kg, vg, coords, rich_query, rich_key, *kept)


FF_CHUNK = 512
ROW_CHUNK = 512

TAIL_SLOPE = 0.35
TAIL = (0.0987331438, 0.0987265523, 0.092954664, 0.0773361877, 0.0814717893, -0.00727472285, 0.100604539, -0.0425525649)


def gelu_pair(values):
    t = 1.0 / (1.0 + (TAIL_SLOPE * math.sqrt(0.5)) * jnp.abs(values))
    poly = TAIL[-1] * t + TAIL[-2]
    for coef in TAIL[-3::-1]:
        poly = poly * t + coef
    bell = jnp.exp2((values * values) * (-0.5 * LOG2E))
    tail = t * poly * bell
    phi = jnp.where(values >= 0.0, 1.0 - tail, tail)
    return values * phi, phi + (values * bell) * (1.0 / math.sqrt(2.0 * math.pi))


def ffn_kernel(tok_ref, ctx_ref, ct_ref, wo_ref, wu_ref, wd_ref, norms_ref,
               out_ref, dmid_ref, dctx_ref, wog_ref, wug_ref, wdg_ref, vec_ref,
               mid_ref, h2_ref, h2t_ref, acc_ref, dh_ref, act_ref, dpre_ref, *, rows):
    step = pl.program_id(0)
    last = pl.num_programs(0) - 1

    @pl.when(step == 0)
    def _():
        @pl.loop(0, rows // ROW_CHUNK)
        def _(index):
            rs = pl.ds(pl.multiple_of(index * ROW_CHUNK, ROW_CHUNK), ROW_CHUNK)
            mid = tok_ref[rs, :].astype(F32) + mm(ctx_ref[rs, :], wo_ref[...])
            mid_ref[rs, :] = mid
            normed, _ = norm_parts(mid)
            h2 = (normed * norms_ref[2:3, :] + norms_ref[3:4, :]).astype(BF16)
            h2_ref[rs, :] = h2
            h2t_ref[:, rs] = jnp.transpose(h2)
            acc_ref[rs, :] = jnp.zeros_like(mid)
            dh_ref[rs, :] = jnp.zeros_like(mid)

    @pl.loop(0, rows // ROW_CHUNK)
    def _(index):
        rs = pl.ds(pl.multiple_of(index * ROW_CHUNK, ROW_CHUNK), ROW_CHUNK)
        pre = mm(h2_ref[rs, :], wu_ref[...])
        dact = mm_nt(ct_ref[rs, :], wd_ref[...])
        act, slope = gelu_pair(pre)
        act_ref[rs, :] = act.astype(BF16)
        dpre_ref[rs, :] = (dact * slope).astype(BF16)
        acc_ref[rs, :] += mm(act_ref[rs, :], wd_ref[...])
        dh_ref[rs, :] += mm_nt(dpre_ref[rs, :], wu_ref[...])
    wug_ref[...] = mm(h2t_ref[...], dpre_ref[...]).astype(BF16)
    wdg_ref[...] = mm_tn(act_ref[...], ct_ref[...]).astype(BF16)

    @pl.when(step == last)
    def _():
        def finish(index, sums):
            rs = pl.ds(pl.multiple_of(index * ROW_CHUNK, ROW_CHUNK), ROW_CHUNK)
            mid = mid_ref[rs, :]
            out_ref[rs, :] = (mid + acc_ref[rs, :]).astype(BF16)
            normed, scale = norm_parts(mid)
            dh = dh_ref[rs, :]
            gains = sums[0] + jnp.sum((dh * normed).reshape(ROW_CHUNK // 8, 8, -1), axis=0)
            shifts = sums[1] + jnp.sum(dh.reshape(ROW_CHUNK // 8, 8, -1), axis=0)
            dmid = ct_ref[rs, :].astype(F32) + norm_pull(dh, normed, scale, norms_ref[2:3, :])
            dmid_ref[rs, :] = dmid
            dattn = dmid.astype(BF16)
            h2_ref[rs, :] = dattn
            dctx_ref[rs, :] = mm_nt(dattn, wo_ref[...]).astype(BF16)
            return gains, shifts

        start = jnp.zeros((8, norms_ref.shape[1]), F32)
        gains, shifts = lax.fori_loop(0, rows // ROW_CHUNK, finish, (start, start))
        wog_ref[...] = mm_tn(ctx_ref[...], h2_ref[...]).astype(BF16)
        vec_ref[0:1, :] = jnp.sum(gains, axis=0, keepdims=True)
        vec_ref[1:2, :] = jnp.sum(shifts, axis=0, keepdims=True)

def feed_forward(tokens, context, cotangent, w_out, w_up, w_down, norms):
    rows, width = tokens.shape
    hidden = w_up.shape[1]
    steps = hidden // FF_CHUNK
    whole = lambda *shape: pl.BlockSpec(shape, lambda s: (0,) * len(shape))
    return pl.pallas_call(
        partial(ffn_kernel, rows=rows),
        grid=(steps,),
        in_specs=[
            whole(rows, width), whole(rows, width), whole(rows, width), whole(width, width),
            pl.BlockSpec((width, FF_CHUNK), lambda s: (0, s)),
            pl.BlockSpec((FF_CHUNK, width), lambda s: (s, 0)),
            whole(*norms.shape),
        ],
        out_specs=[
            whole(rows, width), whole(rows, width), whole(rows, width), whole(width, width),
            pl.BlockSpec((width, FF_CHUNK), lambda s: (0, s)),
            pl.BlockSpec((FF_CHUNK, width), lambda s: (s, 0)),
            whole(8, width),
        ],
        out_shape=[
            jax.ShapeDtypeStruct((rows, width), BF16),
            jax.ShapeDtypeStruct((rows, width), F32),
            jax.ShapeDtypeStruct((rows, width), BF16),
            jax.ShapeDtypeStruct((width, width), BF16),
            jax.ShapeDtypeStruct((width, hidden), BF16),
            jax.ShapeDtypeStruct((hidden, width), BF16),
            jax.ShapeDtypeStruct((8, width), F32),
        ],
        scratch_shapes=[
            pltpu.VMEM((rows, width), F32), pltpu.VMEM((rows, width), BF16), pltpu.VMEM((width, rows), BF16),
            pltpu.VMEM((rows, width), F32), pltpu.VMEM((rows, width), F32),
            pltpu.VMEM((rows, FF_CHUNK), BF16), pltpu.VMEM((rows, FF_CHUNK), BF16),
        ],
        compiler_params=pltpu.CompilerParams(vmem_limit_bytes=VMEM_LIMIT),
        cost_estimate=cost(60.0),
        name="feed_forward",
    )(tokens, context, cotangent, w_out, w_up, w_down, norms)


def qkv_grad_kernel(ht_ref, hg_ref, dqe_ref, dqm_ref, dke_ref, dve_ref, dkm_ref, dvm_ref, before_ref, after_ref,
                    dkge_ref, dvge_ref, dkgm_ref, dvgm_ref, grad_ref, part_ref, glob_ref, dkt_ref):
    step = pl.program_id(0)
    rows, part = part_ref.shape
    width = ht_ref.shape[0]
    edge = 128

    @pl.when(step == 0)
    def _():
        part_ref[0:edge, :] = dqe_ref[0:edge, :]
        part_ref[edge : rows - edge, :] = dqm_ref[...]
        part_ref[rows - edge : rows, :] = dqe_ref[edge : 2 * edge, :]
        grad_ref[...] = mm(ht_ref[...], part_ref[...]).astype(BF16)

    sources = ((1, dke_ref, dkm_ref, dkge_ref, dkgm_ref), (2, dve_ref, dvm_ref, dvge_ref, dvgm_ref))
    for index, edge_ref, mid_ref, edge_glob, mid_glob in sources:

        @pl.when(step == index)
        def _():
            dkt_ref[...] = mid_ref[...].astype(BF16)
            dkt_ref[:, 0:128] = (mid_ref[:, 0:128] + edge_ref[0, :, 128:256] + before_ref[index - 1].astype(F32)).astype(BF16)
            dkt_ref[:, 128:256] = (mid_ref[:, 128:256] + edge_ref[0, :, 256:384]).astype(BF16)
            dkt_ref[:, rows - 256 : rows - 128] = (mid_ref[:, rows - 256 : rows - 128] + edge_ref[1, :, 0:128]).astype(BF16)
            dkt_ref[:, rows - 128 : rows] = (
                mid_ref[:, rows - 128 : rows] + edge_ref[1, :, 128:256] + after_ref[index - 1].astype(F32)
            ).astype(BF16)
            part_ref[...] = jnp.transpose(dkt_ref[...])
            glob = (edge_glob[...] + mid_glob[...]).reshape(-1, part).astype(BF16)
            glob_ref[...] = glob
            hg = hg_ref[...].reshape(-1, width)
            grad_ref[...] = (mm(ht_ref[...], part_ref[...]) + mm_tn(hg, glob)).astype(BF16)


def qkv_grad(hidden_t, hg, dq, dk, dv, rims, dkg, dvg, half, pairs):
    width, rows = hidden_t.shape
    part = pairs * 128
    blocks = hg.shape[0]

    def whole(*shape):
        return pl.BlockSpec(shape, lambda i: (0,) * len(shape))

    edge_keys = pl.BlockSpec((2, part, SPAN), lambda i: (0, half, 0))
    edge_glob = pl.BlockSpec((blocks, GLOB_FORM, part), lambda i: (0, 0, half))
    rim = pl.BlockSpec((2, part, RADIUS), lambda i: (0, half, 0))
    mid_glob = whole(blocks, GLOB_FORM, part)
    return pl.pallas_call(
        qkv_grad_kernel,
        grid=(3,),
        in_specs=[
            whole(width, rows), whole(blocks, GLOB_FORM, width),
            pl.BlockSpec((2 * TILE, part), lambda i: (0, half)), whole(rows - 2 * TILE, part),
            edge_keys, edge_keys, whole(part, rows), whole(part, rows), rim, rim,
            edge_glob, edge_glob, mid_glob, mid_glob,
        ],
        out_specs=[
            pl.BlockSpec((width, part), lambda i: (0, i)),
            pl.BlockSpec((rows, part), lambda i: (0, i)),
            pl.BlockSpec((blocks * GLOB_FORM, part), lambda i: (0, jnp.maximum(i - 1, 0))),
        ],
        out_shape=[
            jax.ShapeDtypeStruct((width, 3 * part), BF16),
            jax.ShapeDtypeStruct((rows, 3 * part), BF16),
            jax.ShapeDtypeStruct((blocks * GLOB_FORM, 2 * part), BF16),
        ],
        scratch_shapes=[pltpu.VMEM((part, rows), BF16)],
        compiler_params=pltpu.CompilerParams(vmem_limit_bytes=VMEM_LIMIT),
        cost_estimate=cost(20.0),
        name="qkv_grad",
    )(hidden_t, hg, dq[0], dq[1], dk[0], dv[0], dk[1], dv[1], rims[0], rims[1], dkg[0], dvg[0], dkg[1], dvg[1])


def token_grad_kernel(pa_ref, pb_ref, tok_ref, dmid_ref, w_ref, norms_ref, ga_ref, gb_ref, oh_ref, ng_ref, second_ref,
                      ve_ref, va_ref, vb_ref, tg_ref, gp_ref, vec_ref, both_ref, gains_ref, shifts_ref, *, pairs, kept):
    step = pl.program_id(0)
    width = tok_ref.shape[1]
    part = pairs * 128

    @pl.when(step == 0)
    def _():
        gains_ref[...] = jnp.zeros_like(gains_ref)
        shifts_ref[...] = jnp.zeros_like(shifts_ref)

    for index in range(3):
        both_ref[:, index * width : index * width + part] = pa_ref[:, index * part : (index + 1) * part]
        both_ref[:, index * width + part : (index + 1) * width] = pb_ref[:, index * part : (index + 1) * part]
    dh = mm_nt(both_ref[...], w_ref[...])
    normed, scale = norm_parts(tok_ref[...].astype(F32))
    count = dh.shape[0] // 8
    gains_ref[...] += jnp.sum((dh * normed).reshape(count, 8, width), axis=0)
    shifts_ref[...] += jnp.sum(dh.reshape(count, 8, width), axis=0)
    tg_ref[...] = (dmid_ref[...] + norm_pull(dh, normed, scale, norms_ref[0:1, :])).astype(BF16)

    @pl.when(step == pl.num_programs(0) - 1)
    def _():
        dhg = jnp.zeros((ga_ref.shape[0], width), F32)
        for index in range(2):
            for half, ref in ((0, ga_ref), (1, gb_ref)):
                start = (index + 1) * width + half * part
                dhg = dhg + mm_nt(ref[:, index * part : (index + 1) * part], w_ref[:, start : start + part])
        glob_normed = ng_ref[...].reshape(-1, width)
        rows_all = [
            jnp.sum(gains_ref[...], axis=0, keepdims=True) + jnp.sum(dhg * glob_normed, axis=0, keepdims=True),
            jnp.sum(shifts_ref[...], axis=0, keepdims=True) + jnp.sum(dhg, axis=0, keepdims=True),
        ]
        vec_ref[0:1, :] = rows_all[0]
        vec_ref[1:2, :] = rows_all[1]
        vec_ref[2:4, :] = second_ref[0:2, :]
        gp_ref[...] = mm_tn(oh_ref[...].reshape(-1, oh_ref.shape[2]), dhg.astype(BF16)).astype(BF16)
        lines = []
        for p in range(2 * pairs):
            mid = va_ref[p] if p < pairs else vb_ref[p - pairs]
            both = ve_ref[p] + mid
            vec_ref[4:12, p * 128 : p * 128 + 128] = both[0:8]
            lines.append(both[8:9])
        lines.append(jnp.zeros((8 - len(lines), 128), F32))
        lines = jnp.concatenate(split3(jnp.concatenate(lines, axis=0)), axis=0).astype(BF16)
        spot = lax.broadcasted_iota(jnp.int32, (128, width), 0)
        lane = lax.broadcasted_iota(jnp.int32, (128, width), 1)
        spread = mm(lines, (lax.rem(lane, kept) == spot).astype(F32).astype(BF16))
        vec_ref[12:20, :] = spread[0:8] + spread[8:16] + spread[16:24]
        vec_ref[20:24, :] = jnp.zeros((4, width), F32)


def token_grad(parts, globs, tokens, grad_middle, w_qkv, norms, picked, glob_normed, second_sums, vecs, pairs, kept):
    rows, width = tokens.shape
    step = 256
    count = picked.shape[2]

    def whole(*shape):
        return pl.BlockSpec(shape, lambda i: (0,) * len(shape))

    def block(columns):
        return pl.BlockSpec((step, columns), lambda i: (i, 0))

    return pl.pallas_call(
        partial(token_grad_kernel, pairs=pairs, kept=kept),
        grid=(rows // step,),
        in_specs=[
            block(parts[0].shape[1]), block(parts[1].shape[1]), block(width), block(width), whole(*w_qkv.shape),
            whole(*norms.shape), whole(*globs[0].shape), whole(*globs[1].shape), whole(*picked.shape),
            whole(*glob_normed.shape), whole(*second_sums.shape),
        ] + [whole(*v.shape) for v in vecs],
        out_specs=[block(width), whole(count, width), whole(24, width)],
        out_shape=[
            jax.ShapeDtypeStruct((rows, width), BF16),
            jax.ShapeDtypeStruct((count, width), BF16),
            jax.ShapeDtypeStruct((24, width), F32),
        ],
        scratch_shapes=[pltpu.VMEM((step, 3 * width), BF16), pltpu.VMEM((8, width), F32), pltpu.VMEM((8, width), F32)],
        compiler_params=pltpu.CompilerParams(vmem_limit_bytes=VMEM_LIMIT),
        cost_estimate=cost(40.0),
        name="token_grad",
    )(*parts, tokens, grad_middle, w_qkv, norms, *globs, picked, glob_normed, second_sums, *vecs)


def swap_on(axis, mask):
    return [(i, i ^ mask) for i in range(lax.axis_size(axis))]


def add_low(kept, received):
    return (kept.astype(F32) + received.astype(F32)).astype(BF16)


def core_halves(grads, place):
    count = lax.axis_size("seq")
    view = grads.reshape(count // 2, 2, grads.shape[0] // count, grads.shape[1])
    send = lax.dynamic_index_in_dim(view, 1 - place % 2, 1, keepdims=False)
    kept = lax.dynamic_index_in_dim(view, place % 2, 1, keepdims=False)
    return kept, send


def core_swap(send):
    return lax.ppermute(send, "seq", swap_on("seq", 1))


def stream_blocks(summed, group_count):
    outer, rows, columns = summed.shape
    return jnp.moveaxis(summed.reshape(outer, group_count, rows // group_count, columns), 1, 0)


def halve_step(blocks, axis, place, bit, width):
    mine = (place >> bit) & 1
    send = lax.dynamic_index_in_dim(blocks, 1 - mine, width, keepdims=False)
    kept = lax.dynamic_index_in_dim(blocks, mine, width, keepdims=False)
    return kept, lax.ppermute(send, axis, swap_on(axis, 1 << bit))


def exchange_parts(blocks, axis, place, stride):
    parts = [lax.dynamic_index_in_dim(blocks, place, 0, keepdims=False)]
    for step in range(1, blocks.shape[0]):
        send = lax.dynamic_index_in_dim(blocks, place ^ step, 0, keepdims=False)
        parts.append(lax.ppermute(send, axis, swap_on(axis, step * stride)))
    return parts


def summed_low(parts):
    total = parts[0].astype(F32)
    for part in parts[1:]:
        total = total + part.astype(F32)
    return total.astype(BF16)


def gather_rows(rows, axis, place, bit):
    other = lax.ppermute(rows, axis, swap_on(axis, bit))
    upper = (place & bit) > 0
    return jnp.concatenate([jnp.where(upper, other, rows), jnp.where(upper, rows, other)], axis=0)


def gather_blocks(rows, axis, place, stride):
    count = lax.axis_size(axis) // stride
    every = [rows] + [lax.ppermute(rows, axis, swap_on(axis, step * stride)) for step in range(1, count)]
    return ordered(jnp.stack(every), place).reshape(count * rows.shape[0], rows.shape[1])


def ordered(stacked, place):
    count = stacked.shape[0]
    rest = stacked.shape[1:]
    bit = 1
    while bit < count:
        view = stacked.reshape((count // (2 * bit), 2, bit) + rest)
        stacked = jnp.where((place & bit) > 0, view[:, ::-1], view).reshape((count,) + rest)
        bit *= 2
    return stacked


def tied(*values):
    return lax.optimization_barrier(values)


def flat_rows(array, width):
    rows, columns = array.shape
    if columns % width == 0:
        return jnp.concatenate([array[:, i : i + width] for i in range(0, columns, width)], axis=0)
    return array.reshape(-1, width)


def flat_blocks(array, width):
    count, columns = array.shape[0], array.shape[-1]
    array = array.reshape(count, -1, columns)
    if columns % width == 0:
        return jnp.concatenate([array[:, :, i : i + width] for i in range(0, columns, width)], axis=1)
    return array.reshape(count, -1, width)


def unflat_rows(stacked, rows, columns):
    count, width = stacked.shape[0], stacked.shape[2]
    if columns % width == 0:
        return jnp.concatenate([stacked[:, i * rows : (i + 1) * rows] for i in range(columns // width)], axis=2)
    return stacked.reshape(count, rows, columns)


def pad_rows(blocks, width):
    count = blocks.shape[0]
    flat = blocks.reshape(count, -1)
    size = -(-flat.shape[1] // (16 * width)) * 16 * width
    return jnp.pad(flat, ((0, 0), (0, size - flat.shape[1]))).reshape(count, -1, width)


def exchange_raw(piece, axis):
    count = lax.axis_size(axis)
    return [piece] + [lax.ppermute(piece, axis, swap_on(axis, step)) for step in range(1, count)]


def body(
    tokens,
    global_states,
    cotangent,
    w_qkv,
    w_out,
    w_up,
    w_down,
    first_gain,
    first_shift,
    second_gain,
    second_shift,
    rich_query,
    rich_key,
    rich_bias,
    rich_theta,
    bucket_units,
    form_lengths,
    coords,
    glob_owner,
):
    row_count = tokens.shape[1]
    model_width = tokens.shape[2]
    place = lax.axis_index("seq")
    group = lax.axis_index("stream")
    seq_count = lax.axis_size("seq")
    group_count = lax.axis_size("stream")
    rich = (rich_query, rich_key, rich_bias, rich_theta)
    offset = (place * row_count).astype(jnp.int32).reshape(1, 1)
    norms = jnp.stack([first_gain, first_shift, second_gain, second_shift])
    up = [(i, i + 1) for i in range(seq_count - 1)]
    down = [(i + 1, i) for i in range(seq_count - 1)]
    pairs = rich_bias.shape[1] // 2
    half_pairs = pairs // 2
    kept_rows = model_width // seq_count

    before = lax.ppermute(tokens[0, row_count - RADIUS :], "seq", up)
    after = lax.ppermute(tokens[0, :RADIUS], "seq", down)
    pair_glob = gather_rows(global_states[0], "seq", place, 1)
    pair_glob, norms, before, after = tied(pair_glob, norms, before, after)
    every_glob = gather_blocks(pair_glob, "seq", place // 2, 2)
    queries, keys, values, hidden_t = project_tokens(tokens[0], w_qkv, norms)
    (context, pn, pf, g0, g1, key_pad, value_pad, glob_keys, glob_values, glob_hidden, glob_normed, picked) = attn_forward(
        queries, keys, values, before, after, every_glob, glob_owner, w_qkv, norms,
        coords[0], bucket_units, form_lengths, offset, rich,
    )
    layer_out, grad_middle, grad_context, grad_w_out, grad_w_up, grad_w_down, second_sums = feed_forward(
        tokens[0], context, cotangent[0], w_out, w_up, w_down, norms
    )

    def attention_back(first_pair, count, edge, grad_context):
        return attn_backward(
            queries, grad_context, context, key_pad, value_pad, glob_keys, glob_values, coords[0], offset, rich,
            (pn, pf, g0, g1), first_pair, count, edge,
        )

    halves = [core_halves(grad, place) for grad in (grad_w_up, grad_w_down, grad_w_out)]
    sends = [half[1] for half in halves]
    grad_context, *sends = tied(grad_context, *sends)
    halves = [(half[0], core_swap(send)) for half, send in zip(halves, sends)]
    dq_e, dk_e, dv_e, dkg_e, dvg_e, vec_e, rim_e = attention_back(0, pairs, True, grad_context)
    to_before, to_after = rim_e[0], rim_e[1]
    rims = (lax.ppermute(to_after, "seq", up), lax.ppermute(to_before, "seq", down))

    (dq_e, *swapped) = tied(dq_e, *[half[1] for half in halves])
    halves = [(half[0], received) for half, received in zip(halves, swapped)]

    sums = [add_low(*half) for half in halves]
    outer = seq_count // 2
    bits = group_count.bit_length() - 1
    pieces = [
        jnp.moveaxis(sums[0].reshape(outer, kept_rows, group_count, -1), 2, 0).reshape(group_count, outer, -1, model_width),
        jnp.moveaxis(sums[1].reshape(outer, group_count, -1, model_width), 1, 0),
        jnp.moveaxis(sums[2].reshape(outer, group_count, -1, model_width), 1, 0),
    ]
    piece_rows = [piece.shape[2] for piece in pieces]
    early = jnp.concatenate(pieces, axis=2).reshape((2,) * bits + (outer, sum(piece_rows), model_width))
    columns = model_width // 2
    early_x, early_y = early[..., :columns], early[..., columns:]
    order_x = list(range(bits))
    order_y = order_x[1:] + order_x[:1]

    def halved(blocks, order, done):
        bit = order[done]
        rest = sorted(order[done:], reverse=True)
        return halve_step(blocks, "stream", group, bit, rest.index(bit))

    early_x, early_y, grad_context, *rims = tied(early_x, early_y, grad_context, *rims)
    (keep_x, got_x), (keep_y, got_y) = halved(early_x, order_x, 0), halved(early_y, order_y, 0)
    dq_a, dk_a, dv_a, dkg_a, dvg_a, vec_a, _ = attention_back(0, half_pairs, False, grad_context)
    grads_a, part_a, glob_a = qkv_grad(
        hidden_t, glob_hidden, (dq_e, dq_a), (dk_e, dk_a), (dv_e, dv_a), rims, (dkg_e, dkg_a), (dvg_e, dvg_a), 0, half_pairs
    )
    got_x, got_y, grads_a = tied(got_x, got_y, grads_a)
    early_x, early_y = add_low(keep_x, got_x), add_low(keep_y, got_y)
    kept_a, send_a = core_halves(grads_a, place)
    split = (2,) * bits + (outer, kept_rows // group_count, -1)
    late_a = stream_blocks(add_low(kept_a, core_swap(send_a)), group_count).reshape(split)
    early_x, early_y, late_a, grad_context = tied(early_x, early_y, late_a, grad_context)
    for done in range(1, bits):
        (keep_x, got_x), (keep_y, got_y) = halved(early_x, order_x, done), halved(early_y, order_y, done)
        early_x, early_y = (keep_x, got_x), (keep_y, got_y)
        if done + 1 < bits:
            early_x, early_y = add_low(*early_x), add_low(*early_y)
    keep_a, got_a = halved(late_a, order_x, 0)
    dq_b, dk_b, dv_b, dkg_b, dvg_b, vec_b, _ = attention_back(half_pairs, half_pairs, False, grad_context)
    got_x, got_y, got_a, dq_b = tied(early_x[1], early_y[1], got_a, dq_b)
    early = jnp.concatenate([add_low(early_x[0], got_x), add_low(early_y[0], got_y)], axis=-1)
    late_a = add_low(keep_a, got_a)
    early, late_a, dq_b = tied(early, late_a, dq_b)
    early = exchange_parts(early, "seq", place // 2, 2)
    for done in range(1, bits):
        late_a = halved(late_a, order_x, done)
        if done + 1 < bits:
            late_a = add_low(*late_a)
    grads_b, part_b, glob_b = qkv_grad(
        hidden_t, glob_hidden, (dq_e, dq_b), (dk_e, dk_b), (dv_e, dv_b), rims, (dkg_e, dkg_b), (dvg_e, dvg_b), 1, half_pairs
    )
    kept_b, send_b = core_halves(grads_b, place)
    got_a, got_b = tied(late_a[1], core_swap(send_b))
    late_a = add_low(late_a[0], got_a)
    late_b = stream_blocks(add_low(kept_b, got_b), group_count).reshape(split)
    late_a, late_b, part_b = tied(late_a, late_b, part_b)
    keep_b, got_b = halved(late_b, order_x, 0)
    tokens_grad, glob_part, vectors = token_grad(
        (part_a, part_b), (glob_a, glob_b), tokens[0], grad_middle, w_qkv, norms, picked, glob_normed, second_sums,
        (vec_e, vec_a, vec_b), half_pairs, kept_rows,
    )
    got_b, glob_part, *received = tied(got_b, glob_part, *early[1:])
    early = summed_low([early[0]] + received)
    late_b = add_low(keep_b, got_b)
    for done in range(1, bits):
        late_b = add_low(*halved(late_b, order_x, done))
    gathered = exchange_raw(early, "stream")
    vec_rows = jnp.moveaxis(vectors.reshape(24, outer, 2 * kept_rows), 1, 0).astype(BF16)
    vec_flat = pad_rows(vec_rows, model_width)
    glob_blocks = glob_part.reshape(outer, -1, model_width)
    late = jnp.concatenate([late_a, late_b], axis=2)
    columns = late.shape[2]
    late_flat = flat_blocks(late, model_width)
    counts = [late_flat.shape[1], glob_blocks.shape[1], vec_flat.shape[1]]
    summed = exchange_parts(jnp.concatenate([late_flat, glob_blocks, vec_flat], axis=1), "seq", place // 2, 2)
    summed = tied(*summed, *gathered)
    gathered = ordered(jnp.stack(summed[outer:]), group)
    summed = summed_low(summed[:outer])
    late_piece = summed[: counts[0]]
    glob_piece = summed[counts[0] : counts[0] + counts[1]].reshape(2, -1, model_width)
    vec_piece = summed[counts[0] + counts[1] :]
    glob_send = lax.dynamic_index_in_dim(glob_piece, 1 - place % 2, 0, keepdims=False)
    glob_kept = lax.dynamic_index_in_dim(glob_piece, place % 2, 0, keepdims=False)
    every = exchange_raw(jnp.concatenate([late_piece, vec_piece], axis=0), "stream")
    glob_got = core_swap(glob_send)
    vec_sum = sum(rows[counts[0] :].astype(F32) for rows in every)
    vec_sum = vec_sum.reshape(-1)[: 24 * 2 * kept_rows].reshape(24, 2, kept_rows)
    vec_send = lax.dynamic_index_in_dim(vec_sum, 1 - place % 2, 1, keepdims=False)
    vec_own = lax.dynamic_index_in_dim(vec_sum, place % 2, 1, keepdims=False) + core_swap(vec_send)
    late = ordered(jnp.stack([rows[: counts[0]] for rows in every]), group)
    late = unflat_rows(late, kept_rows // group_count, columns).reshape(kept_rows, columns).astype(F32)
    grad_glob = glob_kept.astype(F32) + glob_got.astype(F32)
    own_glob, own_scale = norm_parts(global_states[0].astype(F32))
    glob_grad = norm_pull(grad_glob, own_glob, own_scale, first_gain).astype(BF16)

    part = half_pairs * 128
    share_qkv = jnp.concatenate(
        [late[:, (half * 3 + i) * part : (half * 3 + i + 1) * part] for i in range(3) for half in range(2)], axis=1
    )
    early = gathered.astype(F32)
    cuts = [0, piece_rows[0], piece_rows[0] + piece_rows[1], sum(piece_rows)]
    share_up = jnp.moveaxis(early[:, : cuts[1]].reshape(group_count, kept_rows, -1), 0, 1).reshape(kept_rows, -1)
    share_down = early[:, cuts[1] : cuts[2]].reshape(-1, model_width)
    share_out = early[:, cuts[2] :].reshape(-1, model_width)
    own_vectors = vec_own[:12]
    heads = vec_own[12 : 12 + pairs, :12]
    bias_grad = heads[:, :8].reshape(pairs, 2, 4).transpose(2, 0, 1).reshape(rich_bias.shape)
    theta_grad = heads[:, 8:].reshape(pairs, 2, 2).transpose(2, 0, 1).reshape(rich_theta.shape)
    return (
        layer_out[None],
        tokens_grad[None],
        glob_grad[None],
        share_qkv,
        share_out,
        share_up,
        share_down,
        own_vectors[0],
        own_vectors[1],
        own_vectors[2],
        own_vectors[3],
        own_vectors[4:8],
        own_vectors[8:12],
        bias_grad,
        theta_grad,
    )


def solution(mesh):
    return jax.shard_map(
        body,
        mesh=mesh,
        in_specs=(
            P("stream", "seq", None),
            P("stream", "seq", None),
            P("stream", "seq", None),
            P(),
            P(),
            P(),
            P(),
            P(),
            P(),
            P(),
            P(),
            P(),
            P(),
            P(),
            P(),
            P("stream", None),
            P("stream", None),
            P("stream", None, None),
            P("stream", None),
        ),
        out_specs=(
            P("stream", "seq", None),
            P("stream", "seq", None),
            P("stream", "seq", None),
            P("seq", None),
            P("seq", None),
            P("seq", None),
            P("seq", None),
            P("seq"),
            P("seq"),
            P("seq"),
            P("seq"),
            P(None, "seq"),
            P(None, "seq"),
            P(),
            P(),
        ),
        check_vma=False,
    )
```

```python
from functools import partial
import math

import jax
import jax.numpy as jnp
from jax import lax
from jax.experimental import pallas as pl
from jax.experimental.pallas import tpu as pltpu
from jax.sharding import PartitionSpec as P

RADIUS = 128
GLOB_FORM = 64
QBLOCK = 512
TOK_DEV = 1024


EPSILON = 1e-06


TILE = 128
SPAN = 384
LOG2E = math.log2(math.e)
FAR_AWAY = 1e15
CH = 128
UNROLL = 6
BACK_CH = 128
BACK_UNROLL = 3
F32 = jnp.float32
BF16 = jnp.bfloat16
VMEM_LIMIT = 58 * 1024 * 1024


def mm(a, b):
    return lax.dot_general(a, b, (((1,), (0,)), ((), ())), preferred_element_type=F32)


def mm_nt(a, b):
    return lax.dot_general(a, b, (((1,), (1,)), ((), ())), preferred_element_type=F32)


def mm_tn(a, b):
    return lax.dot_general(a, b, (((0,), (0,)), ((), ())), preferred_element_type=F32)


def norm_parts(values):
    centre = jnp.mean(values, axis=-1, keepdims=True)
    centred = values - centre
    spread = jnp.mean(centred * centred, axis=-1, keepdims=True)
    scale = lax.rsqrt(spread + EPSILON)
    return centred * scale, scale


def norm_pull(grad, normed, scale, gain):
    e = grad * gain
    mean_e = jnp.mean(e, axis=-1, keepdims=True)
    mean_en = jnp.mean(e * normed, axis=-1, keepdims=True)
    return scale * (e - mean_e - normed * mean_en)


def split3(values):
    hi = values.astype(BF16).astype(F32)
    rest = values - hi
    mid = rest.astype(BF16).astype(F32)
    return hi, mid, rest - mid


def half_masks(dtype):
    lane = lax.broadcasted_iota(jnp.int32, (1, 128), 1)
    low = (lane < 64).astype(F32)
    return low.astype(dtype), (1.0 - low).astype(dtype)


def by_row(values):
    row = lax.broadcasted_iota(jnp.int32, (8, 128), 0)
    out = jnp.full((8, 128), values[7], F32)
    for index in range(7):
        out = jnp.where(row == index, values[index], out)
    return out


def rich_rows(vectors, scales):
    row = lax.broadcasted_iota(jnp.int32, (8, 128), 0)
    lane = lax.broadcasted_iota(jnp.int32, (8, 128), 1)
    both = jnp.concatenate([vectors, vectors], axis=0)
    both = both if scales is None else both * scales
    return jnp.where((row < 4) == (lane < 64), both, 0.0)


def rich_sums(qp, kp, query_vec, key_vec, scales, bias8):
    rq = jnp.concatenate(split3(rich_rows(query_vec, scales)), axis=1).astype(BF16)
    rk = jnp.concatenate(split3(rich_rows(key_vec, scales)), axis=0).astype(BF16)
    a = mm_nt(jnp.concatenate([qp, qp, qp], axis=1), rq)
    b24 = mm_nt(rk, kp)
    return a, b24[0:8] + b24[8:16] + b24[16:24] + bias8[:, 0:1]


def form_of(units_ref, lengths_ref, row):
    form, low, high, before = 0, 0, lengths_ref[0, 0], 0
    for index in range(1, units_ref.shape[1]):
        before = before + units_ref[0, index - 1]
        start = TOK_DEV // 2 + TOK_DEV * before
        taken = row >= start
        form = jnp.where(taken, index, form)
        low = jnp.where(taken, start, low)
        high = jnp.where(taken, start + lengths_ref[0, index], high)
    return form, low, high


def coord_row(coords_ref, axis, tile_index):
    tile_index = jnp.clip(tile_index, 0, coords_ref.shape[1] // 128 - 1)
    return coords_ref[axis : axis + 1, pl.ds(pl.multiple_of(tile_index * 128, 128), 128)].astype(F32)


def query_columns(coords_ref, axis, tile_index):
    return jnp.transpose(jnp.broadcast_to(coord_row(coords_ref, axis, tile_index), (128, 128)))


def geometry_into(coords_ref, first_tile, span, refs):
    ox_ref, oy_ref, dx_ref, dy_ref = refs
    xq = query_columns(coords_ref, 0, first_tile + 1)
    yq = query_columns(coords_ref, 1, first_tile + 1)
    for lt in range(3):
        xk = coord_row(coords_ref, 0, first_tile + lt)
        yk = coord_row(coords_ref, 1, first_tile + lt)
        out = (slice(None), slice(lt * 128, lt * 128 + 128))
        dx = jnp.log(1.0 + jnp.abs(xq - xk))
        dy = jnp.log(1.0 + jnp.abs(yq - yk))
        if span is not None:
            row = lax.broadcasted_iota(jnp.int32, (128, 128), 0)
            col = lax.broadcasted_iota(jnp.int32, (128, 128), 1) + lt * 128
            near = (col >= row) & (col - row <= 2 * RADIUS)
            dx = jnp.where(near & (col >= span[0]) & (col < span[1]), dx, FAR_AWAY)
            ox_ref[out] = jnp.where(xk > xq, 1.0, -1.0)
            oy_ref[out] = jnp.where(yk > yq, 1.0, -1.0)
        dx_ref[out] = dx
        dy_ref[out] = dy


def qkv_kernel(tok_ref, w_ref, norms_ref, q_ref, k_ref, v_ref, ht_ref):
    width = tok_ref.shape[1]
    normed, _ = norm_parts(tok_ref[...].astype(F32))
    hidden = (normed * norms_ref[0:1, :] + norms_ref[1:2, :]).astype(BF16)
    for index, out in enumerate((q_ref, k_ref, v_ref)):
        out[...] = mm(hidden, w_ref[:, index * width : (index + 1) * width]).astype(BF16)
    ht_ref[...] = jnp.transpose(hidden)


def project_tokens(tokens, w_qkv, norms):
    rows, width = tokens.shape
    step = 256
    block = pl.BlockSpec((step, width), lambda i: (i, 0))
    return pl.pallas_call(
        qkv_kernel,
        grid=(rows // step,),
        in_specs=[block, pl.BlockSpec(w_qkv.shape, lambda i: (0, 0)), pl.BlockSpec(norms.shape, lambda i: (0, 0))],
        out_specs=[block, block, block, pl.BlockSpec((width, step), lambda i: (0, i))],
        out_shape=[jax.ShapeDtypeStruct((rows, width), BF16)] * 3 + [jax.ShapeDtypeStruct((width, rows), BF16)],
        compiler_params=pltpu.CompilerParams(vmem_limit_bytes=VMEM_LIMIT),
        cost_estimate=cost(8.0),
        name="project_tokens",
    )(tokens, w_qkv, norms)


def cost(micros):
    return pl.CostEstimate(flops=int(micros * 1e9), bytes_accessed=0, transcendentals=0)


def global_pairs(form, owner_ref, glob_ref, norms_ref, kw_ref, vw_ref, kg_ref, vg_ref, hg_ref, ng_ref, oh_ref):
    count = glob_ref.shape[0]
    match = (owner_ref[...] == form).astype(F32)
    row = lax.broadcasted_iota(jnp.int32, (count, count), 0)
    col = lax.broadcasted_iota(jnp.int32, (count, count), 1)
    upto = (row <= col).astype(F32).astype(BF16)
    rank = mm(jnp.broadcast_to(match, (16, count)).astype(BF16), upto)[0:1]
    slot = lax.broadcasted_iota(jnp.int32, (GLOB_FORM, count), 0).astype(F32) + 1.0
    picked = jnp.where(rank == slot, match, 0.0).astype(BF16)
    oh_ref[0] = picked
    normed, _ = norm_parts(mm(picked, glob_ref[...]))
    ng_ref[0] = normed
    hidden = (normed * norms_ref[0:1, :] + norms_ref[1:2, :]).astype(BF16)
    hg_ref[0] = hidden
    kg_ref[0] = mm(hidden, kw_ref[...]).astype(BF16)
    vg_ref[0] = mm(hidden, vw_ref[...]).astype(BF16)


def fwd_kernel(units_ref, lengths_ref, offset_ref, bias_ref, theta_ref,
               q_ref, k_ref, v_ref, before_ref, after_ref, glob_ref, owner_ref, kw_ref, vw_ref, norms_ref,
               coords_ref, rq_ref, rk_ref,
               ctx_ref, pn_ref, pf_ref, g0_ref, g1_ref, kp_ref, vp_ref, kg_ref, vg_ref, hg_ref, ng_ref, oh_ref,
               ox_ref, oy_ref, dx_ref, dy_ref, s_ref, sf_ref, a_ref, b_ref, *, pairs, per_block):
    t = pl.program_id(0)
    rows_all = k_ref.shape[0]
    offset = offset_ref[0, 0]
    first = offset + t * TILE
    form, low_end, high_end = form_of(units_ref, lengths_ref, first)

    @pl.when(t == 0)
    def _():
        for refs in ((k_ref, kp_ref, kw_ref), (v_ref, vp_ref, vw_ref)):
            own, padded_ref, weight = refs
            padded_ref[RADIUS : RADIUS + rows_all, :] = own[...]
        for halo, start in ((before_ref, 0), (after_ref, RADIUS + rows_all)):
            normed, _ = norm_parts(halo[...].astype(F32))
            hidden = (normed * norms_ref[0:1, :] + norms_ref[1:2, :]).astype(BF16)
            kp_ref[start : start + RADIUS, :] = mm(hidden, kw_ref[...]).astype(BF16)
            vp_ref[start : start + RADIUS, :] = mm(hidden, vw_ref[...]).astype(BF16)

    @pl.when(t % per_block == 0)
    def _():
        global_pairs(form, owner_ref, glob_ref, norms_ref, kw_ref, vw_ref, kg_ref, vg_ref, hg_ref, ng_ref, oh_ref)

    shifted = first - RADIUS
    geometry_into(coords_ref, offset // 128 + t - 1, (low_end - shifted, high_end - shifted), (ox_ref, oy_ref, dx_ref, dy_ref))
    lo16, hi16 = half_masks(BF16)
    lane = lax.broadcasted_iota(jnp.int32, (CH, 128), 1)
    low = lane < 64
    rows = pl.ds(pl.multiple_of(t * TILE, TILE), SPAN)
    root = math.sqrt(0.5 * LOG2E)

    def widths_of(p):
        return [[theta_ref[i, 2 * p + e] * root for i in range(2)] for e in range(2)]

    def scores(p, slot):
        cols = pl.ds(pl.multiple_of(p * 128, 128), 128)
        qp = q_ref[:, cols]
        kp = kp_ref[rows, cols]
        kgp = kg_ref[0, :, cols]
        widths = widths_of(p)
        scales = by_row([LOG2E, LOG2E] + widths[0] + [LOG2E, LOG2E] + widths[1])
        biases = by_row([bias_ref[c, 2 * p + e] for e in range(2) for c in range(4)]) * scales
        s_ref[slot] = mm_nt(jnp.concatenate([qp * lo16, qp * hi16], axis=0), kp)
        sf_ref[slot] = mm_nt(qp, jnp.concatenate([kgp * lo16, kgp * hi16], axis=0))
        a, b = rich_sums(qp, kp, rq_ref[:, cols], rk_ref[:, cols], scales, biases)
        a_ref[slot] = a
        b_ref[slot] = b

    def weights(p, slot):
        widths = widths_of(p)
        for r in range(0, TILE, CH):
            rs = slice(r, r + CH)
            far = sf_ref[slot, rs, :] * (0.125 * LOG2E)
            tops = []
            held = []
            for e in range(2):
                base = 4 * e
                part = [a_ref[slot, rs, base + c : base + c + 1] for c in range(4)]
                line = [b_ref[slot, base + c : base + c + 1, :] for c in range(4)]
                u0 = (part[0] + line[0]) * ox_ref[rs, :]
                u1 = (part[1] + line[1]) * oy_ref[rs, :]
                e0 = jnp.exp2(jnp.minimum(u0, -u0))
                e1 = jnp.exp2(jnp.minimum(u1, -u1))
                r0 = 1.0 / (1.0 + e0)
                r1 = 1.0 / (1.0 + e1)
                gx = (widths[e][0] * dx_ref[rs, :] - part[2]) - line[2]
                gy = (widths[e][1] * dy_ref[rs, :] - part[3]) - line[3]
                s = s_ref[slot, e * TILE + r : e * TILE + r + CH, :] * (0.125 * LOG2E)
                s = s + jnp.minimum(u0, 0.0) + jnp.minimum(u1, 0.0) - gx * gx - gy * gy
                top = jnp.maximum(jnp.maximum(s[:, 0:128], s[:, 128:256]), s[:, 256:384])
                here = low if e == 0 else ~low
                top = jnp.maximum(top, jnp.where(here, far, -3e38))
                tops.append(jnp.max(top, axis=1, keepdims=True))
                g0 = jnp.where(u0 >= 0.0, e0, 1.0) * (ox_ref[rs, :] * r0)
                g1 = jnp.where(u1 >= 0.0, e1, 1.0) * (oy_ref[rs, :] * r1)
                g0_ref[0, 2 * p + e, rs, :] = g0.astype(BF16)
                g1_ref[0, 2 * p + e, rs, :] = g1.astype(BF16)
                held.append((s, r0 * r1))
            pfar = jnp.exp2(far - jnp.where(low, tops[0], tops[1]))
            invs = []
            for e in range(2):
                s, rr = held[e]
                pe = jnp.exp2(s - tops[e]) * rr
                here = low if e == 0 else ~low
                tot = pe[:, 0:128] + pe[:, 128:256] + pe[:, 256:384] + jnp.where(here, pfar, 0.0)
                inv = 1.0 / jnp.sum(tot, axis=1, keepdims=True)
                invs.append(inv)
                pn_ref[0, 2 * p + e, rs, :] = (pe * inv).astype(BF16)
            pf_ref[0, p, rs, :] = (pfar * jnp.where(low, invs[0], invs[1])).astype(BF16)

    def context(p):
        cols = pl.ds(pl.multiple_of(p * 128, 128), 128)
        vp = vp_ref[rows, cols]
        vgp = vg_ref[0, :, cols]
        ctx = mm(pn_ref[0, 2 * p], vp * lo16) + mm(pn_ref[0, 2 * p + 1], vp * hi16)
        ctx = ctx + mm(pf_ref[0, p], jnp.concatenate([vgp * lo16, vgp * hi16], axis=0))
        ctx_ref[:, cols] = ctx.astype(BF16)

    def group(index, carry):
        first = index * UNROLL
        for u in range(UNROLL):
            scores(first + u, u)
        for u in range(UNROLL):
            weights(first + u, u)
        for u in range(UNROLL):
            context(first + u)
        return carry

    lax.fori_loop(0, pairs // UNROLL, group, 0)


def attn_forward(q, k, v, before, after, every_glob, owner, w_qkv, norms, coords, units, lengths, offset, rich):
    rich_query, rich_key, rich_bias, rich_theta = rich
    rows, width = q.shape
    heads = rich_bias.shape[1]
    pairs = heads // 2
    tiles = rows // TILE
    blocks = rows // QBLOCK
    per_block = tiles // blocks
    padded_rows = rows + 2 * RADIUS
    globs = every_glob.shape[0]
    scalars = pl.BlockSpec(memory_space=pltpu.SMEM)

    def whole(*shape):
        return pl.BlockSpec(shape, lambda t: (0,) * len(shape))

    def block3(*shape):
        return pl.BlockSpec((1,) + shape, lambda t: (t // per_block, 0, 0))

    near = pl.BlockSpec((1, heads, TILE, SPAN), lambda t: (t, 0, 0, 0))
    near_shape = jax.ShapeDtypeStruct((tiles, heads, TILE, SPAN), BF16)
    tile_rows = pl.BlockSpec((TILE, width), lambda t: (t, 0))
    return pl.pallas_call(
        partial(fwd_kernel, pairs=pairs, per_block=per_block),
        grid=(tiles,),
        in_specs=[
            scalars, scalars, scalars, scalars, scalars,
            tile_rows, whole(rows, width), whole(rows, width),
            whole(RADIUS, width), whole(RADIUS, width),
            whole(globs, width), whole(1, globs),
            pl.BlockSpec((width, width), lambda t: (0, 1)),
            pl.BlockSpec((width, width), lambda t: (0, 2)),
            whole(*norms.shape),
            whole(*coords.shape), whole(4, width), whole(4, width),
        ],
        out_specs=[
            tile_rows, near,
            pl.BlockSpec((1, pairs, TILE, 128), lambda t: (t, 0, 0, 0)),
            near, near,
            whole(padded_rows, width), whole(padded_rows, width),
            block3(GLOB_FORM, width), block3(GLOB_FORM, width), block3(GLOB_FORM, width),
            block3(GLOB_FORM, width), block3(GLOB_FORM, globs),
        ],
        out_shape=[
            jax.ShapeDtypeStruct((rows, width), BF16),
            near_shape,
            jax.ShapeDtypeStruct((tiles, pairs, TILE, 128), BF16),
            near_shape, near_shape,
            jax.ShapeDtypeStruct((padded_rows, width), BF16),
            jax.ShapeDtypeStruct((padded_rows, width), BF16),
            jax.ShapeDtypeStruct((blocks, GLOB_FORM, width), BF16),
            jax.ShapeDtypeStruct((blocks, GLOB_FORM, width), BF16),
            jax.ShapeDtypeStruct((blocks, GLOB_FORM, width), BF16),
            jax.ShapeDtypeStruct((blocks, GLOB_FORM, width), F32),
            jax.ShapeDtypeStruct((blocks, GLOB_FORM, globs), BF16),
        ],
        scratch_shapes=[
            pltpu.VMEM((TILE, SPAN), F32), pltpu.VMEM((TILE, SPAN), F32),
            pltpu.VMEM((TILE, SPAN), F32), pltpu.VMEM((TILE, SPAN), F32),
            pltpu.VMEM((UNROLL, 2 * TILE, SPAN), F32), pltpu.VMEM((UNROLL, TILE, 128), F32),
            pltpu.VMEM((UNROLL, TILE, 8), F32), pltpu.VMEM((UNROLL, 8, SPAN), F32),
        ],
        compiler_params=pltpu.CompilerParams(vmem_limit_bytes=VMEM_LIMIT),
        cost_estimate=cost(65.0),
        name="attn_forward",
    )(units, lengths, offset, rich_bias, rich_theta, q, k, v, before, after, every_glob, owner,
      w_qkv, w_qkv, norms, coords, rich_query, rich_key)


def bwd_kernel(offset_ref, bias_ref, theta_ref,
               q_ref, dc_ref, ctx_ref, k_ref, v_ref, kg_ref, vg_ref, coords_ref, rq_ref, rk_ref,
               pn_ref, pf_ref, g0_ref, g1_ref,
               dq_ref, dk_ref, dv_ref, dkg_ref, dvg_ref, vec_ref, rim_ref,
               dx_ref, dy_ref, dp_ref, dpf_ref, ds_ref, dsf_ref, a_ref, b_ref, dqr_ref, db_ref, db_now,
               *, pairs, first_pair, tiles, per_block, edge):
    step = pl.program_id(0)
    t = step * (tiles - 1) if edge else step + 1

    @pl.when(step == 0)
    def _():
        vec_ref[...] = jnp.zeros_like(vec_ref)
        if not edge:
            rim_ref[...] = jnp.zeros_like(rim_ref)
            dk_ref[...] = jnp.zeros_like(dk_ref)
            dv_ref[...] = jnp.zeros_like(dv_ref)
            db_ref[...] = jnp.zeros_like(db_ref)

    if edge:
        fresh = step >= 0
    else:
        fresh = (step == 0) | (t % per_block == 0)

    @pl.when(fresh)
    def _():
        dkg_ref[...] = jnp.zeros_like(dkg_ref)
        dvg_ref[...] = jnp.zeros_like(dvg_ref)

    geometry_into(coords_ref, offset_ref[0, 0] // 128 + t - 1, None, (None, None, dx_ref, dy_ref))
    lo16, hi16 = half_masks(BF16)
    low64 = lax.broadcasted_iota(jnp.int32, (64, 128), 1) < 64
    lane8 = lax.broadcasted_iota(jnp.int32, (4, 128), 1)
    lane1 = lax.broadcasted_iota(jnp.int32, (1, 128), 1)
    sub = lax.broadcasted_iota(jnp.int32, (128, 1), 0)
    lo16c = (sub < 64).astype(F32).astype(BF16)
    hi16c = (sub >= 64).astype(F32).astype(BF16)
    rows = pl.ds(pl.multiple_of(t * TILE, TILE), SPAN)
    out_rows = pl.ds(pl.multiple_of((t - 1) * TILE, TILE), SPAN)

    def rich_key_parts(p, cols, sums, keys, columns):
        head = 2 * (p + first_pair)
        squares = [theta_ref[i, head + e] * theta_ref[i, head + e] for e in range(2) for i in range(2)]
        scales = by_row([1.0, 1.0, squares[0], squares[1], 1.0, 1.0, squares[2], squares[3]])
        scaled = sums * scales[:, 0:1]
        vectors = jnp.concatenate(split3(rich_rows(rk_ref[:, cols], None)), axis=0)
        parts = split3(scaled)
        left = jnp.concatenate([vectors[0:8]] * 3 + [vectors[8:16]] * 2 + [vectors[16:24]], axis=0)
        left = jnp.transpose(left).astype(BF16)
        right = jnp.concatenate([parts[0], parts[1], parts[2], parts[0], parts[1], parts[0]], axis=0).astype(BF16)
        extra = mm(left, right)
        stacked = jnp.concatenate(parts, axis=0).astype(BF16)
        key24 = mm(stacked, keys)
        key8 = key24[0:8] + key24[8:16] + key24[16:24]
        vec_ref[p, 4:8, :] += jnp.where(lane8 < 64, key8[0:4], key8[4:8])
        totals = jnp.sum(scaled, axis=1, keepdims=True)
        line = jnp.zeros((1, 128), F32)
        for index in range(8):
            line = jnp.where(lane1 == index, totals[index : index + 1, :], line)
        vec_ref[p, 8:9, :] += line
        return extra

    low_rows = lax.broadcasted_iota(jnp.int32, (BACK_CH, 128), 1) < 64

    def fold(full):
        return jnp.sum(full.reshape(full.shape[0] // 8, 8, full.shape[1]), axis=0)

    def pair_parts(p):
        cols = pl.ds(pl.multiple_of(p * 128, 128), 128)
        head = 2 * (p + first_pair)
        squares = [[theta_ref[i, head + e] * theta_ref[i, head + e] for i in range(2)] for e in range(2)]
        halves = [jnp.where(lane1 < 64, squares[0][i], squares[1][i]) for i in range(2)]
        return cols, head, halves

    def products(p, slot):
        cols, head, _ = pair_parts(p)
        qp = q_ref[:, cols]
        dcp = dc_ref[:, cols]
        kp = k_ref[rows, cols]
        vgp = vg_ref[0, :, cols]
        dp_ref[slot] = mm_nt(jnp.concatenate([dcp * lo16, dcp * hi16], axis=0), v_ref[rows, cols])
        dpf_ref[slot] = mm_nt(dcp, jnp.concatenate([vgp * lo16, vgp * hi16], axis=0))
        biases = by_row([bias_ref[c, head + e] for e in range(2) for c in range(4)])
        a, b = rich_sums(qp, kp, rq_ref[:, cols], rk_ref[:, cols], None, biases)
        a_ref[slot] = a
        b_ref[slot] = b

    def elements(p, slot):
        cols, head, halves = pair_parts(p)
        lines = [rq_ref[0:1, cols], rq_ref[1:2, cols], rq_ref[2:3, cols] * halves[0], rq_ref[3:4, cols] * halves[1]]
        col_sums = [[jnp.zeros((8, SPAN), F32) for _ in range(4)] for _ in range(2)]
        thetas = [[jnp.zeros((8, 128), F32) for _ in range(2)] for _ in range(2)]
        query_sums = [jnp.zeros((8, 128), F32) for _ in range(4)]
        for r in range(0, TILE, BACK_CH):
            rs = slice(r, r + BACK_CH)
            prod = dc_ref[rs, cols].astype(F32) * ctx_ref[rs, cols].astype(F32)
            row_sums = []
            dots = []
            for e in range(2):
                here = low_rows if e == 0 else ~low_rows
                base = 4 * e
                dot = jnp.sum(jnp.where(here, prod, 0.0), axis=1, keepdims=True)
                dots.append(dot)
                es = slice(e * TILE + r, e * TILE + r + BACK_CH)
                ds = pn_ref[0, 2 * p + e, rs, :].astype(F32) * (dp_ref[slot, es, :] - dot)
                ds_ref[slot, es, :] = ds.astype(BF16)
                t0 = ds * g0_ref[0, 2 * p + e, rs, :].astype(F32)
                t1 = ds * g1_ref[0, 2 * p + e, rs, :].astype(F32)
                gx = (dx_ref[rs, :] - a_ref[slot, rs, base + 2 : base + 3]) - b_ref[slot, base + 2 : base + 3, :]
                gy = (dy_ref[rs, :] - a_ref[slot, rs, base + 3 : base + 4]) - b_ref[slot, base + 3 : base + 4, :]
                tx = ds * gx
                ty = ds * gy
                for i, full in enumerate((tx * gx, ty * gy)):
                    thetas[e][i] = thetas[e][i] + fold(full[:, 0:128] + full[:, 128:256] + full[:, 256:384])
                sums = []
                for c, full in enumerate((t0, t1, tx, ty)):
                    col_sums[e][c] = col_sums[e][c] + fold(full)
                    sums.append(jnp.sum(full[:, 0:128] + full[:, 128:256] + full[:, 256:384], axis=1, keepdims=True))
                row_sums.append(sums)
            dsf = pf_ref[0, p, rs, :].astype(F32) * (dpf_ref[slot, rs, :] - jnp.where(low_rows, dots[0], dots[1]))
            dsf_ref[slot, rs, :] = dsf.astype(BF16)
            qf = q_ref[rs, cols].astype(F32)
            dqr = jnp.zeros((BACK_CH, 128), F32)
            for c in range(4):
                da = jnp.where(low_rows, row_sums[0][c], row_sums[1][c])
                dqr = dqr + da * lines[c]
                query_sums[c] = query_sums[c] + fold(da * qf)
            dqr_ref[slot, rs, :] = dqr
        folded = jnp.concatenate([jnp.sum(query_sums[c], axis=0, keepdims=True) for c in range(4)], axis=0)
        scale4 = jnp.concatenate([jnp.ones((2, 128), F32), halves[0], halves[1]], axis=0)
        vec_ref[p, 0:4, :] += folded * scale4
        line = jnp.zeros((1, 128), F32)
        for e in range(2):
            for i in range(2):
                total = jnp.sum(jnp.sum(thetas[e][i], axis=0, keepdims=True), axis=1, keepdims=True)
                line = jnp.where(lane1 == 8 + 2 * e + i, total * (-theta_ref[i, head + e]), line)
        vec_ref[p, 8:9, :] += line
        db_now[slot] = jnp.concatenate([jnp.sum(col_sums[e][c], axis=0, keepdims=True) for e in range(2) for c in range(4)], axis=0)

    def results(p, slot):
        cols, head, _ = pair_parts(p)
        qp = q_ref[:, cols]
        dcp = dc_ref[:, cols]
        kp = k_ref[rows, cols]
        kgp = kg_ref[0, :, cols]
        packed = db_now[slot]
        dq = mm(ds_ref[slot, 0:TILE, :], kp * lo16) + mm(ds_ref[slot, TILE : 2 * TILE, :], kp * hi16)
        dq = dq + mm(dsf_ref[slot], jnp.concatenate([kgp * lo16, kgp * hi16], axis=0))
        dq_ref[:, cols] = (dq * 0.125 + dqr_ref[slot]).astype(BF16)
        qT = jnp.transpose(qp)
        dcT = jnp.transpose(dcp)
        dk = mm(jnp.concatenate([qT * lo16c, qT * hi16c], axis=1), ds_ref[slot]) * 0.125
        dv = mm(dcT * lo16c, pn_ref[0, 2 * p]) + mm(dcT * hi16c, pn_ref[0, 2 * p + 1])
        if edge:
            dk = dk + rich_key_parts(p, cols, packed, kp, rows)
            dk_ref[0, cols, :] = dk
            dv_ref[0, cols, :] = dv
            for index, full in enumerate((dk, dv)):
                rim = jnp.where(step == 0, full[:, 0:RADIUS], full[:, SPAN - RADIUS : SPAN])
                rim_ref[0, index, cols, :] = rim.astype(BF16)
        else:
            dk_ref[cols, out_rows] += dk
            dv_ref[cols, out_rows] += dv
            db_ref[p, :, out_rows] += packed
        dkg2 = mm(jnp.transpose(dsf_ref[slot]), qp) * 0.125
        dvg2 = mm(jnp.transpose(pf_ref[0, p]), dcp)
        dkg_ref[0, :, cols] += jnp.where(low64, dkg2[0:64], dkg2[64:128])
        dvg_ref[0, :, cols] += jnp.where(low64, dvg2[0:64], dvg2[64:128])

    def group(index, carry):
        first = index * BACK_UNROLL
        for stage in (products, elements, results):
            for u in range(BACK_UNROLL):
                stage(first + u, u)
        return carry

    lax.fori_loop(0, pairs // BACK_UNROLL, group, 0)

    if not edge:

        @pl.when(step == pl.num_programs(0) - 1)
        def _():
            own = k_ref.shape[0] - 2 * RADIUS

            def finish(p, carry):
                cols = pl.ds(pl.multiple_of(p * 128, 128), 128)
                keys = k_ref[RADIUS : RADIUS + own, cols]
                dk_ref[cols, :] += rich_key_parts(p, cols, db_ref[p], keys, None)
                return carry

            lax.fori_loop(0, pairs, finish, 0)


def attn_backward(q, dctx, ctx, k_pad, v_pad, kg, vg, coords, offset, rich, kept, first_pair, pairs, edge):
    rich_query, rich_key, rich_bias, rich_theta = rich
    rows, width = q.shape
    tiles = rows // TILE
    blocks = kg.shape[0]
    per_block = tiles // blocks
    part = pairs * 128
    half = first_pair // pairs
    steps = 2 if edge else tiles - 2
    padded_rows = k_pad.shape[0]
    scalars = pl.BlockSpec(memory_space=pltpu.SMEM)

    def tile(i):
        return i * (tiles - 1) if edge else i + 1

    tile_rows = pl.BlockSpec((TILE, part), lambda i: (tile(i), half))
    padded_cols = pl.BlockSpec((padded_rows, part), lambda i: (0, half))
    block3 = pl.BlockSpec((1, GLOB_FORM, part), lambda i: (tile(i) // per_block, 0, half))
    out3 = pl.BlockSpec((1, GLOB_FORM, part), lambda i: (tile(i) // per_block, 0, 0))
    vectors = pl.BlockSpec((4, part), lambda i: (0, half))
    near = pl.BlockSpec((1, 2 * pairs, TILE, SPAN), lambda i: (tile(i), half, 0, 0))
    far = pl.BlockSpec((1, pairs, TILE, 128), lambda i: (tile(i), half, 0, 0))
    if edge:
        key_out = pl.BlockSpec((1, part, SPAN), lambda i: (i, 0, 0))
        key_shape = jax.ShapeDtypeStruct((2, part, SPAN), F32)
        rim_out = pl.BlockSpec((1, 2, part, RADIUS), lambda i: (i, 0, 0, 0))
        rim_shape = jax.ShapeDtypeStruct((2, 2, part, RADIUS), BF16)
    else:
        key_out = pl.BlockSpec((part, rows), lambda i: (0, 0))
        key_shape = jax.ShapeDtypeStruct((part, rows), F32)
        rim_out = pl.BlockSpec((1, 2, 16, RADIUS), lambda i: (0, 0, 0, 0))
        rim_shape = jax.ShapeDtypeStruct((1, 2, 16, RADIUS), BF16)
    glob_shape = jax.ShapeDtypeStruct((blocks, GLOB_FORM, part), F32)
    return pl.pallas_call(
        partial(bwd_kernel, pairs=pairs, first_pair=first_pair, tiles=tiles, per_block=per_block, edge=edge),
        grid=(steps,),
        in_specs=[
            scalars, scalars, scalars,
            tile_rows, tile_rows, tile_rows, padded_cols, padded_cols, block3, block3,
            pl.BlockSpec(coords.shape, lambda i: (0, 0)), vectors, vectors,
            near, far, near, near,
        ],
        out_specs=[
            pl.BlockSpec((TILE, part), lambda i: (i, 0)),
            key_out, key_out, out3, out3,
            pl.BlockSpec((pairs, 16, 128), lambda i: (0, 0, 0)),
            rim_out,
        ],
        out_shape=[
            jax.ShapeDtypeStruct((steps * TILE, part), BF16),
            key_shape, key_shape, glob_shape, glob_shape,
            jax.ShapeDtypeStruct((pairs, 16, 128), F32),
            rim_shape,
        ],
        scratch_shapes=[
            pltpu.VMEM((TILE, SPAN), F32), pltpu.VMEM((TILE, SPAN), F32),
            pltpu.VMEM((BACK_UNROLL, 2 * TILE, SPAN), F32), pltpu.VMEM((BACK_UNROLL, TILE, 128), F32),
            pltpu.VMEM((BACK_UNROLL, 2 * TILE, SPAN), BF16), pltpu.VMEM((BACK_UNROLL, TILE, 128), BF16),
            pltpu.VMEM((BACK_UNROLL, TILE, 8), F32), pltpu.VMEM((BACK_UNROLL, 8, SPAN), F32),
            pltpu.VMEM((BACK_UNROLL, TILE, 128), F32), pltpu.VMEM((pairs, 8, rows), F32),
            pltpu.VMEM((BACK_UNROLL, 8, SPAN), F32),
        ],
        compiler_params=pltpu.CompilerParams(vmem_limit_bytes=VMEM_LIMIT),
        cost_estimate=cost(8.2 * steps * pairs / 6),
        name="attn_backward_edge" if edge else "attn_backward_mid",
    )(offset, rich_bias, rich_theta, q, dctx, ctx, k_pad, v_pad, kg, vg, coords, rich_query, rich_key, *kept)


FF_CHUNK = 512
ROW_CHUNK = 512

TAIL_SLOPE = 0.35
TAIL = (0.0987331438, 0.0987265523, 0.092954664, 0.0773361877, 0.0814717893, -0.00727472285, 0.100604539, -0.0425525649)


def gelu_pair(values):
    t = 1.0 / (1.0 + (TAIL_SLOPE * math.sqrt(0.5)) * jnp.abs(values))
    poly = TAIL[-1] * t + TAIL[-2]
    for coef in TAIL[-3::-1]:
        poly = poly * t + coef
    bell = jnp.exp2((values * values) * (-0.5 * LOG2E))
    tail = t * poly * bell
    phi = jnp.where(values >= 0.0, 1.0 - tail, tail)
    return values * phi, phi + (values * bell) * (1.0 / math.sqrt(2.0 * math.pi))


def ffn_kernel(tok_ref, ctx_ref, ct_ref, wo_ref, wu_ref, wd_ref, norms_ref,
               out_ref, dmid_ref, dctx_ref, wog_ref, wug_ref, wdg_ref, vec_ref,
               mid_ref, h2_ref, h2t_ref, acc_ref, dh_ref, act_ref, dpre_ref, *, rows):
    step = pl.program_id(0)
    last = pl.num_programs(0) - 1

    @pl.when(step == 0)
    def _():
        @pl.loop(0, rows // ROW_CHUNK)
        def _(index):
            rs = pl.ds(pl.multiple_of(index * ROW_CHUNK, ROW_CHUNK), ROW_CHUNK)
            mid = tok_ref[rs, :].astype(F32) + mm(ctx_ref[rs, :], wo_ref[...])
            mid_ref[rs, :] = mid
            normed, _ = norm_parts(mid)
            h2 = (normed * norms_ref[2:3, :] + norms_ref[3:4, :]).astype(BF16)
            h2_ref[rs, :] = h2
            h2t_ref[:, rs] = jnp.transpose(h2)
            acc_ref[rs, :] = jnp.zeros_like(mid)
            dh_ref[rs, :] = jnp.zeros_like(mid)

    @pl.loop(0, rows // ROW_CHUNK)
    def _(index):
        rs = pl.ds(pl.multiple_of(index * ROW_CHUNK, ROW_CHUNK), ROW_CHUNK)
        pre = mm(h2_ref[rs, :], wu_ref[...])
        dact = mm_nt(ct_ref[rs, :], wd_ref[...])
        act, slope = gelu_pair(pre)
        act_ref[rs, :] = act.astype(BF16)
        dpre_ref[rs, :] = (dact * slope).astype(BF16)
        acc_ref[rs, :] += mm(act_ref[rs, :], wd_ref[...])
        dh_ref[rs, :] += mm_nt(dpre_ref[rs, :], wu_ref[...])
    wug_ref[...] = mm(h2t_ref[...], dpre_ref[...]).astype(BF16)
    wdg_ref[...] = mm_tn(act_ref[...], ct_ref[...]).astype(BF16)

    @pl.when(step == last)
    def _():
        def finish(index, sums):
            rs = pl.ds(pl.multiple_of(index * ROW_CHUNK, ROW_CHUNK), ROW_CHUNK)
            mid = mid_ref[rs, :]
            out_ref[rs, :] = (mid + acc_ref[rs, :]).astype(BF16)
            normed, scale = norm_parts(mid)
            dh = dh_ref[rs, :]
            gains = sums[0] + jnp.sum((dh * normed).reshape(ROW_CHUNK // 8, 8, -1), axis=0)
            shifts = sums[1] + jnp.sum(dh.reshape(ROW_CHUNK // 8, 8, -1), axis=0)
            dmid = ct_ref[rs, :].astype(F32) + norm_pull(dh, normed, scale, norms_ref[2:3, :])
            dmid_ref[rs, :] = dmid
            dattn = dmid.astype(BF16)
            h2_ref[rs, :] = dattn
            dctx_ref[rs, :] = mm_nt(dattn, wo_ref[...]).astype(BF16)
            return gains, shifts

        start = jnp.zeros((8, norms_ref.shape[1]), F32)
        gains, shifts = lax.fori_loop(0, rows // ROW_CHUNK, finish, (start, start))
        wog_ref[...] = mm_tn(ctx_ref[...], h2_ref[...]).astype(BF16)
        vec_ref[0:1, :] = jnp.sum(gains, axis=0, keepdims=True)
        vec_ref[1:2, :] = jnp.sum(shifts, axis=0, keepdims=True)

def feed_forward(tokens, context, cotangent, w_out, w_up, w_down, norms):
    rows, width = tokens.shape
    hidden = w_up.shape[1]
    steps = hidden // FF_CHUNK
    whole = lambda *shape: pl.BlockSpec(shape, lambda s: (0,) * len(shape))
    return pl.pallas_call(
        partial(ffn_kernel, rows=rows),
        grid=(steps,),
        in_specs=[
            whole(rows, width), whole(rows, width), whole(rows, width), whole(width, width),
            pl.BlockSpec((width, FF_CHUNK), lambda s: (0, s)),
            pl.BlockSpec((FF_CHUNK, width), lambda s: (s, 0)),
            whole(*norms.shape),
        ],
        out_specs=[
            whole(rows, width), whole(rows, width), whole(rows, width), whole(width, width),
            pl.BlockSpec((width, FF_CHUNK), lambda s: (0, s)),
            pl.BlockSpec((FF_CHUNK, width), lambda s: (s, 0)),
            whole(8, width),
        ],
        out_shape=[
            jax.ShapeDtypeStruct((rows, width), BF16),
            jax.ShapeDtypeStruct((rows, width), F32),
            jax.ShapeDtypeStruct((rows, width), BF16),
            jax.ShapeDtypeStruct((width, width), BF16),
            jax.ShapeDtypeStruct((width, hidden), BF16),
            jax.ShapeDtypeStruct((hidden, width), BF16),
            jax.ShapeDtypeStruct((8, width), F32),
        ],
        scratch_shapes=[
            pltpu.VMEM((rows, width), F32), pltpu.VMEM((rows, width), BF16), pltpu.VMEM((width, rows), BF16),
            pltpu.VMEM((rows, width), F32), pltpu.VMEM((rows, width), F32),
            pltpu.VMEM((rows, FF_CHUNK), BF16), pltpu.VMEM((rows, FF_CHUNK), BF16),
        ],
        compiler_params=pltpu.CompilerParams(vmem_limit_bytes=VMEM_LIMIT),
        cost_estimate=cost(60.0),
        name="feed_forward",
    )(tokens, context, cotangent, w_out, w_up, w_down, norms)


def qkv_grad_kernel(ht_ref, hg_ref, dqe_ref, dqm_ref, dke_ref, dve_ref, dkm_ref, dvm_ref, before_ref, after_ref,
                    dkge_ref, dvge_ref, dkgm_ref, dvgm_ref, grad_ref, part_ref, glob_ref, dkt_ref):
    step = pl.program_id(0)
    rows, part = part_ref.shape
    width = ht_ref.shape[0]
    edge = 128

    @pl.when(step == 0)
    def _():
        part_ref[0:edge, :] = dqe_ref[0:edge, :]
        part_ref[edge : rows - edge, :] = dqm_ref[...]
        part_ref[rows - edge : rows, :] = dqe_ref[edge : 2 * edge, :]
        grad_ref[...] = mm(ht_ref[...], part_ref[...]).astype(BF16)

    sources = ((1, dke_ref, dkm_ref, dkge_ref, dkgm_ref), (2, dve_ref, dvm_ref, dvge_ref, dvgm_ref))
    for index, edge_ref, mid_ref, edge_glob, mid_glob in sources:

        @pl.when(step == index)
        def _():
            dkt_ref[...] = mid_ref[...].astype(BF16)
            dkt_ref[:, 0:128] = (mid_ref[:, 0:128] + edge_ref[0, :, 128:256] + before_ref[index - 1].astype(F32)).astype(BF16)
            dkt_ref[:, 128:256] = (mid_ref[:, 128:256] + edge_ref[0, :, 256:384]).astype(BF16)
            dkt_ref[:, rows - 256 : rows - 128] = (mid_ref[:, rows - 256 : rows - 128] + edge_ref[1, :, 0:128]).astype(BF16)
            dkt_ref[:, rows - 128 : rows] = (
                mid_ref[:, rows - 128 : rows] + edge_ref[1, :, 128:256] + after_ref[index - 1].astype(F32)
            ).astype(BF16)
            part_ref[...] = jnp.transpose(dkt_ref[...])
            glob = (edge_glob[...] + mid_glob[...]).reshape(-1, part).astype(BF16)
            glob_ref[...] = glob
            hg = hg_ref[...].reshape(-1, width)
            grad_ref[...] = (mm(ht_ref[...], part_ref[...]) + mm_tn(hg, glob)).astype(BF16)


def qkv_grad(hidden_t, hg, dq, dk, dv, rims, dkg, dvg, half, pairs):
    width, rows = hidden_t.shape
    part = pairs * 128
    blocks = hg.shape[0]

    def whole(*shape):
        return pl.BlockSpec(shape, lambda i: (0,) * len(shape))

    edge_keys = pl.BlockSpec((2, part, SPAN), lambda i: (0, half, 0))
    edge_glob = pl.BlockSpec((blocks, GLOB_FORM, part), lambda i: (0, 0, half))
    rim = pl.BlockSpec((2, part, RADIUS), lambda i: (0, half, 0))
    mid_glob = whole(blocks, GLOB_FORM, part)
    return pl.pallas_call(
        qkv_grad_kernel,
        grid=(3,),
        in_specs=[
            whole(width, rows), whole(blocks, GLOB_FORM, width),
            pl.BlockSpec((2 * TILE, part), lambda i: (0, half)), whole(rows - 2 * TILE, part),
            edge_keys, edge_keys, whole(part, rows), whole(part, rows), rim, rim,
            edge_glob, edge_glob, mid_glob, mid_glob,
        ],
        out_specs=[
            pl.BlockSpec((width, part), lambda i: (0, i)),
            pl.BlockSpec((rows, part), lambda i: (0, i)),
            pl.BlockSpec((blocks * GLOB_FORM, part), lambda i: (0, jnp.maximum(i - 1, 0))),
        ],
        out_shape=[
            jax.ShapeDtypeStruct((width, 3 * part), BF16),
            jax.ShapeDtypeStruct((rows, 3 * part), BF16),
            jax.ShapeDtypeStruct((blocks * GLOB_FORM, 2 * part), BF16),
        ],
        scratch_shapes=[pltpu.VMEM((part, rows), BF16)],
        compiler_params=pltpu.CompilerParams(vmem_limit_bytes=VMEM_LIMIT),
        cost_estimate=cost(20.0),
        name="qkv_grad",
    )(hidden_t, hg, dq[0], dq[1], dk[0], dv[0], dk[1], dv[1], rims[0], rims[1], dkg[0], dvg[0], dkg[1], dvg[1])


def token_grad_kernel(pa_ref, pb_ref, tok_ref, dmid_ref, w_ref, norms_ref, ga_ref, gb_ref, oh_ref, ng_ref, second_ref,
                      ve_ref, va_ref, vb_ref, tg_ref, gp_ref, vec_ref, both_ref, gains_ref, shifts_ref, *, pairs, kept):
    step = pl.program_id(0)
    width = tok_ref.shape[1]
    part = pairs * 128

    @pl.when(step == 0)
    def _():
        gains_ref[...] = jnp.zeros_like(gains_ref)
        shifts_ref[...] = jnp.zeros_like(shifts_ref)

    for index in range(3):
        both_ref[:, index * width : index * width + part] = pa_ref[:, index * part : (index + 1) * part]
        both_ref[:, index * width + part : (index + 1) * width] = pb_ref[:, index * part : (index + 1) * part]
    dh = mm_nt(both_ref[...], w_ref[...])
    normed, scale = norm_parts(tok_ref[...].astype(F32))
    count = dh.shape[0] // 8
    gains_ref[...] += jnp.sum((dh * normed).reshape(count, 8, width), axis=0)
    shifts_ref[...] += jnp.sum(dh.reshape(count, 8, width), axis=0)
    tg_ref[...] = (dmid_ref[...] + norm_pull(dh, normed, scale, norms_ref[0:1, :])).astype(BF16)

    @pl.when(step == pl.num_programs(0) - 1)
    def _():
        dhg = jnp.zeros((ga_ref.shape[0], width), F32)
        for index in range(2):
            for half, ref in ((0, ga_ref), (1, gb_ref)):
                start = (index + 1) * width + half * part
                dhg = dhg + mm_nt(ref[:, index * part : (index + 1) * part], w_ref[:, start : start + part])
        glob_normed = ng_ref[...].reshape(-1, width)
        rows_all = [
            jnp.sum(gains_ref[...], axis=0, keepdims=True) + jnp.sum(dhg * glob_normed, axis=0, keepdims=True),
            jnp.sum(shifts_ref[...], axis=0, keepdims=True) + jnp.sum(dhg, axis=0, keepdims=True),
        ]
        vec_ref[0:1, :] = rows_all[0]
        vec_ref[1:2, :] = rows_all[1]
        vec_ref[2:4, :] = second_ref[0:2, :]
        gp_ref[...] = mm_tn(oh_ref[...].reshape(-1, oh_ref.shape[2]), dhg.astype(BF16)).astype(BF16)
        lines = []
        for p in range(2 * pairs):
            mid = va_ref[p] if p < pairs else vb_ref[p - pairs]
            both = ve_ref[p] + mid
            vec_ref[4:12, p * 128 : p * 128 + 128] = both[0:8]
            lines.append(both[8:9])
        lines.append(jnp.zeros((8 - len(lines), 128), F32))
        lines = jnp.concatenate(split3(jnp.concatenate(lines, axis=0)), axis=0).astype(BF16)
        spot = lax.broadcasted_iota(jnp.int32, (128, width), 0)
        lane = lax.broadcasted_iota(jnp.int32, (128, width), 1)
        spread = mm(lines, (lax.rem(lane, kept) == spot).astype(F32).astype(BF16))
        vec_ref[12:20, :] = spread[0:8] + spread[8:16] + spread[16:24]
        vec_ref[20:24, :] = jnp.zeros((4, width), F32)


def token_grad(parts, globs, tokens, grad_middle, w_qkv, norms, picked, glob_normed, second_sums, vecs, pairs, kept):
    rows, width = tokens.shape
    step = 256
    count = picked.shape[2]

    def whole(*shape):
        return pl.BlockSpec(shape, lambda i: (0,) * len(shape))

    def block(columns):
        return pl.BlockSpec((step, columns), lambda i: (i, 0))

    return pl.pallas_call(
        partial(token_grad_kernel, pairs=pairs, kept=kept),
        grid=(rows // step,),
        in_specs=[
            block(parts[0].shape[1]), block(parts[1].shape[1]), block(width), block(width), whole(*w_qkv.shape),
            whole(*norms.shape), whole(*globs[0].shape), whole(*globs[1].shape), whole(*picked.shape),
            whole(*glob_normed.shape), whole(*second_sums.shape),
        ] + [whole(*v.shape) for v in vecs],
        out_specs=[block(width), whole(count, width), whole(24, width)],
        out_shape=[
            jax.ShapeDtypeStruct((rows, width), BF16),
            jax.ShapeDtypeStruct((count, width), BF16),
            jax.ShapeDtypeStruct((24, width), F32),
        ],
        scratch_shapes=[pltpu.VMEM((step, 3 * width), BF16), pltpu.VMEM((8, width), F32), pltpu.VMEM((8, width), F32)],
        compiler_params=pltpu.CompilerParams(vmem_limit_bytes=VMEM_LIMIT),
        cost_estimate=cost(40.0),
        name="token_grad",
    )(*parts, tokens, grad_middle, w_qkv, norms, *globs, picked, glob_normed, second_sums, *vecs)


def swap_on(axis, mask):
    return [(i, i ^ mask) for i in range(lax.axis_size(axis))]


def add_low(kept, received):
    return (kept.astype(F32) + received.astype(F32)).astype(BF16)


def core_halves(grads, place):
    count = lax.axis_size("seq")
    view = grads.reshape(count // 2, 2, grads.shape[0] // count, grads.shape[1])
    send = lax.dynamic_index_in_dim(view, 1 - place % 2, 1, keepdims=False)
    kept = lax.dynamic_index_in_dim(view, place % 2, 1, keepdims=False)
    return kept, send


def core_swap(send):
    return lax.ppermute(send, "seq", swap_on("seq", 1))


def stream_blocks(summed, group_count):
    outer, rows, columns = summed.shape
    return jnp.moveaxis(summed.reshape(outer, group_count, rows // group_count, columns), 1, 0)


def halve_step(blocks, axis, place, bit, width):
    mine = (place >> bit) & 1
    send = lax.dynamic_index_in_dim(blocks, 1 - mine, width, keepdims=False)
    kept = lax.dynamic_index_in_dim(blocks, mine, width, keepdims=False)
    return kept, lax.ppermute(send, axis, swap_on(axis, 1 << bit))


def exchange_parts(blocks, axis, place, stride):
    parts = [lax.dynamic_index_in_dim(blocks, place, 0, keepdims=False)]
    for step in range(1, blocks.shape[0]):
        send = lax.dynamic_index_in_dim(blocks, place ^ step, 0, keepdims=False)
        parts.append(lax.ppermute(send, axis, swap_on(axis, step * stride)))
    return parts


def summed_low(parts):
    total = parts[0].astype(F32)
    for part in parts[1:]:
        total = total + part.astype(F32)
    return total.astype(BF16)


def gather_rows(rows, axis, place, bit):
    other = lax.ppermute(rows, axis, swap_on(axis, bit))
    upper = (place & bit) > 0
    return jnp.concatenate([jnp.where(upper, other, rows), jnp.where(upper, rows, other)], axis=0)


def gather_blocks(rows, axis, place, stride):
    count = lax.axis_size(axis) // stride
    every = [rows] + [lax.ppermute(rows, axis, swap_on(axis, step * stride)) for step in range(1, count)]
    return ordered(jnp.stack(every), place).reshape(count * rows.shape[0], rows.shape[1])


def ordered(stacked, place):
    count = stacked.shape[0]
    rest = stacked.shape[1:]
    bit = 1
    while bit < count:
        view = stacked.reshape((count // (2 * bit), 2, bit) + rest)
        stacked = jnp.where((place & bit) > 0, view[:, ::-1], view).reshape((count,) + rest)
        bit *= 2
    return stacked


def tied(*values):
    return lax.optimization_barrier(values)


def flat_rows(array, width):
    rows, columns = array.shape
    if columns % width == 0:
        return jnp.concatenate([array[:, i : i + width] for i in range(0, columns, width)], axis=0)
    return array.reshape(-1, width)


def flat_blocks(array, width):
    count, columns = array.shape[0], array.shape[-1]
    array = array.reshape(count, -1, columns)
    if columns % width == 0:
        return jnp.concatenate([array[:, :, i : i + width] for i in range(0, columns, width)], axis=1)
    return array.reshape(count, -1, width)


def unflat_rows(stacked, rows, columns):
    count, width = stacked.shape[0], stacked.shape[2]
    if columns % width == 0:
        return jnp.concatenate([stacked[:, i * rows : (i + 1) * rows] for i in range(columns // width)], axis=2)
    return stacked.reshape(count, rows, columns)


def pad_rows(blocks, width):
    count = blocks.shape[0]
    flat = blocks.reshape(count, -1)
    size = -(-flat.shape[1] // (16 * width)) * 16 * width
    return jnp.pad(flat, ((0, 0), (0, size - flat.shape[1]))).reshape(count, -1, width)


def exchange_raw(piece, axis):
    count = lax.axis_size(axis)
    return [piece] + [lax.ppermute(piece, axis, swap_on(axis, step)) for step in range(1, count)]


def body(
    tokens,
    global_states,
    cotangent,
    w_qkv,
    w_out,
    w_up,
    w_down,
    first_gain,
    first_shift,
    second_gain,
    second_shift,
    rich_query,
    rich_key,
    rich_bias,
    rich_theta,
    bucket_units,
    form_lengths,
    coords,
    glob_owner,
):
    row_count = tokens.shape[1]
    model_width = tokens.shape[2]
    place = lax.axis_index("seq")
    group = lax.axis_index("stream")
    seq_count = lax.axis_size("seq")
    group_count = lax.axis_size("stream")
    rich = (rich_query, rich_key, rich_bias, rich_theta)
    offset = (place * row_count).astype(jnp.int32).reshape(1, 1)
    norms = jnp.stack([first_gain, first_shift, second_gain, second_shift])
    up = [(i, i + 1) for i in range(seq_count - 1)]
    down = [(i + 1, i) for i in range(seq_count - 1)]
    pairs = rich_bias.shape[1] // 2
    half_pairs = pairs // 2
    kept_rows = model_width // seq_count

    before = lax.ppermute(tokens[0, row_count - RADIUS :], "seq", up)
    after = lax.ppermute(tokens[0, :RADIUS], "seq", down)
    pair_glob = gather_rows(global_states[0], "seq", place, 1)
    pair_glob, norms, before, after = tied(pair_glob, norms, before, after)
    every_glob = gather_blocks(pair_glob, "seq", place // 2, 2)
    queries, keys, values, hidden_t = project_tokens(tokens[0], w_qkv, norms)
    (context, pn, pf, g0, g1, key_pad, value_pad, glob_keys, glob_values, glob_hidden, glob_normed, picked) = attn_forward(
        queries, keys, values, before, after, every_glob, glob_owner, w_qkv, norms,
        coords[0], bucket_units, form_lengths, offset, rich,
    )
    layer_out, grad_middle, grad_context, grad_w_out, grad_w_up, grad_w_down, second_sums = feed_forward(
        tokens[0], context, cotangent[0], w_out, w_up, w_down, norms
    )

    def attention_back(first_pair, count, edge, grad_context):
        return attn_backward(
            queries, grad_context, context, key_pad, value_pad, glob_keys, glob_values, coords[0], offset, rich,
            (pn, pf, g0, g1), first_pair, count, edge,
        )

    halves = [core_halves(grad, place) for grad in (grad_w_up, grad_w_down, grad_w_out)]
    sends = [half[1] for half in halves]
    grad_context, *sends = tied(grad_context, *sends)
    halves = [(half[0], core_swap(send)) for half, send in zip(halves, sends)]
    dq_e, dk_e, dv_e, dkg_e, dvg_e, vec_e, rim_e = attention_back(0, pairs, True, grad_context)
    to_before, to_after = rim_e[0], rim_e[1]
    rims = (lax.ppermute(to_after, "seq", up), lax.ppermute(to_before, "seq", down))

    (dq_e, *swapped) = tied(dq_e, *[half[1] for half in halves])
    halves = [(half[0], received) for half, received in zip(halves, swapped)]

    sums = [add_low(*half) for half in halves]
    outer = seq_count // 2
    bits = group_count.bit_length() - 1
    pieces = [
        jnp.moveaxis(sums[0].reshape(outer, kept_rows, group_count, -1), 2, 0).reshape(group_count, outer, -1, model_width),
        jnp.moveaxis(sums[1].reshape(outer, group_count, -1, model_width), 1, 0),
        jnp.moveaxis(sums[2].reshape(outer, group_count, -1, model_width), 1, 0),
    ]
    piece_rows = [piece.shape[2] for piece in pieces]
    early = jnp.concatenate(pieces, axis=2).reshape((2,) * bits + (outer, sum(piece_rows), model_width))
    columns = model_width // 2
    early_x, early_y = early[..., :columns], early[..., columns:]
    order_x = list(range(bits))
    order_y = order_x[1:] + order_x[:1]

    def halved(blocks, order, done):
        bit = order[done]
        rest = sorted(order[done:], reverse=True)
        return halve_step(blocks, "stream", group, bit, rest.index(bit))

    early_x, early_y, grad_context, *rims = tied(early_x, early_y, grad_context, *rims)
    (keep_x, got_x), (keep_y, got_y) = halved(early_x, order_x, 0), halved(early_y, order_y, 0)
    dq_a, dk_a, dv_a, dkg_a, dvg_a, vec_a, _ = attention_back(0, half_pairs, False, grad_context)
    grads_a, part_a, glob_a = qkv_grad(
        hidden_t, glob_hidden, (dq_e, dq_a), (dk_e, dk_a), (dv_e, dv_a), rims, (dkg_e, dkg_a), (dvg_e, dvg_a), 0, half_pairs
    )
    got_x, got_y, grads_a = tied(got_x, got_y, grads_a)
    early_x, early_y = add_low(keep_x, got_x), add_low(keep_y, got_y)
    kept_a, send_a = core_halves(grads_a, place)
    split = (2,) * bits + (outer, kept_rows // group_count, -1)
    late_a = stream_blocks(add_low(kept_a, core_swap(send_a)), group_count).reshape(split)
    early_x, early_y, late_a, grad_context = tied(early_x, early_y, late_a, grad_context)
    for done in range(1, bits):
        (keep_x, got_x), (keep_y, got_y) = halved(early_x, order_x, done), halved(early_y, order_y, done)
        early_x, early_y = (keep_x, got_x), (keep_y, got_y)
        if done + 1 < bits:
            early_x, early_y = add_low(*early_x), add_low(*early_y)
    keep_a, got_a = halved(late_a, order_x, 0)
    dq_b, dk_b, dv_b, dkg_b, dvg_b, vec_b, _ = attention_back(half_pairs, half_pairs, False, grad_context)
    got_x, got_y, got_a, dq_b = tied(early_x[1], early_y[1], got_a, dq_b)
    early = jnp.concatenate([add_low(early_x[0], got_x), add_low(early_y[0], got_y)], axis=-1)
    late_a = add_low(keep_a, got_a)
    early, late_a, dq_b = tied(early, late_a, dq_b)
    early = exchange_parts(early, "seq", place // 2, 2)
    for done in range(1, bits):
        late_a = halved(late_a, order_x, done)
        if done + 1 < bits:
            late_a = add_low(*late_a)
    grads_b, part_b, glob_b = qkv_grad(
        hidden_t, glob_hidden, (dq_e, dq_b), (dk_e, dk_b), (dv_e, dv_b), rims, (dkg_e, dkg_b), (dvg_e, dvg_b), 1, half_pairs
    )
    kept_b, send_b = core_halves(grads_b, place)
    got_a, got_b = tied(late_a[1], core_swap(send_b))
    late_a = add_low(late_a[0], got_a)
    late_b = stream_blocks(add_low(kept_b, got_b), group_count).reshape(split)
    late_a, late_b, part_b = tied(late_a, late_b, part_b)
    keep_b, got_b = halved(late_b, order_x, 0)
    tokens_grad, glob_part, vectors = token_grad(
        (part_a, part_b), (glob_a, glob_b), tokens[0], grad_middle, w_qkv, norms, picked, glob_normed, second_sums,
        (vec_e, vec_a, vec_b), half_pairs, kept_rows,
    )
    got_b, glob_part, *received = tied(got_b, glob_part, *early[1:2])
    late_b = add_low(keep_b, got_b)
    for done in range(1, bits):
        keep_b, got_b = halved(late_b, order_x, done)
        if done + 1 < bits:
            late_b = add_low(keep_b, got_b)
    got_b, *last = tied(got_b, *early[2:])
    late_b = add_low(keep_b, got_b)
    early = summed_low([early[0]] + received + last)
    gathered = exchange_raw(early, "stream")
    vec_rows = jnp.moveaxis(vectors.reshape(24, outer, 2 * kept_rows), 1, 0).astype(BF16)
    vec_flat = pad_rows(vec_rows, model_width)
    glob_blocks = glob_part.reshape(outer, -1, model_width)
    late = jnp.concatenate([late_a, late_b], axis=2)
    columns = late.shape[2]
    late_flat = flat_blocks(late, model_width)
    counts = [late_flat.shape[1], glob_blocks.shape[1], vec_flat.shape[1]]
    summed = exchange_parts(jnp.concatenate([late_flat, glob_blocks, vec_flat], axis=1), "seq", place // 2, 2)
    summed = tied(*summed, *gathered)
    gathered = ordered(jnp.stack(summed[outer:]), group)
    summed = summed_low(summed[:outer])
    late_piece = summed[: counts[0]]
    glob_piece = summed[counts[0] : counts[0] + counts[1]].reshape(2, -1, model_width)
    vec_piece = summed[counts[0] + counts[1] :]
    glob_send = lax.dynamic_index_in_dim(glob_piece, 1 - place % 2, 0, keepdims=False)
    glob_kept = lax.dynamic_index_in_dim(glob_piece, place % 2, 0, keepdims=False)
    every = exchange_raw(jnp.concatenate([late_piece, vec_piece], axis=0), "stream")
    glob_got = core_swap(glob_send)
    vec_sum = sum(rows[counts[0] :].astype(F32) for rows in every)
    vec_sum = vec_sum.reshape(-1)[: 24 * 2 * kept_rows].reshape(24, 2, kept_rows)
    vec_send = lax.dynamic_index_in_dim(vec_sum, 1 - place % 2, 1, keepdims=False)
    vec_own = lax.dynamic_index_in_dim(vec_sum, place % 2, 1, keepdims=False) + core_swap(vec_send)
    late = ordered(jnp.stack([rows[: counts[0]] for rows in every]), group)
    late = unflat_rows(late, kept_rows // group_count, columns).reshape(kept_rows, columns).astype(F32)
    grad_glob = glob_kept.astype(F32) + glob_got.astype(F32)
    own_glob, own_scale = norm_parts(global_states[0].astype(F32))
    glob_grad = norm_pull(grad_glob, own_glob, own_scale, first_gain).astype(BF16)

    part = half_pairs * 128
    share_qkv = jnp.concatenate(
        [late[:, (half * 3 + i) * part : (half * 3 + i + 1) * part] for i in range(3) for half in range(2)], axis=1
    )
    early = gathered.astype(F32)
    cuts = [0, piece_rows[0], piece_rows[0] + piece_rows[1], sum(piece_rows)]
    share_up = jnp.moveaxis(early[:, : cuts[1]].reshape(group_count, kept_rows, -1), 0, 1).reshape(kept_rows, -1)
    share_down = early[:, cuts[1] : cuts[2]].reshape(-1, model_width)
    share_out = early[:, cuts[2] :].reshape(-1, model_width)
    own_vectors = vec_own[:12]
    heads = vec_own[12 : 12 + pairs, :12]
    bias_grad = heads[:, :8].reshape(pairs, 2, 4).transpose(2, 0, 1).reshape(rich_bias.shape)
    theta_grad = heads[:, 8:].reshape(pairs, 2, 2).transpose(2, 0, 1).reshape(rich_theta.shape)
    return (
        layer_out[None],
        tokens_grad[None],
        glob_grad[None],
        share_qkv,
        share_out,
        share_up,
        share_down,
        own_vectors[0],
        own_vectors[1],
        own_vectors[2],
        own_vectors[3],
        own_vectors[4:8],
        own_vectors[8:12],
        bias_grad,
        theta_grad,
    )


def solution(mesh):
    return jax.shard_map(
        body,
        mesh=mesh,
        in_specs=(
            P("stream", "seq", None),
            P("stream", "seq", None),
            P("stream", "seq", None),
            P(),
            P(),
            P(),
            P(),
            P(),
            P(),
            P(),
            P(),
            P(),
            P(),
            P(),
            P(),
            P("stream", None),
            P("stream", None),
            P("stream", None, None),
            P("stream", None),
        ),
        out_specs=(
            P("stream", "seq", None),
            P("stream", "seq", None),
            P("stream", "seq", None),
            P("seq", None),
            P("seq", None),
            P("seq", None),
            P("seq", None),
            P("seq"),
            P("seq"),
            P("seq"),
            P("seq"),
            P(None, "seq"),
            P(None, "seq"),
            P(),
            P(),
        ),
        check_vma=False,
    )
```
